256 devices in a mesh: blk: 32 (over y_hi, z, core), fsdp: 8 (over x, y_lo).
Axes of the slice: x: 4, y: 4 (y_hi: 2, y_lo: 2; y = y_hi * 2 + y_lo), z: 8, core: 2. Of those that a mesh axis runs over, the one named last changes fastest.
Arguments:
- volumes: float32 [8, 256, 16, 16, 128], P('fsdp', 'blk'), may hold values from -6 to 6
- weight_one: float32 [3456, 256], P('fsdp'), may hold values from -0.109375 to 0.109375
- weight_two: float32 [6912, 256], P('fsdp'), may hold values from -0.078125 to 0.078125
- cotangent: float32 [8, 64, 4, 4, 256], P('fsdp', 'blk'), may hold values from -6 to 6
Outputs:
- section_out: float32 [8, 64, 4, 4, 256], P('fsdp', 'blk')
- grad_input: float32 [8, 256, 16, 16, 128], P('fsdp', 'blk')
- grad_one: float32 [3456, 256], P('fsdp', 'blk')
- grad_two: float32 [6912, 256], P('fsdp', 'blk')
The draws below stay inside these ranges and needn't reach their ends.
All inputs are finite; a program needn't handle non-finite values.
Results may differ from the reference program's by a relative error of at most 0.00018.
Values sent between devices are 32-bit elements; how exact they have to be, the bound alone decides.
No kernel may reach another device: no remote copies, remote signals or barrier semaphores. Data moves between devices by JAX's collectives and lax.ppermute only.
A program may use at most 128 MiB of HBM per device.

```python
import jax
import jax.numpy as jnp
from jax import lax

CI = 128
CO = 256
NY = 16
NX = 16
NZ = 256
VOLUMES = 8


def strengthened(entries, own_key, source, target, parts, factor):
    def block_of(axis_at):
        return (jnp.arange(entries.shape[axis_at]) // (entries.shape[axis_at] // parts)).reshape((-1,) + (1,) * (entries.ndim - 1 - axis_at))

    near = jax.random.permutation(own_key, parts)[block_of(target)]
    far = (block_of(target) + parts // 2) % parts
    return jnp.where((block_of(source) == near) | (block_of(source) == far), factor * entries, entries)


def block_scale(key, extent, cuts, smallest, largest):
    factor_of = 1.0
    for position, parts in cuts:
        steps = jax.random.uniform(jax.random.fold_in(jax.random.fold_in(key, 6), position), (parts,), jnp.float32, smallest / len(cuts), largest / len(cuts))
        factor_of = factor_of * jnp.repeat(jnp.exp(steps), extent[position] // parts).reshape((-1,) + (1,) * (len(extent) - 1 - position))
    return factor_of


def normal_values(stream_key, dims, spread, most, shards=(), dtype=jnp.bfloat16):
    factor_of = block_scale(stream_key, dims, shards, -0.22, 0.18) if shards else 1.0
    drawn = jax.random.normal(stream_key, dims, jnp.float32) * spread * factor_of
    return jnp.minimum(jnp.maximum(drawn, -most), most).astype(dtype)


def gaussian_with(rng, shape, scale, reach, cuts, heavy, dtype=jnp.bfloat16):
    drawn = scale * jax.random.normal(rng, shape, jnp.float32)
    if cuts:
        drawn = drawn * block_scale(rng, shape, cuts, -0.22, 0.18)
    return jnp.clip(strengthened(drawn, jax.random.fold_in(rng, 3), *heavy), -reach, reach).astype(dtype)


def setup_inputs(seed: int = 0) -> dict:
    seeds = jax.random.split(jax.random.key(seed), 5)
    return {
        "volumes": normal_values(seeds[0], (VOLUMES, NZ, NY, NX, CI), 1.0, 6.0, ((0, 8), (1, 32)), jnp.float32),
        "weight_one": normal_values(seeds[1], (27 * CI, CO), (27 * CI) ** -0.5, 0.109375, ((0, 8),), jnp.float32),
        "weight_two": normal_values(seeds[2], (27 * CO, CO), (27 * CO) ** -0.5, 0.078125, ((0, 8),), jnp.float32),
        "cotangent": gaussian_with(seeds[3], (VOLUMES, NZ // 4, NY // 4, NX // 4, CO), 1.0, 6.0, ((0, 8), (1, 32)), (1, 4, 32, 2.75), jnp.float32),
    }


def convolve(field, weights, chans_in, chans_out):
    kernel = weights.reshape(3, 3, 3, chans_in, chans_out)
    return lax.conv_general_dilated(field, kernel, (2, 2, 2), ((1, 1), (1, 1), (1, 1)), dimension_numbers=('NDHWC', 'DHWIO', 'NDHWC'), precision=lax.Precision.HIGHEST)

def reference(volumes, weight_one, weight_two, cotangent):

    def forward(field, first, second):
        preact = convolve(field, first, CI, CO)
        hidden = jax.nn.silu(preact)
        return convolve(hidden, second, CO, CO)
    section_out, pullback = jax.vjp(forward, volumes, weight_one, weight_two)
    grad_input, grad_first, grad_second = pullback(cotangent)
    scale_one = 1.0 / (VOLUMES * (NZ // 2) * (NY // 2) * (NX // 2)) ** 0.5
    scale_two = 1.0 / (VOLUMES * (NZ // 4) * (NY // 4) * (NX // 4)) ** 0.5
    return (section_out, grad_input, grad_first * scale_one, grad_second * scale_two)
```

```python
import functools

import jax
import jax.numpy as jnp
import ml_dtypes
import numpy as np
from jax import lax
from jax.experimental import pallas as pl
from jax.experimental.pallas import tpu as pltpu
from jax.sharding import PartitionSpec as P

F32 = jnp.float32
BF16 = jnp.bfloat16
ROWS_ONE = 432
ROWS_TWO = 864
HALF = 216
TAPS = [(a, b, c) for a in range(3) for b in range(3) for c in range(3)]
VMEM = pl.BlockSpec(memory_space=pltpu.VMEM)
SMEM = pl.BlockSpec(memory_space=pltpu.SMEM)
PARAMS = pltpu.CompilerParams(vmem_limit_bytes=56 * 1024 * 1024)


def split(value):
    high = value.astype(BF16)
    return high, (value - high.astype(F32)).astype(BF16)


def contract(left, right, dims=((1,), (0,))):
    def one(x, y):
        return lax.dot_general(x, y, (dims, ((), ())), preferred_element_type=F32)

    return one(left[0], right[0]) + (one(left[0], right[1]) + one(left[1], right[0]))


def selections():
    take = np.zeros((27, 2, 4, 4, 5, 8, 8), np.float32)
    fold = np.zeros((4, 8, 8, 27, 2, 4, 4), np.float32)
    for t, (a, b, c) in enumerate(TAPS):
        for i in range(2):
            for j in range(4):
                for k in range(4):
                    y, x = 2 * j - 1 + b, 2 * k - 1 + c
                    if y < 0 or x < 0:
                        continue
                    take[t, i, j, k, 2 * i + a, y, x] = 1
                    fold[2 * i + (0 if a == 1 else 1), y, x, t, i, j, k] = 1
    return take.reshape(864, 320).astype(ml_dtypes.bfloat16), fold.reshape(256, 864).astype(ml_dtypes.bfloat16)


def spans(width, shard):
    for t in range(27):
        done = 0
        while done < width:
            j, at = divmod(t * width + done, shard)
            size = min(width - done, shard - at)
            yield t, done, j, at, size
            done += size


def cot_kernel(group_ref, cot_ref, above_ref, w_ref, out_ref):
    cells = cot_ref[...]
    plain = cells.reshape(256, 256)
    moved = jnp.concatenate([cells[:, 16:], above_ref[...]], 1).reshape(256, 256)
    weights = split(w_ref[...])
    nt = ((1,), (1,))
    here = contract(split(plain), weights, nt)
    next_up = contract(split(moved), weights, nt)
    row = group_ref[0] * ROWS_TWO + lax.broadcasted_iota(jnp.int32, (256, ROWS_TWO), 1)
    out_ref[...] = jnp.where(row < 9 * 256, next_up, here).reshape(8, 32, ROWS_TWO)


def first_kernel(core_ref, vol_ref, below_ref, mine_ref, other_ref, take_ref, back_ref,
                 pre_ref, send_ref, ph_ref, pl_ref, wh_ref, wl_ref, x_ref, eh_ref, el_ref):
    core = core_ref[0]
    for s in range(8):
        mine, other = mine_ref[s, :HALF], other_ref[s]
        both = jnp.concatenate([jnp.where(core == 0, mine, other), jnp.where(core == 0, other, mine)], 0)
        high, low = split(both)
        wh_ref[ROWS_ONE * s : ROWS_ONE * (s + 1)] = high
        wl_ref[ROWS_ONE * s : ROWS_ONE * (s + 1)] = low
    lane_row = lax.broadcasted_iota(jnp.int32, (16, 8, 128), 1)
    for z in range(11):
        source, at = (below_ref, z) if z < 3 else (vol_ref, z - 3)
        even = source[at, :, pl.ds(0, 8, stride=2), :]
        odd = source[at, :, pl.ds(1, 8, stride=2), :]
        x_ref[0, z, 1:17] = jnp.where(lane_row == 0, 0.0, pltpu.roll(odd, 1, 1))
        x_ref[1, z, 1:17] = even
        x_ref[2, z, 1:17] = odd
        for c in range(3):
            x_ref[c, z, 0] = jnp.zeros((8, 128), F32)
    for t, (a, b, c) in enumerate(TAPS):
        tiles = [x_ref[c, 2 * n + a, 2 * j + b] for n in range(5) for j in range(8)]
        high, low = split(jnp.concatenate(tiles, 0))
        cols = slice(128 * t, 128 * (t + 1))
        eh_ref[:, cols] = high[:64]
        el_ref[:, cols] = low[:64]
        ph_ref[:, cols] = high[64:]
        pl_ref[:, cols] = low[64:]
    weights = (wh_ref[...], wl_ref[...])
    edge = contract((eh_ref[...], el_ref[...]), weights)
    pre = contract((ph_ref[...], pl_ref[...]), weights)
    pre_ref[...] = pre
    full = jnp.concatenate([edge, pre], 0)
    hidden = full / (1.0 + jnp.exp(-full))
    high, low = split(hidden)
    take = take_ref[...]
    taken = jnp.dot(take, high, preferred_element_type=F32) + jnp.dot(take, low, preferred_element_type=F32)
    for t, begin, j, at, size in spans(256, ROWS_TWO):
        send_ref[j, :32, at : at + size] = taken[32 * t : 32 * (t + 1), begin : begin + size]
    send_ref[:, 32:] = back_ref[...]


def halves(grads, shard, core, keep_ref, send_ref):
    for j in range(keep_ref.shape[0]):
        block = grads[:, shard * j : shard * (j + 1)].reshape(16, 2, 8, shard)
        even, odd = block[:, 0].reshape(128, shard), block[:, 1].reshape(128, shard)
        keep_ref[j] = jnp.where(core == 0, even, odd)
        send_ref[j] = jnp.where(core == 0, odd, even)


def pre_kernel(scale, core_ref, got_ref, pre_ref, fold_ref, ph_ref, pl_ref, gp_ref, keep_ref, send_ref, gh_ref, gl_ref):
    for t, begin, j, at, size in spans(256, ROWS_TWO):
        high, low = split(got_ref[j, 32:, at : at + size])
        gh_ref[32 * t : 32 * (t + 1), begin : begin + size] = high
        gl_ref[32 * t : 32 * (t + 1), begin : begin + size] = low
    fold = fold_ref[...]
    hidden_grad = jnp.dot(fold, gh_ref[...], preferred_element_type=F32) + jnp.dot(fold, gl_ref[...], preferred_element_type=F32)
    pre = pre_ref[...]
    sigma = 1.0 / (1.0 + jnp.exp(-pre))
    pre_grad = hidden_grad * sigma * (1.0 + pre * (1.0 - sigma))
    gp_ref[...] = pre_grad
    turned = split(pre_grad.T * scale)
    grads = contract(turned, (ph_ref[...], pl_ref[...]))
    halves(grads, ROWS_ONE, core_ref[0], keep_ref, send_ref)


def second_kernel(scale, core_ref, got_ref, cot_ref, w_ref, out_ref, keep_ref, send_ref):
    patches = split(got_ref[:, :32].reshape(256, ROWS_TWO))
    out_ref[...] = contract(patches, split(w_ref[...])).reshape(8, 32, 256)
    turned = split(cot_ref[...].reshape(256, 256).T * scale)
    grads = contract(turned, patches)
    halves(grads, ROWS_TWO, core_ref[0], keep_ref, send_ref)


def back_kernel(gp_ref, above_ref, wh_ref, wl_ref, out_ref):
    cells = split(jnp.concatenate([gp_ref[...], above_ref[...]], 0))
    weights = (wh_ref, wl_ref)
    last = lax.broadcasted_iota(jnp.int32, (5, 8, 8, 128), 2) == 7
    zero = jnp.zeros((5, 1, 8, 128), F32)

    def tap(a, b, c):
        t = (a * 3 + b) * 3 + c
        rows = slice(128 * t, 128 * (t + 1))
        return contract(cells, (wh_ref[rows], wl_ref[rows]), ((1,), (1,))).reshape(5, 8, 8, 128)

    def along_x(a, b):
        low = tap(a, b, 0).reshape(40, 8, 128)
        moved = jnp.where(last, 0.0, pltpu.roll(low, 7, 1).reshape(5, 8, 8, 128))
        return tap(a, b, 1), tap(a, b, 2) + moved

    def along_y(a):
        low, mid, high = along_x(a, 0), along_x(a, 1), along_x(a, 2)
        return [[mid[p], high[p] + jnp.concatenate([low[p][:, 1:], zero], 1)] for p in range(2)]

    low, mid, high = along_y(0), along_y(1), along_y(2)
    for px in range(2):
        for py in range(2):
            even = mid[px][py]
            odd = high[px][py][:4] + low[px][py][1:]
            for i in range(4):
                for j in range(8):
                    out_ref[2 * i, 2 * j + py, pl.ds(px, 8, stride=2), :] = even[i, j]
                    out_ref[2 * i + 1, 2 * j + py, pl.ds(px, 8, stride=2), :] = odd[i, j]


def call(kernel, out_shapes, scratch=(), specs=None, flops=0, moved=0):
    single = not isinstance(out_shapes, (list, tuple))
    return pl.pallas_call(
        kernel,
        out_shape=out_shapes,
        in_specs=specs,
        out_specs=VMEM if single else [VMEM] * len(out_shapes),
        scratch_shapes=list(scratch),
        compiler_params=PARAMS,
        cost_estimate=pl.CostEstimate(flops=flops, bytes_accessed=moved, transcendentals=0),
    )


def shaped(*dims, dtype=F32):
    return jax.ShapeDtypeStruct(dims, dtype)


def on_device(volumes, weight_one, weight_two, cotangent):
    blocks = lax.axis_size("blk")
    groups = lax.axis_size("fsdp")
    blk = lax.axis_index("blk")
    core = lax.rem(blk, 2)
    core_scalar = core.reshape(1).astype(jnp.int32)
    group_scalar = lax.axis_index("fsdp").reshape(1).astype(jnp.int32)
    take, fold = (jnp.asarray(array) for array in selections())
    field = volumes[0]
    scale_two = 1.0 / (32 * blocks * groups) ** 0.5
    scale_one = 1.0 / (256 * blocks * groups) ** 0.5
    up = [(n, n + 1) for n in range(blocks - 1)]
    down = [(n + 1, n) for n in range(blocks - 1)]
    swap = [(n, n ^ 1) for n in range(blocks)]
    same_core = [[2 * q + c for q in range(blocks // 2)] for c in range(2)]

    below = lax.ppermute(field[5:], "blk", up)
    half = lax.dynamic_slice_in_dim(weight_one, core * HALF, HALF, 0)
    sent = jnp.concatenate([half, cotangent.reshape(32, 256)], 0)
    gathered = lax.all_to_all(jnp.broadcast_to(sent, (groups, 248, 256)), "fsdp", 0, 0, tiled=True)
    other = lax.ppermute(gathered[:, :HALF], "blk", swap)
    cots = gathered[:, HALF:]
    cots_above = lax.ppermute(cots[:, :16], "blk", down)

    back = call(cot_kernel, shaped(8, 32, ROWS_TWO), specs=[SMEM, VMEM, VMEM, VMEM])(group_scalar, cots, cots_above, weight_two)
    patch = shaped(256, 3456, dtype=BF16)
    weights = shaped(3456, 256, dtype=BF16)
    pre, sent, patch_high, patch_low, w_high, w_low = call(
        first_kernel,
        [shaped(256, 256), shaped(8, 64, ROWS_TWO), patch, patch, weights, weights],
        [pltpu.VMEM((3, 11, 17, 8, 128), F32), pltpu.VMEM((64, 3456), BF16), pltpu.VMEM((64, 3456), BF16)],
        specs=[SMEM] + [VMEM] * 6,
    )(core_scalar, field, below, gathered, other, take, back)
    got = lax.all_to_all(sent, "fsdp", 0, 0, tiled=True)

    half_one = shaped(8, 128, ROWS_ONE)
    grad_pre, keep_one, send_one = call(
        functools.partial(pre_kernel, scale_one),
        [shaped(256, 256), half_one, half_one],
        [pltpu.VMEM((864, 256), BF16), pltpu.VMEM((864, 256), BF16)],
        specs=[SMEM] + [VMEM] * 5,
    )(core_scalar, got, pre, fold, patch_high, patch_low)
    swapped_one = lax.ppermute(send_one, "blk", swap)
    pre_above = lax.ppermute(grad_pre[:64], "blk", down)

    half_two = shaped(1, 128, ROWS_TWO)
    out_part, keep_two, send_two = call(
        functools.partial(second_kernel, scale_two),
        [shaped(8, 32, 256), half_two, half_two],
        specs=[SMEM] + [VMEM] * 3,
    )(core_scalar, got, cots, weight_two)
    swapped_two = lax.ppermute(send_two, "blk", swap)

    one = lax.all_to_all(keep_one + swapped_one, "fsdp", 0, 0, tiled=True)
    grad_input = call(back_kernel, shaped(8, 16, 16, 128), specs=[VMEM] * 4)(grad_pre, pre_above, w_high, w_low)
    out = lax.all_to_all(out_part, "fsdp", 0, 0, tiled=True).sum(0)
    one = one.sum(0).reshape(16, 8, ROWS_ONE)
    two = (keep_two + swapped_two).reshape(16, 8, ROWS_TWO)
    last = jnp.concatenate([one, two], 2)
    last = lax.all_to_all(last, "blk", 0, 0, tiled=True, axis_index_groups=same_core).sum(0)
    grad_one = last[:, :ROWS_ONE].T
    grad_two = last[:, ROWS_ONE:].T
    return (out.reshape(1, 2, 4, 4, 256), grad_input[None], grad_one, grad_two)


def solution(mesh):
    placed = (
        P("fsdp", "blk", None, None, None),
        P("fsdp", None),
        P("fsdp", None),
        P("fsdp", "blk", None, None, None),
    )
    return jax.shard_map(
        on_device,
        mesh=mesh,
        in_specs=placed,
        out_specs=(
            P("fsdp", "blk", None, None, None),
            P("fsdp", "blk", None, None, None),
            P("fsdp", "blk"),
            P("fsdp", "blk"),
        ),
        check_vma=False,
    )
```

```python
import functools

import jax
import jax.numpy as jnp
import ml_dtypes
import numpy as np
from jax import lax
from jax.experimental import pallas as pl
from jax.experimental.pallas import tpu as pltpu
from jax.sharding import PartitionSpec as P

F32 = jnp.float32
BF16 = jnp.bfloat16
ROWS_ONE = 432
ROWS_TWO = 864
HALF = 216
TAPS = [(a, b, c) for a in range(3) for b in range(3) for c in range(3)]
VMEM = pl.BlockSpec(memory_space=pltpu.VMEM)
SMEM = pl.BlockSpec(memory_space=pltpu.SMEM)
PARAMS = pltpu.CompilerParams(vmem_limit_bytes=24 * 1024 * 1024)


def split(value):
    high = value.astype(BF16)
    return high, (value - high.astype(F32)).astype(BF16)


def contract(left, right, dims=((1,), (0,))):
    def one(x, y):
        return lax.dot_general(x, y, (dims, ((), ())), preferred_element_type=F32)

    return one(left[0], right[0]) + (one(left[0], right[1]) + one(left[1], right[0]))


def selections():
    take = np.zeros((27, 2, 4, 4, 5, 8, 8), np.float32)
    fold = np.zeros((4, 8, 8, 27, 2, 4, 4), np.float32)
    for t, (a, b, c) in enumerate(TAPS):
        for i in range(2):
            for j in range(4):
                for k in range(4):
                    y, x = 2 * j - 1 + b, 2 * k - 1 + c
                    if y < 0 or x < 0:
                        continue
                    take[t, i, j, k, 2 * i + a, y, x] = 1
                    fold[2 * i + (0 if a == 1 else 1), y, x, t, i, j, k] = 1
    take = np.concatenate([take[:, :, :, :, 1:], take[:, :, :, :, :1]], 4)
    return take.reshape(864, 320).astype(ml_dtypes.bfloat16), fold.reshape(256, 864).astype(ml_dtypes.bfloat16)


def spans(width, shard):
    for t in range(27):
        done = 0
        while done < width:
            j, at = divmod(t * width + done, shard)
            size = min(width - done, shard - at)
            yield t, done, j, at, size
            done += size


def peer(me, d, sign=1):
    x = lax.rem(me // 2 + sign * (d // 2) + 4, 4)
    y = lax.rem(me + d, 2)
    return 2 * x + y


def cot_kernel(group_ref, *refs):
    cot_refs, w_ref, out_ref, cots_ref = refs[:8], refs[8], refs[9], refs[10]
    me = group_ref[0]
    plain = jnp.concatenate([ref[:32] for ref in cot_refs], 0)
    moved = jnp.concatenate([ref[16:] for ref in cot_refs], 0)
    weights = split(w_ref[...])
    nt = ((1,), (1,))
    here = contract(split(plain), weights, nt)
    next_up = contract(split(moved), weights, nt)
    row = me * ROWS_TWO + lax.broadcasted_iota(jnp.int32, (256, ROWS_TWO), 1)
    back = jnp.where(row < 9 * 256, next_up, here)
    for d in range(8):
        owner = peer(me, d, -1)
        out_ref[owner] = back[32 * d : 32 * (d + 1)]
        cots_ref[owner] = cot_refs[d][:32]


def patch_kernel(vol_ref, below_ref, ph_ref, pl_ref, x_ref):
    lane_row = lax.broadcasted_iota(jnp.int32, (16, 8, 128), 1)
    for z in range(11):
        source, at = (below_ref, z) if z < 3 else (vol_ref, z - 3)
        even = source[at, :, pl.ds(0, 8, stride=2), :]
        odd = source[at, :, pl.ds(1, 8, stride=2), :]
        x_ref[0, z, 1:17] = jnp.where(lane_row == 0, 0.0, pltpu.roll(odd, 1, 1))
        x_ref[1, z, 1:17] = even
        x_ref[2, z, 1:17] = odd
        for c in range(3):
            x_ref[c, z, 0] = jnp.zeros((8, 128), F32)
    for t, (a, b, c) in enumerate(TAPS):
        tiles = [x_ref[c, 2 * n + a, 2 * j + b] for n in (1, 2, 3, 4, 0) for j in range(8)]
        high, low = split(jnp.concatenate(tiles, 0))
        cols = slice(128 * t, 128 * (t + 1))
        ph_ref[:, cols] = high
        pl_ref[:, cols] = low


def first_kernel(core_ref, ph_ref, pl_ref, mine_ref, other_ref, take_ref, pre_ref, send_ref, wh_ref, wl_ref):
    core = core_ref[0]
    for s in range(8):
        mine, other = mine_ref[s], other_ref[s]
        both = jnp.concatenate([jnp.where(core == 0, mine, other), jnp.where(core == 0, other, mine)], 0)
        high, low = split(both)
        wh_ref[ROWS_ONE * s : ROWS_ONE * (s + 1)] = high
        wl_ref[ROWS_ONE * s : ROWS_ONE * (s + 1)] = low
    full = contract((ph_ref[...], pl_ref[...]), (wh_ref[...], wl_ref[...]))
    pre_ref[...] = full[:256]
    hidden = full / (1.0 + jnp.exp(-full))
    high, low = split(hidden)
    take = take_ref[...]
    taken = jnp.dot(take, high, preferred_element_type=F32) + jnp.dot(take, low, preferred_element_type=F32)
    for t, begin, j, at, size in spans(256, ROWS_TWO):
        send_ref[j, :, at : at + size] = taken[32 * t : 32 * (t + 1), begin : begin + size]


def stack(block):
    wide = jnp.concatenate([block[:, 384:], jnp.zeros((128, 512 - block.shape[1]), F32)], 1)
    return jnp.concatenate([block[:, 128 * n : 128 * (n + 1)] for n in range(3)] + [wide.T[: block.shape[1] - 384]], 0)


def unstack(block):
    wide = jnp.concatenate([block[384:], jnp.zeros((512 - block.shape[0], 128), F32)], 0)
    return jnp.concatenate([block[128 * n : 128 * (n + 1)] for n in range(3)] + [wide.T[:, : block.shape[0] - 384]], 1)


def halves(grads, shard, core, keep_ref, send_ref, form):
    for j in range(keep_ref.shape[0]):
        block = grads[:, shard * j : shard * (j + 1)].reshape(16, 2, 8, shard)
        even, odd = block[:, 0].reshape(128, shard), block[:, 1].reshape(128, shard)
        keep_ref[j] = form(jnp.where(core == 0, even, odd))
        send_ref[j] = form(jnp.where(core == 0, odd, even))


def pre_kernel(scale, core_ref, got_ref, pre_ref, fold_ref, ph_ref, pl_ref, gp_ref, keep_ref, send_ref, gh_ref, gl_ref):
    for t, begin, j, at, size in spans(256, ROWS_TWO):
        high, low = split(got_ref[j, :, at : at + size])
        gh_ref[32 * t : 32 * (t + 1), begin : begin + size] = high
        gl_ref[32 * t : 32 * (t + 1), begin : begin + size] = low
    fold = fold_ref[...]
    hidden_grad = jnp.dot(fold, gh_ref[...], preferred_element_type=F32) + jnp.dot(fold, gl_ref[...], preferred_element_type=F32)
    pre = pre_ref[...]
    sigma = 1.0 / (1.0 + jnp.exp(-pre))
    pre_grad = hidden_grad * sigma * (1.0 + pre * (1.0 - sigma))
    gp_ref[...] = pre_grad
    turned = split(pre_grad.T * scale)
    grads = contract(turned, (ph_ref[:256], pl_ref[:256]))
    halves(grads, ROWS_ONE, core_ref[0], keep_ref, send_ref, stack)


def second_kernel(scale, core_ref, group_ref, got_ref, cot_ref, w_ref, *refs):
    out_refs, keep_ref, send_ref, part_ref = refs[:8], refs[8], refs[9], refs[10]
    patches = split(got_ref[...].reshape(256, ROWS_TWO))
    part_ref[...] = contract(patches, split(w_ref[...])).reshape(8, 32, 256)
    for d in range(8):
        out_refs[d][...] = part_ref[peer(group_ref[0], d)]
    turned = split(cot_ref[...].reshape(256, 256).T * scale)
    grads = contract(turned, patches)
    halves(grads, ROWS_TWO, core_ref[0], keep_ref, send_ref, lambda block: block)


def sum_kernel(got_ref, keep_ref, swapped_ref, out_ref):
    total = got_ref[0]
    for j in range(1, 8):
        total = total + got_ref[j]
    both = keep_ref[0] + swapped_ref[0]
    out_ref[:, :, :ROWS_TWO] = both.reshape(16, 8, ROWS_TWO)
    out_ref[:, :, 896 : 896 + ROWS_ONE] = unstack(total).reshape(16, 8, ROWS_ONE)
    out_ref[:, :, ROWS_TWO:896] = jnp.zeros((16, 8, 896 - ROWS_TWO), F32)
    out_ref[:, :, 896 + ROWS_ONE :] = jnp.zeros((16, 8, 1408 - 896 - ROWS_ONE), F32)


def end_kernel(got_ref, one_ref, two_ref):
    total = got_ref[0]
    for j in range(1, 16):
        total = total + got_ref[j]
    two_ref[...] = total[:, :ROWS_TWO]
    one_ref[...] = total[:, 896 : 896 + ROWS_ONE]


def back_kernel(gp_ref, above_ref, wh_ref, wl_ref, out_ref):
    cells = split(jnp.concatenate([gp_ref[...], above_ref[...]], 0))
    weights = (wh_ref, wl_ref)
    last = lax.broadcasted_iota(jnp.int32, (5, 8, 8, 128), 2) == 7
    zero = jnp.zeros((5, 1, 8, 128), F32)

    def tap(a, b, c):
        t = (a * 3 + b) * 3 + c
        rows = slice(128 * t, 128 * (t + 1))
        return contract(cells, (wh_ref[rows], wl_ref[rows]), ((1,), (1,))).reshape(5, 8, 8, 128)

    def along_x(a, b):
        low = tap(a, b, 0).reshape(40, 8, 128)
        moved = jnp.where(last, 0.0, pltpu.roll(low, 7, 1).reshape(5, 8, 8, 128))
        return tap(a, b, 1), tap(a, b, 2) + moved

    def along_y(a):
        low, mid, high = along_x(a, 0), along_x(a, 1), along_x(a, 2)
        return [[mid[p], high[p] + jnp.concatenate([low[p][:, 1:], zero], 1)] for p in range(2)]

    low, mid, high = along_y(0), along_y(1), along_y(2)
    for px in range(2):
        for py in range(2):
            even = mid[px][py]
            odd = high[px][py][:4] + low[px][py][1:]
            for i in range(4):
                for j in range(8):
                    out_ref[2 * i, 2 * j + py, pl.ds(px, 8, stride=2), :] = even[i, j]
                    out_ref[2 * i + 1, 2 * j + py, pl.ds(px, 8, stride=2), :] = odd[i, j]


def call(kernel, out_shapes, scalars, blocks, micros, scratch=()):
    single = not isinstance(out_shapes, (list, tuple))
    return pl.pallas_call(
        kernel,
        out_shape=out_shapes,
        in_specs=[SMEM] * scalars + [VMEM] * blocks,
        out_specs=VMEM if single else [VMEM] * len(out_shapes),
        scratch_shapes=list(scratch),
        compiler_params=PARAMS,
        cost_estimate=pl.CostEstimate(flops=int(micros * 1.1e9), bytes_accessed=1 << 20, transcendentals=0),
    )


def shaped(*dims, dtype=F32):
    return jax.ShapeDtypeStruct(dims, dtype)


def on_device(volumes, weight_one, weight_two, cotangent):
    blocks = lax.axis_size("blk")
    groups = lax.axis_size("fsdp")
    core = lax.rem(lax.axis_index("blk"), 2)
    core_scalar = core.reshape(1).astype(jnp.int32)
    group_scalar = lax.axis_index("fsdp").reshape(1).astype(jnp.int32)
    take, fold = (jnp.asarray(array) for array in selections())
    field = volumes[0]
    scale_two = 1.0 / (32 * blocks * groups) ** 0.5
    scale_one = 1.0 / (256 * blocks * groups) ** 0.5
    up = [(n, n + 1) for n in range(blocks - 1)]
    down = [(n + 1, n) for n in range(blocks - 1)]
    swap = [(n, n ^ 1) for n in range(blocks)]
    same_core = [[2 * q + c for q in range(blocks // 2)] for c in range(2)]
    turns = [[(n, (n // 2 + d // 2) % 4 * 2 + (n + d) % 2) for n in range(groups)] for d in range(groups)]

    cot = cotangent.reshape(32, 256)
    cot_above = lax.ppermute(cot[:16], "blk", down)
    below = lax.ppermute(field[5:], "blk", up)
    cot = jnp.concatenate([cot, cot_above], 0)
    cots = [cot] + [lax.ppermute(cot, "fsdp", turns[d]) for d in range(1, groups)]
    half = lax.dynamic_slice_in_dim(weight_one, core * HALF, HALF, 0)
    mine = lax.all_to_all(jnp.broadcast_to(half, (groups, HALF, 256)), "fsdp", 0, 0, tiled=True)

    patch = shaped(320, 3456, dtype=BF16)
    patch_high, patch_low = call(patch_kernel, [patch, patch], 0, 2, 5, [pltpu.VMEM((3, 11, 17, 8, 128), F32)])(field, below)
    back, cots = call(cot_kernel, [shaped(8, 32, ROWS_TWO), shaped(8, 32, 256)], 1, 9, 3)(group_scalar, *cots, weight_two)
    mine, back, patch_high, patch_low = lax.optimization_barrier((mine, back, patch_high, patch_low))
    other = lax.ppermute(mine, "blk", swap)
    back = lax.all_to_all(back, "fsdp", 0, 0, tiled=True)

    weights = shaped(3456, 256, dtype=BF16)
    pre, taken, w_high, w_low = call(first_kernel, [shaped(256, 256), shaped(8, 32, ROWS_TWO), weights, weights], 1, 5, 7)(
        core_scalar, patch_high, patch_low, mine, other, take
    )
    got = lax.all_to_all(taken, "fsdp", 0, 0, tiled=True)

    half_one = shaped(8, ROWS_ONE, 128)
    grad_pre, keep_one, send_one = call(
        functools.partial(pre_kernel, scale_one),
        [shaped(256, 256), half_one, half_one],
        1,
        5,
        7,
        [pltpu.VMEM((864, 256), BF16), pltpu.VMEM((864, 256), BF16)],
    )(core_scalar, back, pre, fold, patch_high, patch_low)
    swapped_one = lax.ppermute(send_one, "blk", swap)
    pre_above = lax.ppermute(grad_pre[:64], "blk", down)
    one = lax.all_to_all(keep_one + swapped_one, "fsdp", 0, 0, tiled=True)

    half_two = shaped(1, 128, ROWS_TWO)
    *parts, keep_two, send_two = call(
        functools.partial(second_kernel, scale_two),
        [shaped(32, 256)] * 8 + [half_two, half_two],
        2,
        3,
        4,
        [pltpu.VMEM((8, 32, 256), F32)],
    )(core_scalar, group_scalar, got, cots, weight_two)
    swapped_two = lax.ppermute(send_two, "blk", swap)
    out = parts[0]
    for d in range(1, groups):
        out = out + lax.ppermute(parts[d], "fsdp", turns[d])
    grad_input = call(back_kernel, shaped(8, 16, 16, 128), 0, 4, 7)(grad_pre, pre_above, w_high, w_low)

    one, grad_input = lax.optimization_barrier((one, grad_input))
    last = call(sum_kernel, shaped(16, 8, 1408), 0, 3, 2)(one, keep_two, swapped_two)
    last = lax.all_to_all(last, "blk", 0, 0, tiled=True, axis_index_groups=same_core)
    one, two = call(end_kernel, [shaped(8, ROWS_ONE), shaped(8, ROWS_TWO)], 0, 1, 1)(last)
    return (out.reshape(1, 2, 4, 4, 256), grad_input[None], one.T, two.T)


def solution(mesh):
    placed = (
        P("fsdp", "blk", None, None, None),
        P("fsdp", None),
        P("fsdp", None),
        P("fsdp", "blk", None, None, None),
    )
    return jax.shard_map(
        on_device,
        mesh=mesh,
        in_specs=placed,
        out_specs=(
            P("fsdp", "blk", None, None, None),
            P("fsdp", "blk", None, None, None),
            P("fsdp", "blk"),
            P("fsdp", "blk"),
        ),
        check_vma=False,
    )
```

```python
import functools

import jax
import jax.numpy as jnp
import ml_dtypes
import numpy as np
from jax import lax
from jax.experimental import pallas as pl
from jax.experimental.pallas import tpu as pltpu
from jax.sharding import PartitionSpec as P

F32 = jnp.float32
BF16 = jnp.bfloat16
ROWS_ONE = 432
ROWS_TWO = 864
HALF = 216
TAPS = [(a, b, c) for a in range(3) for b in range(3) for c in range(3)]
VMEM = pl.BlockSpec(memory_space=pltpu.VMEM)
SMEM = pl.BlockSpec(memory_space=pltpu.SMEM)
FAR = pl.BlockSpec(memory_space=pltpu.HBM)
PARAMS = pltpu.CompilerParams(vmem_limit_bytes=60 * 1024 * 1024)
SENT = ROWS_ONE + 216


def split(value):
    high = value.astype(BF16)
    return high, (value - high.astype(F32)).astype(BF16)


def contract(left, right, dims=((1,), (0,))):
    def one(x, y):
        return lax.dot_general(x, y, (dims, ((), ())), preferred_element_type=F32)

    return one(left[0], right[0]) + (one(left[0], right[1]) + one(left[1], right[0]))


def selections():
    take = np.zeros((27, 2, 4, 4, 5, 8, 8), np.float32)
    fold = np.zeros((4, 8, 8, 27, 2, 4, 4), np.float32)
    for t, (a, b, c) in enumerate(TAPS):
        for i in range(2):
            for j in range(4):
                for k in range(4):
                    y, x = 2 * j - 1 + b, 2 * k - 1 + c
                    if y < 0 or x < 0:
                        continue
                    take[t, i, j, k, 2 * i + a, y, x] = 1
                    fold[2 * i + (0 if a == 1 else 1), y, x, t, i, j, k] = 1
    take = np.concatenate([take[:, :, :, :, 1:], take[:, :, :, :, :1]], 4)
    return take.reshape(864, 320).astype(ml_dtypes.bfloat16), fold.reshape(256, 864).astype(ml_dtypes.bfloat16)


def spans(width, shard):
    for t in range(27):
        done = 0
        while done < width:
            j, at = divmod(t * width + done, shard)
            size = min(width - done, shard - at)
            yield t, done, j, at, size
            done += size


def peer(me, d):
    return 2 * lax.rem(me // 2 + d // 2, 4) + lax.rem(me + d, 2)


def pack(block):
    rest = block[:, 768:]
    corner = rest[24:]
    tail = [jnp.concatenate([rest[8 * n : 8 * (n + 1)], corner[:, 32 * n : 32 * (n + 1)]], 1) for n in range(3)]
    return jnp.concatenate([block[:, 128 * n : 128 * (n + 1)] for n in range(6)] + tail, 0)


def unpack(block):
    wide = [block[32 * n : 32 * (n + 1)] for n in range(6)]
    tail = [block[192 + 8 * n : 200 + 8 * n] for n in range(3)]
    corner = jnp.concatenate([part[:, 96:] for part in tail], 1)
    rest = jnp.concatenate([part[:, :96] for part in tail] + [corner], 0)
    return jnp.concatenate(wide + [rest], 1)


def split_weights(core, mine_ref, other_ref, wh_ref, wl_ref):
    for s in range(8):
        mine, other = mine_ref[s], other_ref[s]
        both = jnp.concatenate([jnp.where(core == 0, mine, other), jnp.where(core == 0, other, mine)], 0)
        high, low = split(both)
        wh_ref[ROWS_ONE * s : ROWS_ONE * (s + 1)] = high
        wl_ref[ROWS_ONE * s : ROWS_ONE * (s + 1)] = low


def patches_of(vol_ref, below_ref, layers, x_ref, ph_ref, pl_ref):
    lane_row = lax.broadcasted_iota(jnp.int32, (16, 8, 128), 1)
    for z in range(2 * min(layers), 11):
        source, at = (below_ref, z) if z < 3 else (vol_ref, z - 3)
        even = source[at, :, pl.ds(0, 8, stride=2), :]
        odd = source[at, :, pl.ds(1, 8, stride=2), :]
        x_ref[0, z, 1:17] = jnp.where(lane_row == 0, 0.0, pltpu.roll(odd, 1, 1))
        x_ref[1, z, 1:17] = even
        x_ref[2, z, 1:17] = odd
        for c in range(3):
            x_ref[c, z, 0] = jnp.zeros((8, 128), F32)
    for t, (a, b, c) in enumerate(TAPS):
        tiles = [x_ref[c, 2 * n + a, 2 * j + b] for n in layers for j in range(8)]
        high, low = split(jnp.concatenate(tiles, 0))
        cols = slice(128 * t, 128 * (t + 1))
        ph_ref[:, cols] = high
        pl_ref[:, cols] = low


def cot_kernel(scalars, get, outs, scratch):
    weights = split(get(0)[...])
    cells = get(1)[...]
    plain = cells.reshape(256, 256)
    moved = jnp.concatenate([cells[:, 16:], get(2)[...]], 1).reshape(256, 256)
    nt = ((1,), (1,))
    here = contract(split(plain), weights, nt)
    next_up = contract(split(moved), weights, nt)
    row = scalars[0][0] * ROWS_TWO + lax.broadcasted_iota(jnp.int32, (256, ROWS_TWO), 1)
    outs[0][...] = jnp.where(row < 9 * 256, next_up, here).reshape(8, 32, ROWS_TWO)


def first_kernel(scalars, get, outs, scratch):
    pre_ref, send_ref = outs
    x_ref, ph_ref, pl_ref, wh_ref, wl_ref, row_ref = scratch
    patches_of(get(0), get(1), (1, 2, 3, 4, 0), x_ref, ph_ref, pl_ref)
    split_weights(scalars[0][0], get(2), get(3), wh_ref, wl_ref)
    full = contract((ph_ref[...], pl_ref[...]), (wh_ref[...], wl_ref[...]))
    pre_ref[...] = full[:256]
    hidden = full / (1.0 + jnp.exp(-full))
    high, low = split(hidden)
    take = get(4)[...]
    taken = jnp.dot(take, high, preferred_element_type=F32) + jnp.dot(take, low, preferred_element_type=F32)
    for t, begin, j, at, size in spans(256, ROWS_TWO):
        row_ref[j, :, at : at + size] = taken[32 * t : 32 * (t + 1), begin : begin + size]
    for j in range(8):
        send_ref[j] = pack(row_ref[j])


def pre_kernel(scale, scalars, get, outs, scratch):
    gp_ref, keep_ref, send_ref = outs
    x_ref, ph_ref, pl_ref, gh_ref, gl_ref = scratch
    patches_of(get(0), get(1), (1, 2, 3, 4), x_ref, ph_ref, pl_ref)
    got_ref = get(2)
    for t, begin, j, at, size in spans(256, ROWS_TWO):
        high, low = split(got_ref[j, :, at : at + size])
        gh_ref[32 * t : 32 * (t + 1), begin : begin + size] = high
        gl_ref[32 * t : 32 * (t + 1), begin : begin + size] = low
    fold = get(3)[...]
    hidden_grad = jnp.dot(fold, gh_ref[...], preferred_element_type=F32) + jnp.dot(fold, gl_ref[...], preferred_element_type=F32)
    pre = get(4)[...]
    sigma = 1.0 / (1.0 + jnp.exp(-pre))
    pre_grad = hidden_grad * sigma * (1.0 + pre * (1.0 - sigma))
    gp_ref[...] = pre_grad
    grads = contract(split(pre_grad.T * scale), (ph_ref[...], pl_ref[...]))
    halves(grads, ROWS_ONE, scalars[0][0], keep_ref, send_ref, stack)


def join_kernel(keep_ref, swapped_ref, taken_ref, out_ref):
    out_ref[:, :ROWS_ONE] = keep_ref[...] + swapped_ref[...]
    out_ref[:, ROWS_ONE:] = taken_ref[...]


def second_kernel(scale, scalars, get, outs, scratch):
    out_refs, keep_ref, send_ref = outs[:8], outs[8], outs[9]
    (part_ref,) = scratch
    weights = split(get(0)[...])
    turned = split(get(1)[...].reshape(256, 256).T * scale)
    got_ref = get(2)
    patches = split(jnp.concatenate([unpack(got_ref[j]) for j in range(8)], 0))
    grads = contract(turned, patches)
    halves(grads, ROWS_TWO, scalars[0][0], keep_ref, send_ref, lambda block: block)
    part_ref[...] = contract(patches, weights).reshape(8, 32, 256)
    for d in range(8):
        out_refs[d][...] = part_ref[peer(scalars[1][0], d)]


def sum_kernel(scalars, get, outs, scratch):
    (out_ref,) = outs
    got_ref = get(0)
    total = got_ref[0]
    for j in range(1, 8):
        total = total + got_ref[j]
    both = get(1)[0] + get(2)[0]
    out_ref[:, :, :ROWS_TWO] = both.reshape(16, 8, ROWS_TWO)
    out_ref[:, :, 896 : 896 + ROWS_ONE] = unstack(total).reshape(16, 8, ROWS_ONE)
    out_ref[:, :, ROWS_TWO:896] = jnp.zeros((16, 8, 896 - ROWS_TWO), F32)
    out_ref[:, :, 896 + ROWS_ONE :] = jnp.zeros((16, 8, 1408 - 896 - ROWS_ONE), F32)


def end_kernel(got_ref, one_ref, two_ref):
    total = got_ref[0]
    for j in range(1, 16):
        total = total + got_ref[j]
    two_ref[...] = total[:, :ROWS_TWO]
    one_ref[...] = total[:, 896 : 896 + ROWS_ONE]


def stack(block):
    wide = jnp.concatenate([block[:, 384:], jnp.zeros((128, 512 - block.shape[1]), F32)], 1)
    return jnp.concatenate([block[:, 128 * n : 128 * (n + 1)] for n in range(3)] + [wide.T[: block.shape[1] - 384]], 0)


def unstack(block):
    wide = jnp.concatenate([block[384:], jnp.zeros((512 - block.shape[0], 128), F32)], 0)
    return jnp.concatenate([block[128 * n : 128 * (n + 1)] for n in range(3)] + [wide.T[:, : block.shape[0] - 384]], 1)


def halves(grads, shard, core, keep_ref, send_ref, form):
    for j in range(keep_ref.shape[0]):
        block = grads[:, shard * j : shard * (j + 1)].reshape(16, 2, 8, shard)
        even, odd = block[:, 0].reshape(128, shard), block[:, 1].reshape(128, shard)
        keep_ref[j] = form(jnp.where(core == 0, even, odd))
        send_ref[j] = form(jnp.where(core == 0, odd, even))


def back_kernel(scalars, get, outs, scratch):
    (out_ref,), (wh_ref, wl_ref) = outs, scratch
    split_weights(scalars[0][0], get(0), get(1), wh_ref, wl_ref)
    cells = split(jnp.concatenate([get(2)[...], get(3)[...]], 0))
    last = lax.broadcasted_iota(jnp.int32, (5, 8, 8, 128), 2) == 7
    zero = jnp.zeros((5, 1, 8, 128), F32)

    def tap(a, b, c):
        t = (a * 3 + b) * 3 + c
        rows = slice(128 * t, 128 * (t + 1))
        return contract(cells, (wh_ref[rows], wl_ref[rows]), ((1,), (1,))).reshape(5, 8, 8, 128)

    def along_x(a, b):
        low = tap(a, b, 0).reshape(40, 8, 128)
        moved = jnp.where(last, 0.0, pltpu.roll(low, 7, 1).reshape(5, 8, 8, 128))
        return tap(a, b, 1), tap(a, b, 2) + moved

    def along_y(a):
        low, mid, high = along_x(a, 0), along_x(a, 1), along_x(a, 2)
        return [[mid[p], high[p] + jnp.concatenate([low[p][:, 1:], zero], 1)] for p in range(2)]

    low, mid, high = along_y(0), along_y(1), along_y(2)
    for px in range(2):
        for py in range(2):
            even = mid[px][py]
            odd = high[px][py][:4] + low[px][py][1:]
            for i in range(4):
                for j in range(8):
                    out_ref[2 * i, 2 * j + py, pl.ds(px, 8, stride=2), :] = even[i, j]
                    out_ref[2 * i + 1, 2 * j + py, pl.ds(px, 8, stride=2), :] = odd[i, j]


def call(kernel, out_shapes, blocks, micros):
    return pl.pallas_call(
        kernel,
        out_shape=out_shapes,
        in_specs=[VMEM] * blocks,
        out_specs=[VMEM] * len(out_shapes),
        compiler_params=PARAMS,
        cost_estimate=pl.CostEstimate(flops=int(micros * 1.1e9), bytes_accessed=1 << 20, transcendentals=0),
    )


def staged(body, out_shapes, scalars, operands, micros, scratch=()):
    pairs = [operand if isinstance(operand, tuple) else (operand, None) for operand in operands]
    count, outs = len(pairs), len(out_shapes)

    def kernel(*refs):
        scalar_refs, refs = refs[: len(scalars)], refs[len(scalars) :]
        sources, refs = refs[:count], refs[count:]
        out_refs, refs = refs[:outs], refs[outs:]
        buffers, scratch_refs, sems = refs[:count], refs[count:-1], refs[-1]
        copies = []
        for n, (_, window) in enumerate(pairs):
            source = sources[n] if window is None else sources[n].at[:, window[0] : window[1]]
            copies.append(pltpu.make_async_copy(source, buffers[n], sems.at[n]))
        for copy in copies:
            copy.start()

        def get(n):
            copies[n].wait()
            return buffers[n]

        body(scalar_refs, get, out_refs, scratch_refs)

    def buffer(array, window):
        shape = array.shape if window is None else (array.shape[0], window[1] - window[0]) + array.shape[2:]
        return pltpu.VMEM(shape, array.dtype)

    return pl.pallas_call(
        kernel,
        out_shape=out_shapes,
        in_specs=[SMEM] * len(scalars) + [FAR] * count,
        out_specs=[VMEM] * outs,
        scratch_shapes=[buffer(*pair) for pair in pairs] + list(scratch) + [pltpu.SemaphoreType.DMA((count,))],
        compiler_params=PARAMS,
        cost_estimate=pl.CostEstimate(flops=int(micros * 1.1e9), bytes_accessed=1 << 20, transcendentals=0),
    )(*scalars, *[array for array, _ in pairs])


def shaped(*dims, dtype=F32):
    return jax.ShapeDtypeStruct(dims, dtype)


def on_device(volumes, weight_one, weight_two, cotangent):
    blocks = lax.axis_size("blk")
    groups = lax.axis_size("fsdp")
    core_index = lax.rem(lax.axis_index("blk"), 2)
    core = core_index.reshape(1).astype(jnp.int32)
    group = lax.axis_index("fsdp").reshape(1).astype(jnp.int32)
    take, fold = (jnp.asarray(array) for array in selections())
    field = volumes[0]
    scale_two = 1.0 / (32 * blocks * groups) ** 0.5
    scale_one = 1.0 / (256 * blocks * groups) ** 0.5
    up = [(n, n + 1) for n in range(blocks - 1)]
    down = [(n + 1, n) for n in range(blocks - 1)]
    swap = [(n, n ^ 1) for n in range(blocks)]
    same_core = [[2 * q + c for q in range(blocks // 2)] for c in range(2)]
    turns = [[(n, (n // 2 + d // 2) % 4 * 2 + (n + d) % 2) for n in range(groups)] for d in range(groups)]

    below = lax.ppermute(field[5:], "blk", up)
    half = lax.dynamic_slice_in_dim(weight_one, core_index * HALF, HALF, 0)
    sent = jnp.concatenate([half, cotangent.reshape(32, 256)], 0)
    mine = lax.all_to_all(jnp.broadcast_to(sent, (groups, 248, 256)), "fsdp", 0, 0, tiled=True)
    cots_above = lax.ppermute(mine[:, HALF : HALF + 16], "blk", down)
    other = lax.ppermute(mine, "blk", swap)
    (back,) = staged(cot_kernel, [shaped(8, 32, ROWS_TWO)], [group], [weight_two, (mine, (HALF, 248)), cots_above], 3)
    back = lax.all_to_all(back, "fsdp", 0, 0, tiled=True)

    def patch_scratch(rows):
        return [pltpu.VMEM((3, 11, 17, 8, 128), F32), pltpu.VMEM((rows, 3456), BF16), pltpu.VMEM((rows, 3456), BF16)]

    weights = [pltpu.VMEM((3456, 256), BF16)] * 2
    halves_of = [(mine, (0, HALF)), (other, (0, HALF))]
    pre, taken = staged(
        first_kernel,
        [shaped(256, 256), shaped(8, 216, 128)],
        [core],
        [field, below, *halves_of, take],
        8,
        patch_scratch(320) + weights + [pltpu.VMEM((8, 32, ROWS_TWO), F32)],
    )
    half_one = shaped(8, ROWS_ONE, 128)
    grad_pre, keep_one, send_one = staged(
        functools.partial(pre_kernel, scale_one),
        [shaped(256, 256), half_one, half_one],
        [core],
        [field, below, back, fold, pre],
        7,
        patch_scratch(256) + [pltpu.VMEM((864, 256), BF16)] * 2,
    )
    swapped_one = lax.ppermute(send_one, "blk", swap)
    pre_above = lax.ppermute(grad_pre[:64], "blk", down)
    (joined,) = call(join_kernel, [shaped(8, SENT, 128)], 3, 2)(keep_one, swapped_one, taken)
    got = lax.all_to_all(joined, "fsdp", 0, 0, tiled=True)

    (grad_input,) = staged(back_kernel, [shaped(8, 16, 16, 128)], [core], [*halves_of, grad_pre, pre_above], 7, weights)
    got, grad_input = lax.optimization_barrier((got, grad_input))
    half_two = shaped(1, 128, ROWS_TWO)
    *parts, keep_two, send_two = staged(
        functools.partial(second_kernel, scale_two),
        [shaped(32, 256)] * 8 + [half_two, half_two],
        [core, group],
        [weight_two, (mine, (HALF, 248)), (got, (ROWS_ONE, SENT))],
        3,
        [pltpu.VMEM((8, 32, 256), F32)],
    )
    swapped_two = lax.ppermute(send_two, "blk", swap)
    (last,) = staged(sum_kernel, [shaped(16, 8, 1408)], [], [(got, (0, ROWS_ONE)), keep_two, swapped_two], 2)
    last = lax.all_to_all(last, "blk", 0, 0, tiled=True, axis_index_groups=same_core)
    out = parts[0]
    for d in range(1, groups):
        out = out + lax.ppermute(parts[d], "fsdp", turns[d])
    one, two = call(end_kernel, [shaped(8, ROWS_ONE), shaped(8, ROWS_TWO)], 1, 1)(last)
    return (out.reshape(1, 2, 4, 4, 256), grad_input[None], one.T, two.T)


def solution(mesh):
    placed = (
        P("fsdp", "blk", None, None, None),
        P("fsdp", None),
        P("fsdp", None),
        P("fsdp", "blk", None, None, None),
    )
    return jax.shard_map(
        on_device,
        mesh=mesh,
        in_specs=placed,
        out_specs=(
            P("fsdp", "blk", None, None, None),
            P("fsdp", "blk", None, None, None),
            P("fsdp", "blk"),
            P("fsdp", "blk"),
        ),
        check_vma=False,
    )
```

```python
import functools

import jax
import jax.numpy as jnp
import ml_dtypes
import numpy as np
from jax import lax
from jax.experimental import pallas as pl
from jax.experimental.pallas import tpu as pltpu
from jax.sharding import PartitionSpec as P

F32 = jnp.float32
BF16 = jnp.bfloat16
ROWS_ONE = 432
ROWS_TWO = 864
HALF = 216
TAPS = [(a, b, c) for a in range(3) for b in range(3) for c in range(3)]
VMEM = pl.BlockSpec(memory_space=pltpu.VMEM)
SMEM = pl.BlockSpec(memory_space=pltpu.SMEM)
FAR = pl.BlockSpec(memory_space=pltpu.HBM)
PARAMS = pltpu.CompilerParams(vmem_limit_bytes=60 * 1024 * 1024)


def split(value):
    high = value.astype(BF16)
    return high, (value - high.astype(F32)).astype(BF16)


def contract(left, right, dims=((1,), (0,))):
    def one(x, y):
        return lax.dot_general(x, y, (dims, ((), ())), preferred_element_type=F32)

    return one(left[0], right[0]) + (one(left[0], right[1]) + one(left[1], right[0]))


def selections():
    take = np.zeros((27, 2, 4, 4, 5, 8, 8), np.float32)
    fold = np.zeros((4, 8, 8, 27, 2, 4, 4), np.float32)
    for t, (a, b, c) in enumerate(TAPS):
        for i in range(2):
            for j in range(4):
                for k in range(4):
                    y, x = 2 * j - 1 + b, 2 * k - 1 + c
                    if y < 0 or x < 0:
                        continue
                    take[t, i, j, k, 2 * i + a, y, x] = 1
                    fold[2 * i + (0 if a == 1 else 1), y, x, t, i, j, k] = 1
    take = np.concatenate([take[:, :, :, :, 1:], take[:, :, :, :, :1]], 4)
    return take.reshape(864, 320).astype(ml_dtypes.bfloat16), fold.reshape(256, 864).astype(ml_dtypes.bfloat16)


def spans(width, shard):
    for t in range(27):
        done = 0
        while done < width:
            j, at = divmod(t * width + done, shard)
            size = min(width - done, shard - at)
            yield t, done, j, at, size
            done += size


def peer(me, d):
    return 2 * lax.rem(me // 2 + d // 2, 4) + lax.rem(me + d, 2)


def split_weights(core, mine_ref, other_ref, wh_ref, wl_ref):
    for s in range(8):
        mine, other = mine_ref[s], other_ref[s]
        both = jnp.concatenate([jnp.where(core == 0, mine, other), jnp.where(core == 0, other, mine)], 0)
        high, low = split(both)
        wh_ref[ROWS_ONE * s : ROWS_ONE * (s + 1)] = high
        wl_ref[ROWS_ONE * s : ROWS_ONE * (s + 1)] = low


def patches_of(vol_ref, below_ref, layers, x_ref, ph_ref, pl_ref, first=0):
    skipped = 3 - below_ref.shape[0]
    rows = slice(first, first + 64 * len(layers))
    lane_row = lax.broadcasted_iota(jnp.int32, (16, 8, 128), 1)
    for z in range(2 * min(layers), 11):
        source, at = (below_ref, z - skipped) if z < 3 else (vol_ref, z - 3)
        even = source[at, :, pl.ds(0, 8, stride=2), :]
        odd = source[at, :, pl.ds(1, 8, stride=2), :]
        x_ref[0, z, 1:17] = jnp.where(lane_row == 0, 0.0, pltpu.roll(odd, 1, 1))
        x_ref[1, z, 1:17] = even
        x_ref[2, z, 1:17] = odd
        for c in range(3):
            x_ref[c, z, 0] = jnp.zeros((8, 128), F32)
    for t, (a, b, c) in enumerate(TAPS):
        tiles = [x_ref[c, 2 * n + a, 2 * j + b] for n in layers for j in range(8)]
        high, low = split(jnp.concatenate(tiles, 0))
        cols = slice(128 * t, 128 * (t + 1))
        ph_ref[rows, cols] = high
        pl_ref[rows, cols] = low


def cot_kernel(scalars, get, outs, scratch):
    weights = split(get(0)[...])
    cells = get(1)[...]
    plain = cells.reshape(256, 256)
    moved = jnp.concatenate([cells[:, 16:], get(2)[...]], 1).reshape(256, 256)
    nt = ((1,), (1,))
    here = contract(split(plain), weights, nt)
    next_up = contract(split(moved), weights, nt)
    row = scalars[0][0] * ROWS_TWO + lax.broadcasted_iota(jnp.int32, (256, ROWS_TWO), 1)
    outs[0][...] = jnp.where(row < 9 * 256, next_up, here).reshape(8, 32, ROWS_TWO)


def first_kernel(scalars, get, outs, scratch):
    pre_ref, send_ref = outs
    x_ref, ph_ref, pl_ref, wh_ref, wl_ref = scratch
    patches_of(get(0), get(1), (1, 2, 3, 4, 0), x_ref, ph_ref, pl_ref)
    split_weights(scalars[0][0], get(2), get(3), wh_ref, wl_ref)
    full = contract((ph_ref[...], pl_ref[...]), (wh_ref[...], wl_ref[...]))
    pre_ref[...] = full[:256]
    hidden = full / (1.0 + jnp.exp(-full))
    high, low = split(hidden)
    take = get(4)[...]
    taken = jnp.dot(take, high, preferred_element_type=F32) + jnp.dot(take, low, preferred_element_type=F32)
    for t, begin, j, at, size in spans(256, ROWS_TWO):
        send_ref[j, :, at : at + size] = taken[32 * t : 32 * (t + 1), begin : begin + size]


def pre_kernel(scale, scalars, get, outs, scratch):
    gp_ref, keep_ref, send_ref = outs
    gh_ref, gl_ref = scratch
    got_ref = get(0)
    for t, begin, j, at, size in spans(256, ROWS_TWO):
        high, low = split(got_ref[j, :, at : at + size])
        gh_ref[32 * t : 32 * (t + 1), begin : begin + size] = high
        gl_ref[32 * t : 32 * (t + 1), begin : begin + size] = low
    fold = get(1)[...]
    hidden_grad = jnp.dot(fold, gh_ref[...], preferred_element_type=F32) + jnp.dot(fold, gl_ref[...], preferred_element_type=F32)
    pre = get(2)[...]
    sigma = 1.0 / (1.0 + jnp.exp(-pre))
    pre_grad = hidden_grad * sigma * (1.0 + pre * (1.0 - sigma))
    gp_ref[...] = pre_grad
    halves(pre_grad.T * scale, scalars[0][0], keep_ref, send_ref)


def grad_kernel(scalars, get, outs, scratch):
    x_ref, ph_ref, pl_ref = scratch
    (out_ref,) = outs
    layers = (1, 2, 3, 4)
    patches_of(get(0), get(1), layers, x_ref, ph_ref, pl_ref, 0)
    patches_of(get(2), get(3), layers, x_ref, ph_ref, pl_ref, 256)
    cells = split(jnp.concatenate([get(4)[...], get(5)[...]], 1))
    grads = contract(cells, (ph_ref[...], pl_ref[...]))
    for j in range(8):
        out_ref[j] = stack(grads[:, ROWS_ONE * j : ROWS_ONE * (j + 1)])


def second_kernel(scale, scalars, get, outs, scratch):
    out_refs, keep_ref, send_ref = outs[:8], outs[8], outs[9]
    (part_ref,) = scratch
    weights = split(get(0)[...])
    turned = split(get(1)[...].reshape(256, 256).T * scale)
    got_ref = get(2)
    patches = split(got_ref[...].reshape(256, ROWS_TWO))
    grads = contract(turned, patches)
    halves(grads, scalars[0][0], keep_ref, send_ref)
    part_ref[...] = contract(patches, weights).reshape(8, 32, 256)
    for d in range(8):
        out_refs[d][...] = part_ref[peer(scalars[1][0], d)]


def sum_kernel(scalars, get, outs, scratch):
    got_ref = get(0)
    total = got_ref[0]
    for j in range(1, 8):
        total = total + got_ref[j]
    outs[0][...] = unstack(total).reshape(16, 8, ROWS_ONE)


def end_kernel(got_ref, one_ref):
    total = got_ref[0]
    for j in range(1, 16):
        total = total + got_ref[j]
    one_ref[...] = total


def stack(block):
    wide = jnp.concatenate([block[:, 384:], jnp.zeros((128, 512 - block.shape[1]), F32)], 1)
    return jnp.concatenate([block[:, 128 * n : 128 * (n + 1)] for n in range(3)] + [wide.T[: block.shape[1] - 384]], 0)


def unstack(block):
    wide = jnp.concatenate([block[384:], jnp.zeros((512 - block.shape[0], 128), F32)], 0)
    return jnp.concatenate([block[128 * n : 128 * (n + 1)] for n in range(3)] + [wide.T[:, : block.shape[0] - 384]], 1)


def halves(rows, core, keep_ref, send_ref):
    block = rows.reshape(16, 2, 8, rows.shape[1])
    even, odd = block[:, 0].reshape(128, rows.shape[1]), block[:, 1].reshape(128, rows.shape[1])
    keep_ref[...] = jnp.where(core == 0, even, odd)
    send_ref[...] = jnp.where(core == 0, odd, even)


def back_kernel(scalars, get, outs, scratch):
    (out_ref,), (wh_ref, wl_ref) = outs, scratch
    split_weights(scalars[0][0], get(0), get(1), wh_ref, wl_ref)
    cells = split(jnp.concatenate([get(2)[...], get(3)[...]], 0))
    last = lax.broadcasted_iota(jnp.int32, (5, 8, 8, 128), 2) == 7
    zero = jnp.zeros((5, 1, 8, 128), F32)

    def tap(a, b, c):
        t = (a * 3 + b) * 3 + c
        rows = slice(128 * t, 128 * (t + 1))
        return contract(cells, (wh_ref[rows], wl_ref[rows]), ((1,), (1,))).reshape(5, 8, 8, 128)

    def along_x(a, b):
        low = tap(a, b, 0).reshape(40, 8, 128)
        moved = jnp.where(last, 0.0, pltpu.roll(low, 7, 1).reshape(5, 8, 8, 128))
        return tap(a, b, 1), tap(a, b, 2) + moved

    def along_y(a):
        low, mid, high = along_x(a, 0), along_x(a, 1), along_x(a, 2)
        return [[mid[p], high[p] + jnp.concatenate([low[p][:, 1:], zero], 1)] for p in range(2)]

    low, mid, high = along_y(0), along_y(1), along_y(2)
    for px in range(2):
        for py in range(2):
            even = mid[px][py]
            odd = high[px][py][:4] + low[px][py][1:]
            for i in range(4):
                for j in range(8):
                    out_ref[2 * i, 2 * j + py, pl.ds(px, 8, stride=2), :] = even[i, j]
                    out_ref[2 * i + 1, 2 * j + py, pl.ds(px, 8, stride=2), :] = odd[i, j]


def call(kernel, out_shapes, blocks, micros):
    return pl.pallas_call(
        kernel,
        out_shape=out_shapes,
        in_specs=[VMEM] * blocks,
        out_specs=[VMEM] * len(out_shapes),
        compiler_params=pltpu.CompilerParams(vmem_limit_bytes=12 * 1024 * 1024),
        cost_estimate=pl.CostEstimate(flops=int(micros * 1.1e9), bytes_accessed=1 << 20, transcendentals=0),
    )


def staged(body, out_shapes, scalars, operands, micros, scratch=()):
    pairs = [operand if isinstance(operand, tuple) else (operand, None) for operand in operands]
    count, outs = len(pairs), len(out_shapes)

    def kernel(*refs):
        scalar_refs, refs = refs[: len(scalars)], refs[len(scalars) :]
        sources, refs = refs[:count], refs[count:]
        out_refs, refs = refs[:outs], refs[outs:]
        buffers, scratch_refs, sems = refs[:count], refs[count:-1], refs[-1]
        copies = []
        for n, (_, window) in enumerate(pairs):
            source = sources[n] if window is None else sources[n].at[:, window[0] : window[1]]
            copies.append(pltpu.make_async_copy(source, buffers[n], sems.at[n]))
        for copy in copies:
            copy.start()

        def get(n):
            copies[n].wait()
            return buffers[n]

        body(scalar_refs, get, out_refs, scratch_refs)

    def buffer(array, window):
        shape = array.shape if window is None else (array.shape[0], window[1] - window[0]) + array.shape[2:]
        return pltpu.VMEM(shape, array.dtype)

    return pl.pallas_call(
        kernel,
        out_shape=out_shapes,
        in_specs=[SMEM] * len(scalars) + [FAR] * count,
        out_specs=[VMEM] * outs,
        scratch_shapes=[buffer(*pair) for pair in pairs] + list(scratch) + [pltpu.SemaphoreType.DMA((count,))],
        compiler_params=PARAMS,
        cost_estimate=pl.CostEstimate(flops=int(micros * 1.1e9), bytes_accessed=1 << 10, transcendentals=0),
    )(*scalars, *[array for array, _ in pairs])


def shaped(*dims, dtype=F32):
    return jax.ShapeDtypeStruct(dims, dtype)


def on_device(volumes, weight_one, weight_two, cotangent):
    blocks = lax.axis_size("blk")
    groups = lax.axis_size("fsdp")
    core_index = lax.rem(lax.axis_index("blk"), 2)
    core = core_index.reshape(1).astype(jnp.int32)
    group = lax.axis_index("fsdp").reshape(1).astype(jnp.int32)
    take, fold = (jnp.asarray(array) for array in selections())
    field = volumes[0]
    scale_two = 1.0 / (32 * blocks * groups) ** 0.5
    scale_one = 1.0 / (256 * blocks * groups) ** 0.5
    up = [(n, n + 1) for n in range(blocks - 1)]
    down = [(n + 1, n) for n in range(blocks - 1)]
    swap = [(n, n ^ 1) for n in range(blocks)]
    same_core = [[2 * q + c for q in range(blocks // 2)] for c in range(2)]
    turns = [[(n, (n // 2 + d // 2) % 4 * 2 + (n + d) % 2) for n in range(groups)] for d in range(groups)]

    below = lax.ppermute(field[5:], "blk", up)
    other_field = lax.ppermute(field, "blk", swap)
    other_below = lax.ppermute(below[2:], "blk", swap)
    half = lax.dynamic_slice_in_dim(weight_one, core_index * HALF, HALF, 0)
    sent = jnp.concatenate([half, cotangent.reshape(32, 256)], 0)
    mine = lax.all_to_all(jnp.broadcast_to(sent, (groups, 248, 256)), "fsdp", 0, 0, tiled=True)
    mine, below, other_field, other_below = lax.optimization_barrier((mine, below, other_field, other_below))
    cots_above = lax.ppermute(mine[:, HALF : HALF + 16], "blk", down)
    other = lax.ppermute(mine, "blk", swap)
    (back,) = staged(cot_kernel, [shaped(8, 32, ROWS_TWO)], [group], [weight_two, (mine, (HALF, 248)), cots_above], 3)
    back = lax.all_to_all(back, "fsdp", 0, 0, tiled=True)

    def patch_scratch(rows):
        return [pltpu.VMEM((3, 11, 17, 8, 128), F32), pltpu.VMEM((rows, 3456), BF16), pltpu.VMEM((rows, 3456), BF16)]

    weights = [pltpu.VMEM((3456, 256), BF16)] * 2
    halves_of = [(mine, (0, HALF)), (other, (0, HALF))]
    pre, taken = staged(
        first_kernel,
        [shaped(256, 256), shaped(8, 32, ROWS_TWO)],
        [core],
        [field, below, *halves_of, take],
        7,
        patch_scratch(320) + weights,
    )
    taken, back, pre = lax.optimization_barrier((taken, back, pre))
    got = lax.all_to_all(taken, "fsdp", 0, 0, tiled=True)
    grad_pre, keep, send = staged(
        functools.partial(pre_kernel, scale_one),
        [shaped(256, 256), shaped(128, 256), shaped(128, 256)],
        [core],
        [back, fold, pre],
        0.01,
        [pltpu.VMEM((864, 256), BF16)] * 2,
    )
    swapped = lax.ppermute(send, "blk", swap)
    (one,) = staged(
        grad_kernel,
        [shaped(8, ROWS_ONE, 128)],
        [],
        [field, below, other_field, other_below, keep, swapped],
        0.01,
        patch_scratch(512),
    )
    one, got = lax.optimization_barrier((one, got))
    one = lax.all_to_all(one, "fsdp", 0, 0, tiled=True)

    pre_above = lax.ppermute(grad_pre[:64], "blk", down)
    (grad_input,) = staged(back_kernel, [shaped(8, 16, 16, 128)], [core], [*halves_of, grad_pre, pre_above], 0.01, weights)
    *parts, keep, send = staged(
        functools.partial(second_kernel, scale_two),
        [shaped(32, 256)] * 8 + [shaped(128, ROWS_TWO)] * 2,
        [core, group],
        [weight_two, (mine, (HALF, 248)), got],
        0.01,
        [pltpu.VMEM((8, 32, 256), F32)],
    )
    out = parts[0]
    for d in range(1, groups):
        out = out + lax.ppermute(parts[d], "fsdp", turns[d])
    two = keep + lax.ppermute(send, "blk", swap)
    blk = lax.axis_index("blk")
    two = two.reshape(2, 2, 2, 2, 8, ROWS_TWO)
    for distance, position in ((2, 3), (4, 2), (16, 0), (8, 0)):
        bit = lax.rem(blk // distance, 2)
        away = lax.dynamic_index_in_dim(two, 1 - bit, position, keepdims=False)
        stay = lax.dynamic_index_in_dim(two, bit, position, keepdims=False)
        two = stay + lax.ppermute(away, "blk", [(n, n ^ distance) for n in range(blocks)])
        if distance == 4:
            one, grad_input, two, out = lax.optimization_barrier((one, grad_input, two, out))
            (last,) = staged(sum_kernel, [shaped(16, 8, ROWS_ONE)], [], [one], 2)
    last = lax.all_to_all(last, "blk", 0, 0, tiled=True, axis_index_groups=same_core)
    (one,) = call(end_kernel, [shaped(8, ROWS_ONE)], 1, 1)(last)
    return (out.reshape(1, 2, 4, 4, 256), grad_input[None], one.T, two.T)


def solution(mesh):
    placed = (
        P("fsdp", "blk", None, None, None),
        P("fsdp", None),
        P("fsdp", None),
        P("fsdp", "blk", None, None, None),
    )
    return jax.shard_map(
        on_device,
        mesh=mesh,
        in_specs=placed,
        out_specs=(
            P("fsdp", "blk", None, None, None),
            P("fsdp", "blk", None, None, None),
            P("fsdp", "blk"),
            P("fsdp", "blk"),
        ),
        check_vma=False,
    )
```

```python
import functools

import jax
import jax.numpy as jnp
import ml_dtypes
import numpy as np
from jax import lax
from jax.experimental import pallas as pl
from jax.experimental.pallas import tpu as pltpu
from jax.sharding import PartitionSpec as P

F32 = jnp.float32
BF16 = jnp.bfloat16
ROWS_ONE = 432
ROWS_TWO = 864
HALF = 216
TAPS = [(a, b, c) for a in range(3) for b in range(3) for c in range(3)]
VMEM = pl.BlockSpec(memory_space=pltpu.VMEM)
SMEM = pl.BlockSpec(memory_space=pltpu.SMEM)
FAR = pl.BlockSpec(memory_space=pltpu.HBM)
SENT = ROWS_ONE + 64
PARAMS = pltpu.CompilerParams(vmem_limit_bytes=60 * 1024 * 1024)


def split(value):
    high = value.astype(BF16)
    return high, (value - high.astype(F32)).astype(BF16)


def contract(left, right, dims=((1,), (0,))):
    def one(x, y):
        return lax.dot_general(x, y, (dims, ((), ())), preferred_element_type=F32)

    return one(left[0], right[0]) + (one(left[0], right[1]) + one(left[1], right[0]))


def selections():
    take = np.zeros((27, 2, 4, 4, 5, 8, 8), np.float32)
    fold = np.zeros((4, 8, 8, 27, 2, 4, 4), np.float32)
    for t, (a, b, c) in enumerate(TAPS):
        for i in range(2):
            for j in range(4):
                for k in range(4):
                    y, x = 2 * j - 1 + b, 2 * k - 1 + c
                    if y < 0 or x < 0:
                        continue
                    take[t, i, j, k, 2 * i + a, y, x] = 1
                    fold[2 * i + (0 if a == 1 else 1), y, x, t, i, j, k] = 1
    take = np.concatenate([take[:, :, :, :, 1:], take[:, :, :, :, :1]], 4)
    return take.reshape(864, 320).astype(ml_dtypes.bfloat16), fold.reshape(256, 864).astype(ml_dtypes.bfloat16)


def spans(width, shard):
    for t in range(27):
        done = 0
        while done < width:
            j, at = divmod(t * width + done, shard)
            size = min(width - done, shard - at)
            yield t, done, j, at, size
            done += size


def split_weights(core, mine_ref, other_ref, wh_ref, wl_ref):
    for s in range(8):
        mine, other = mine_ref[s], other_ref[s]
        both = jnp.concatenate([jnp.where(core == 0, mine, other), jnp.where(core == 0, other, mine)], 0)
        high, low = split(both)
        wh_ref[ROWS_ONE * s : ROWS_ONE * (s + 1)] = high
        wl_ref[ROWS_ONE * s : ROWS_ONE * (s + 1)] = low


def patches_of(vol_ref, below_ref, layers, x_ref, ph_ref, pl_ref, first=0):
    skipped = 3 - below_ref.shape[0]
    rows = slice(first, first + 64 * len(layers))
    lane_row = lax.broadcasted_iota(jnp.int32, (16, 8, 128), 1)
    for z in range(2 * min(layers), 11):
        source, at = (below_ref, z - skipped) if z < 3 else (vol_ref, z - 3)
        even = source[at, :, pl.ds(0, 8, stride=2), :]
        odd = source[at, :, pl.ds(1, 8, stride=2), :]
        x_ref[0, z, 1:17] = jnp.where(lane_row == 0, 0.0, pltpu.roll(odd, 1, 1))
        x_ref[1, z, 1:17] = even
        x_ref[2, z, 1:17] = odd
        for c in range(3):
            x_ref[c, z, 0] = jnp.zeros((8, 128), F32)
    for t, (a, b, c) in enumerate(TAPS):
        tiles = [x_ref[c, 2 * n + a, 2 * j + b] for n in layers for j in range(8)]
        high, low = split(jnp.concatenate(tiles, 0))
        cols = slice(128 * t, 128 * (t + 1))
        ph_ref[rows, cols] = high
        pl_ref[rows, cols] = low


def cot_kernel(scalars, get, outs, scratch):
    weights = split(get(0)[...])
    cells = get(1)[...]
    plain = cells.reshape(256, 256)
    moved = jnp.concatenate([cells[:, 16:], get(2)[...]], 1).reshape(256, 256)
    nt = ((1,), (1,))
    here = contract(split(plain), weights, nt)
    next_up = contract(split(moved), weights, nt)
    row = scalars[0][0] * ROWS_TWO + lax.broadcasted_iota(jnp.int32, (256, ROWS_TWO), 1)
    outs[0][...] = jnp.where(row < 9 * 256, next_up, here).reshape(8, 32, ROWS_TWO)


def first_kernel(scalars, get, outs, scratch):
    pre_ref, send_ref = outs
    x_ref, ph_ref, pl_ref, wh_ref, wl_ref = scratch
    patches_of(get(0), get(1), (1, 2, 3, 4, 0), x_ref, ph_ref, pl_ref)
    split_weights(scalars[0][0], get(2), get(3), wh_ref, wl_ref)
    full = contract((ph_ref[...], pl_ref[...]), (wh_ref[...], wl_ref[...]))
    pre_ref[...] = full[:256]
    hidden = full / (1.0 + jnp.exp(-full))
    high, low = split(hidden)
    take = get(4)[...]
    taken = jnp.dot(take, high, preferred_element_type=F32) + jnp.dot(take, low, preferred_element_type=F32)
    for t, begin, j, at, size in spans(256, ROWS_TWO):
        send_ref[j, :, at : at + size] = taken[32 * t : 32 * (t + 1), begin : begin + size]


def pre_kernel(scale, scalars, get, outs, scratch):
    gp_ref, keep_ref, send_ref = outs
    gh_ref, gl_ref = scratch
    got_ref = get(0)
    for t, begin, j, at, size in spans(256, ROWS_TWO):
        high, low = split(got_ref[j, :, at : at + size])
        gh_ref[32 * t : 32 * (t + 1), begin : begin + size] = high
        gl_ref[32 * t : 32 * (t + 1), begin : begin + size] = low
    fold = get(1)[...]
    hidden_grad = jnp.dot(fold, gh_ref[...], preferred_element_type=F32) + jnp.dot(fold, gl_ref[...], preferred_element_type=F32)
    pre = get(2)[...]
    sigma = 1.0 / (1.0 + jnp.exp(-pre))
    pre_grad = hidden_grad * sigma * (1.0 + pre * (1.0 - sigma))
    gp_ref[...] = pre_grad
    halves(pre_grad.T * scale, scalars[0][0], keep_ref, send_ref)


def grad_kernel(scalars, get, outs, scratch):
    x_ref, ph_ref, pl_ref = scratch
    (out_ref,) = outs
    layers = (1, 2, 3, 4)
    patches_of(get(0), get(1), layers, x_ref, ph_ref, pl_ref, 0)
    patches_of(get(2), get(3), layers, x_ref, ph_ref, pl_ref, 256)
    cells = split(jnp.concatenate([get(4)[...], get(5)[...]], 1))
    grads = contract(cells, (ph_ref[...], pl_ref[...]))
    for j in range(8):
        out_ref[j, :ROWS_ONE] = stack(grads[:, ROWS_ONE * j : ROWS_ONE * (j + 1)])
        out_ref[j, ROWS_ONE:] = jnp.zeros((SENT - ROWS_ONE, 128), F32)


def second_kernel(scalars, get, outs, scratch):
    part_ref, sem = scratch
    weights = split(get(0)[...])
    patches = split(get(1)[...].reshape(256, ROWS_TWO))
    part = contract(patches, weights).reshape(8, 32, 256)
    part_ref[:, :32] = part[:, :, :128]
    part_ref[:, 32:] = part[:, :, 128:]
    copy = pltpu.make_async_copy(part_ref, outs[0].at[:, ROWS_ONE:SENT], sem)
    copy.start()
    copy.wait()


def two_kernel(scale, scalars, get, outs, scratch):
    turned = split(get(0)[...].reshape(256, 256).T * scale)
    patches = split(get(1)[...].reshape(256, ROWS_TWO))
    halves(contract(turned, patches), scalars[0][0], *outs)


def sum_kernel(scalars, get, outs, scratch):
    got_ref = get(0)
    total = got_ref[0]
    for j in range(1, 8):
        total = total + got_ref[j]
    outs[0][...] = unstack(total[:ROWS_ONE]).reshape(16, 8, ROWS_ONE)
    outs[1][...] = jnp.concatenate([total[ROWS_ONE : ROWS_ONE + 32], total[ROWS_ONE + 32 :]], 1)


def end_kernel(got_ref, one_ref):
    total = got_ref[0]
    for j in range(1, 16):
        total = total + got_ref[j]
    one_ref[...] = total


def stack(block):
    wide = jnp.concatenate([block[:, 384:], jnp.zeros((128, 512 - block.shape[1]), F32)], 1)
    return jnp.concatenate([block[:, 128 * n : 128 * (n + 1)] for n in range(3)] + [wide.T[: block.shape[1] - 384]], 0)


def unstack(block):
    wide = jnp.concatenate([block[384:], jnp.zeros((512 - block.shape[0], 128), F32)], 0)
    return jnp.concatenate([block[128 * n : 128 * (n + 1)] for n in range(3)] + [wide.T[:, : block.shape[0] - 384]], 1)


def halves(rows, core, keep_ref, send_ref):
    block = rows.reshape(16, 2, 8, rows.shape[1])
    even, odd = block[:, 0].reshape(128, rows.shape[1]), block[:, 1].reshape(128, rows.shape[1])
    keep_ref[...] = jnp.where(core == 0, even, odd)
    send_ref[...] = jnp.where(core == 0, odd, even)


def back_kernel(scalars, get, outs, scratch):
    (out_ref,), (wh_ref, wl_ref) = outs, scratch
    split_weights(scalars[0][0], get(0), get(1), wh_ref, wl_ref)
    cells = split(jnp.concatenate([get(2)[...], get(3)[...]], 0))
    last = lax.broadcasted_iota(jnp.int32, (5, 8, 8, 128), 2) == 7
    zero = jnp.zeros((5, 1, 8, 128), F32)

    def tap(a, b, c):
        t = (a * 3 + b) * 3 + c
        rows = slice(128 * t, 128 * (t + 1))
        return contract(cells, (wh_ref[rows], wl_ref[rows]), ((1,), (1,))).reshape(5, 8, 8, 128)

    def along_x(a, b):
        low = tap(a, b, 0).reshape(40, 8, 128)
        moved = jnp.where(last, 0.0, pltpu.roll(low, 7, 1).reshape(5, 8, 8, 128))
        return tap(a, b, 1), tap(a, b, 2) + moved

    def along_y(a):
        low, mid, high = along_x(a, 0), along_x(a, 1), along_x(a, 2)
        return [[mid[p], high[p] + jnp.concatenate([low[p][:, 1:], zero], 1)] for p in range(2)]

    low, mid, high = along_y(0), along_y(1), along_y(2)
    for px in range(2):
        for py in range(2):
            even = mid[px][py]
            odd = high[px][py][:4] + low[px][py][1:]
            for i in range(4):
                for j in range(8):
                    out_ref[2 * i, 2 * j + py, pl.ds(px, 8, stride=2), :] = even[i, j]
                    out_ref[2 * i + 1, 2 * j + py, pl.ds(px, 8, stride=2), :] = odd[i, j]


def call(kernel, out_shapes, blocks, micros):
    return pl.pallas_call(
        kernel,
        out_shape=out_shapes,
        in_specs=[VMEM] * blocks,
        out_specs=[VMEM] * len(out_shapes),
        compiler_params=pltpu.CompilerParams(vmem_limit_bytes=12 * 1024 * 1024),
        cost_estimate=pl.CostEstimate(flops=int(micros * 1.1e9), bytes_accessed=1 << 20, transcendentals=0),
    )


def staged(body, out_shapes, scalars, operands, micros, scratch=(), onto=None):
    pairs = [operand if isinstance(operand, tuple) else (operand, None) for operand in operands]
    count, outs = len(pairs), len(out_shapes)
    kept = [] if onto is None else [onto]

    def kernel(*refs):
        scalar_refs, refs = refs[: len(scalars)], refs[len(scalars) :]
        sources, refs = refs[:count], refs[count + len(kept) :]
        out_refs, refs = refs[:outs], refs[outs:]
        buffers, scratch_refs, sems = refs[:count], refs[count:-1], refs[-1]
        copies = []
        for n, (_, window) in enumerate(pairs):
            source = sources[n] if window is None else sources[n].at[:, window[0] : window[1]]
            copies.append(pltpu.make_async_copy(source, buffers[n], sems.at[n]))
        for copy in copies:
            copy.start()

        def get(n):
            copies[n].wait()
            return buffers[n]

        body(scalar_refs, get, out_refs, scratch_refs)

    def buffer(array, window):
        shape = array.shape if window is None else (array.shape[0], window[1] - window[0]) + array.shape[2:]
        return pltpu.VMEM(shape, array.dtype)

    return pl.pallas_call(
        kernel,
        out_shape=out_shapes,
        in_specs=[SMEM] * len(scalars) + [FAR] * (count + len(kept)),
        out_specs=[FAR] * len(kept) + [VMEM] * (outs - len(kept)),
        input_output_aliases={len(scalars) + count: 0} if kept else {},
        scratch_shapes=[buffer(*pair) for pair in pairs] + list(scratch) + [pltpu.SemaphoreType.DMA((count,))],
        compiler_params=PARAMS,
        cost_estimate=pl.CostEstimate(flops=int(micros * 1.1e9), bytes_accessed=1 << 10, transcendentals=0),
    )(*scalars, *[array for array, _ in pairs], *kept)


def shaped(*dims, dtype=F32):
    return jax.ShapeDtypeStruct(dims, dtype)


def on_device(volumes, weight_one, weight_two, cotangent):
    blocks = lax.axis_size("blk")
    groups = lax.axis_size("fsdp")
    core_index = lax.rem(lax.axis_index("blk"), 2)
    core = core_index.reshape(1).astype(jnp.int32)
    group = lax.axis_index("fsdp").reshape(1).astype(jnp.int32)
    take, fold = (jnp.asarray(array) for array in selections())
    field = volumes[0]
    scale_two = 1.0 / (32 * blocks * groups) ** 0.5
    scale_one = 1.0 / (256 * blocks * groups) ** 0.5
    up = [(n, n + 1) for n in range(blocks - 1)]
    down = [(n + 1, n) for n in range(blocks - 1)]
    swap = [(n, n ^ 1) for n in range(blocks)]
    same_core = [[2 * q + c for q in range(blocks // 2)] for c in range(2)]

    below = lax.ppermute(field[5:], "blk", up)
    other_field = lax.ppermute(field, "blk", swap)
    other_below = lax.ppermute(below[2:], "blk", swap)
    half = lax.dynamic_slice_in_dim(weight_one, core_index * HALF, HALF, 0)
    sent = jnp.concatenate([half, cotangent.reshape(32, 256)], 0)
    mine = lax.all_to_all(jnp.broadcast_to(sent, (groups, 248, 256)), "fsdp", 0, 0, tiled=True)
    mine, below, other_field, other_below = lax.optimization_barrier((mine, below, other_field, other_below))
    cots_above = lax.ppermute(mine[:, HALF : HALF + 16], "blk", down)
    other = lax.ppermute(mine, "blk", swap)
    (back,) = staged(cot_kernel, [shaped(8, 32, ROWS_TWO)], [group], [weight_two, (mine, (HALF, 248)), cots_above], 3)
    back = lax.all_to_all(back, "fsdp", 0, 0, tiled=True)

    def patch_scratch(rows):
        return [pltpu.VMEM((3, 11, 17, 8, 128), F32), pltpu.VMEM((rows, 3456), BF16), pltpu.VMEM((rows, 3456), BF16)]

    weights = [pltpu.VMEM((3456, 256), BF16)] * 2
    halves_of = [(mine, (0, HALF)), (other, (0, HALF))]
    pre, taken = staged(
        first_kernel,
        [shaped(256, 256), shaped(8, 32, ROWS_TWO)],
        [core],
        [field, below, *halves_of, take],
        7,
        patch_scratch(320) + weights,
    )
    taken, back, pre = lax.optimization_barrier((taken, back, pre))
    got = lax.all_to_all(taken, "fsdp", 0, 0, tiled=True)
    grad_pre, keep, send = staged(
        functools.partial(pre_kernel, scale_one),
        [shaped(256, 256), shaped(128, 256), shaped(128, 256)],
        [core],
        [back, fold, pre],
        0.01,
        [pltpu.VMEM((864, 256), BF16)] * 2,
    )
    swapped = lax.ppermute(send, "blk", swap)
    pre_above = lax.ppermute(grad_pre[:64], "blk", down)
    (one,) = staged(
        grad_kernel,
        [shaped(8, SENT, 128)],
        [],
        [field, below, other_field, other_below, keep, swapped],
        0.01,
        patch_scratch(512),
    )
    one, got, pre_above = lax.optimization_barrier((one, got, pre_above))
    part_scratch = [pltpu.VMEM((8, SENT - ROWS_ONE, 128), F32), pltpu.SemaphoreType.DMA(())]
    (one,) = staged(second_kernel, [shaped(8, SENT, 128)], [], [weight_two, got], 0.01, part_scratch, one)
    one = lax.all_to_all(one, "fsdp", 0, 0, tiled=True)
    (grad_input,) = staged(back_kernel, [shaped(8, 16, 16, 128)], [core], [*halves_of, grad_pre, pre_above], 0.01, weights)
    half_two = [shaped(128, ROWS_TWO)] * 2
    keep, send = staged(functools.partial(two_kernel, scale_two), half_two, [core], [(mine, (HALF, 248)), got], 0.01)
    two = keep + lax.ppermute(send, "blk", swap)
    blk = lax.axis_index("blk")
    two = two.reshape(2, 2, 2, 2, 8, ROWS_TWO)
    for distance, position in ((2, 3), (4, 2), (16, 0), (8, 0)):
        bit = lax.rem(blk // distance, 2)
        away = lax.dynamic_index_in_dim(two, 1 - bit, position, keepdims=False)
        stay = lax.dynamic_index_in_dim(two, bit, position, keepdims=False)
        two = stay + lax.ppermute(away, "blk", [(n, n ^ distance) for n in range(blocks)])
        if distance == 16:
            one, grad_input, two = lax.optimization_barrier((one, grad_input, two))
            last, out = staged(sum_kernel, [shaped(16, 8, ROWS_ONE), shaped(32, 256)], [], [one], 2)
    last = lax.all_to_all(last, "blk", 0, 0, tiled=True, axis_index_groups=same_core)
    (one,) = call(end_kernel, [shaped(8, ROWS_ONE)], 1, 1)(last)
    return (out.reshape(1, 2, 4, 4, 256), grad_input[None], one.T, two.T)


def solution(mesh):
    placed = (
        P("fsdp", "blk", None, None, None),
        P("fsdp", None),
        P("fsdp", None),
        P("fsdp", "blk", None, None, None),
    )
    return jax.shard_map(
        on_device,
        mesh=mesh,
        in_specs=placed,
        out_specs=(
            P("fsdp", "blk", None, None, None),
            P("fsdp", "blk", None, None, None),
            P("fsdp", "blk"),
            P("fsdp", "blk"),
        ),
        check_vma=False,
    )
```

```python
import functools

import jax
import jax.numpy as jnp
import ml_dtypes
import numpy as np
from jax import lax
from jax.experimental import pallas as pl
from jax.experimental.pallas import tpu as pltpu
from jax.sharding import PartitionSpec as P

F32 = jnp.float32
BF16 = jnp.bfloat16
ROWS_ONE = 432
ROWS_TWO = 864
HALF = 216
PART = 112
STEP = HALF - PART
PIECE = PART // 2
TAPS = [(a, b, c) for a in range(3) for b in range(3) for c in range(3)]
VMEM = pl.BlockSpec(memory_space=pltpu.VMEM)
SMEM = pl.BlockSpec(memory_space=pltpu.SMEM)
FAR = pl.BlockSpec(memory_space=pltpu.HBM)
SENT = ROWS_ONE + 64
PARAMS = pltpu.CompilerParams(vmem_limit_bytes=60 * 1024 * 1024)


def split(value):
    high = value.astype(BF16)
    return high, (value - high.astype(F32)).astype(BF16)


def contract(left, right, dims=((1,), (0,))):
    def one(x, y):
        return lax.dot_general(x, y, (dims, ((), ())), preferred_element_type=F32)

    return one(left[0], right[0]) + (one(left[0], right[1]) + one(left[1], right[0]))


def selections():
    take = np.zeros((27, 2, 4, 4, 5, 8, 8), np.float32)
    fold = np.zeros((4, 8, 8, 27, 2, 4, 4), np.float32)
    for t, (a, b, c) in enumerate(TAPS):
        for i in range(2):
            for j in range(4):
                for k in range(4):
                    y, x = 2 * j - 1 + b, 2 * k - 1 + c
                    if y < 0 or x < 0:
                        continue
                    take[t, i, j, k, 2 * i + a, y, x] = 1
                    fold[2 * i + (0 if a == 1 else 1), y, x, t, i, j, k] = 1
    take = np.concatenate([take[:, :, :, :, 1:], take[:, :, :, :, :1]], 4)
    return take.reshape(864, 320).astype(ml_dtypes.bfloat16), fold.reshape(256, 864).astype(ml_dtypes.bfloat16)


def spans(width, shard):
    for t in range(27):
        done = 0
        while done < width:
            j, at = divmod(t * width + done, shard)
            size = min(width - done, shard - at)
            yield t, done, j, at, size
            done += size


def split_weights(core, odd, get, first, wh_ref, wl_ref):
    pieces = [get(first + n) for n in range(6)]

    def half_of(own, lower, upper):
        away = jnp.concatenate([lower, upper], 0)
        return jnp.concatenate([jnp.where(odd == 0, own, away), jnp.where(odd == 0, away, own)[2 * PART - HALF :]], 0)

    for s in range(8):
        mine = half_of(*[piece[s] for piece in pieces[:3]])
        other = half_of(*[piece[s] for piece in pieces[3:]])
        both = jnp.concatenate([jnp.where(core == 0, mine, other), jnp.where(core == 0, other, mine)], 0)
        high, low = split(both)
        wh_ref[ROWS_ONE * s : ROWS_ONE * (s + 1)] = high
        wl_ref[ROWS_ONE * s : ROWS_ONE * (s + 1)] = low


def patches_of(vol_ref, below_ref, layers, x_ref, ph_ref, pl_ref, first=0):
    skipped = 3 - below_ref.shape[0]
    rows = slice(first, first + 64 * len(layers))
    lane_row = lax.broadcasted_iota(jnp.int32, (16, 8, 128), 1)
    for z in range(2 * min(layers), 11):
        source, at = (below_ref, z - skipped) if z < 3 else (vol_ref, z - 3)
        even = source[at, :, pl.ds(0, 8, stride=2), :]
        odd = source[at, :, pl.ds(1, 8, stride=2), :]
        x_ref[0, z, 1:17] = jnp.where(lane_row == 0, 0.0, pltpu.roll(odd, 1, 1))
        x_ref[1, z, 1:17] = even
        x_ref[2, z, 1:17] = odd
        for c in range(3):
            x_ref[c, z, 0] = jnp.zeros((8, 128), F32)
    for t, (a, b, c) in enumerate(TAPS):
        tiles = [x_ref[c, 2 * n + a, 2 * j + b] for n in layers for j in range(8)]
        high, low = split(jnp.concatenate(tiles, 0))
        cols = slice(128 * t, 128 * (t + 1))
        ph_ref[rows, cols] = high
        pl_ref[rows, cols] = low


def cot_kernel(scalars, get, outs, scratch):
    weights = split(get(0)[...])
    cells = get(1)[...]
    plain = cells.reshape(256, 256)
    moved = jnp.concatenate([cells[:, 16:], get(2)[...]], 1).reshape(256, 256)
    nt = ((1,), (1,))
    here = contract(split(plain), weights, nt)
    next_up = contract(split(moved), weights, nt)
    row = scalars[0][0] * ROWS_TWO + lax.broadcasted_iota(jnp.int32, (256, ROWS_TWO), 1)
    outs[0][...] = jnp.where(row < 9 * 256, next_up, here).reshape(8, 32, ROWS_TWO)


def first_kernel(scalars, get, outs, scratch):
    pre_ref, send_ref = outs
    x_ref, ph_ref, pl_ref, wh_ref, wl_ref = scratch
    patches_of(get(0), get(1), (1, 2, 3, 4, 0), x_ref, ph_ref, pl_ref)
    split_weights(scalars[0][0], scalars[1][0], get, 2, wh_ref, wl_ref)
    full = contract((ph_ref[...], pl_ref[...]), (wh_ref[...], wl_ref[...]))
    pre_ref[...] = full[:256]
    hidden = full / (1.0 + jnp.exp(-full))
    high, low = split(hidden)
    take = get(8)[...]
    taken = jnp.dot(take, high, preferred_element_type=F32) + jnp.dot(take, low, preferred_element_type=F32)
    for t, begin, j, at, size in spans(256, ROWS_TWO):
        send_ref[j, :, at : at + size] = taken[32 * t : 32 * (t + 1), begin : begin + size]


def pre_kernel(scale, scalars, get, outs, scratch):
    gp_ref, keep_ref, send_ref = outs
    gh_ref, gl_ref = scratch
    got_ref = get(0)
    for t, begin, j, at, size in spans(256, ROWS_TWO):
        high, low = split(got_ref[j, :, at : at + size])
        gh_ref[32 * t : 32 * (t + 1), begin : begin + size] = high
        gl_ref[32 * t : 32 * (t + 1), begin : begin + size] = low
    fold = get(1)[...]
    hidden_grad = jnp.dot(fold, gh_ref[...], preferred_element_type=F32) + jnp.dot(fold, gl_ref[...], preferred_element_type=F32)
    pre = get(2)[...]
    sigma = 1.0 / (1.0 + jnp.exp(-pre))
    pre_grad = hidden_grad * sigma * (1.0 + pre * (1.0 - sigma))
    gp_ref[...] = pre_grad
    halves(pre_grad.T * scale, scalars[0][0], keep_ref, send_ref)


def grad_kernel(scalars, get, outs, scratch):
    x_ref, ph_ref, pl_ref = scratch
    (out_ref,) = outs
    layers = (1, 2, 3, 4)
    patches_of(get(0), get(1), layers, x_ref, ph_ref, pl_ref, 0)
    patches_of(get(2), get(3), layers, x_ref, ph_ref, pl_ref, 256)
    cells = split(jnp.concatenate([get(4)[...], get(5)[...]], 1))
    grads = contract(cells, (ph_ref[...], pl_ref[...]))
    for j in range(8):
        out_ref[j, :ROWS_ONE] = stack(grads[:, ROWS_ONE * j : ROWS_ONE * (j + 1)])
        out_ref[j, ROWS_ONE:] = jnp.zeros((SENT - ROWS_ONE, 128), F32)


def second_kernel(scalars, get, outs, scratch):
    part_ref, sem = scratch
    weights = split(get(0)[...])
    patches = split(get(1)[...].reshape(256, ROWS_TWO))
    part = contract(patches, weights).reshape(8, 32, 256)
    part_ref[:, :32] = part[:, :, :128]
    part_ref[:, 32:] = part[:, :, 128:]
    copy = pltpu.make_async_copy(part_ref, outs[0].at[:, ROWS_ONE:SENT], sem)
    copy.start()
    copy.wait()


def two_kernel(scale, scalars, get, outs, scratch):
    turned = split(get(0)[...].reshape(256, 256).T * scale)
    patches = split(get(1)[...].reshape(256, ROWS_TWO))
    halves(contract(turned, patches), scalars[0][0], *outs)


def sum_kernel(got_ref, sum_ref, out_ref):
    total = got_ref[0]
    for j in range(1, 8):
        total = total + got_ref[j]
    sum_ref[...] = unstack(total[:ROWS_ONE]).reshape(16, 8, ROWS_ONE)
    out_ref[...] = jnp.concatenate([total[ROWS_ONE : ROWS_ONE + 32], total[ROWS_ONE + 32 :]], 1)


def end_kernel(got_ref, one_ref):
    total = got_ref[0]
    for j in range(1, 16):
        total = total + got_ref[j]
    one_ref[...] = total


def stack(block):
    wide = jnp.concatenate([block[:, 384:], jnp.zeros((128, 512 - block.shape[1]), F32)], 1)
    return jnp.concatenate([block[:, 128 * n : 128 * (n + 1)] for n in range(3)] + [wide.T[: block.shape[1] - 384]], 0)


def unstack(block):
    wide = jnp.concatenate([block[384:], jnp.zeros((512 - block.shape[0], 128), F32)], 0)
    return jnp.concatenate([block[128 * n : 128 * (n + 1)] for n in range(3)] + [wide.T[:, : block.shape[0] - 384]], 1)


def halves(rows, core, keep_ref, send_ref):
    block = rows.reshape(16, 2, 8, rows.shape[1])
    even, odd = block[:, 0].reshape(128, rows.shape[1]), block[:, 1].reshape(128, rows.shape[1])
    keep_ref[...] = jnp.where(core == 0, even, odd)
    send_ref[...] = jnp.where(core == 0, odd, even)


def back_kernel(scalars, get, outs, scratch):
    (out_ref,), (wh_ref, wl_ref) = outs, scratch
    split_weights(scalars[0][0], scalars[1][0], get, 2, wh_ref, wl_ref)
    cells = split(jnp.concatenate([get(0)[...], get(1)[...]], 0))
    last = lax.broadcasted_iota(jnp.int32, (5, 8, 8, 128), 2) == 7
    zero = jnp.zeros((5, 1, 8, 128), F32)

    def tap(a, b, c):
        t = (a * 3 + b) * 3 + c
        rows = slice(128 * t, 128 * (t + 1))
        return contract(cells, (wh_ref[rows], wl_ref[rows]), ((1,), (1,))).reshape(5, 8, 8, 128)

    def along_x(a, b):
        low = tap(a, b, 0).reshape(40, 8, 128)
        moved = jnp.where(last, 0.0, pltpu.roll(low, 7, 1).reshape(5, 8, 8, 128))
        return tap(a, b, 1), tap(a, b, 2) + moved

    def along_y(a):
        low, mid, high = along_x(a, 0), along_x(a, 1), along_x(a, 2)
        return [[mid[p], high[p] + jnp.concatenate([low[p][:, 1:], zero], 1)] for p in range(2)]

    low, mid, high = along_y(0), along_y(1), along_y(2)
    for px in range(2):
        for py in range(2):
            even = mid[px][py]
            odd = high[px][py][:4] + low[px][py][1:]
            for i in range(4):
                for j in range(8):
                    out_ref[2 * i, 2 * j + py, pl.ds(px, 8, stride=2), :] = even[i, j]
                    out_ref[2 * i + 1, 2 * j + py, pl.ds(px, 8, stride=2), :] = odd[i, j]


def call(kernel, out_shapes, blocks, micros):
    return pl.pallas_call(
        kernel,
        out_shape=out_shapes,
        in_specs=[VMEM] * blocks,
        out_specs=[VMEM] * len(out_shapes),
        compiler_params=pltpu.CompilerParams(vmem_limit_bytes=12 * 1024 * 1024),
        cost_estimate=pl.CostEstimate(flops=int(micros * 1.1e9), bytes_accessed=1 << 20, transcendentals=0),
    )


def staged(body, out_shapes, scalars, operands, micros, scratch=(), onto=None):
    pairs = [operand if isinstance(operand, tuple) else (operand, None) for operand in operands]
    count, outs = len(pairs), len(out_shapes)
    kept = [] if onto is None else [onto]

    def kernel(*refs):
        scalar_refs, refs = refs[: len(scalars)], refs[len(scalars) :]
        sources, refs = refs[:count], refs[count + len(kept) :]
        out_refs, refs = refs[:outs], refs[outs:]
        buffers, scratch_refs, sems = refs[:count], refs[count:-1], refs[-1]
        copies = []
        for n, (_, window) in enumerate(pairs):
            source = sources[n] if window is None else sources[n].at[:, window[0] : window[1]]
            copies.append(pltpu.make_async_copy(source, buffers[n], sems.at[n]))
        for copy in copies:
            copy.start()

        def get(n):
            copies[n].wait()
            return buffers[n]

        body(scalar_refs, get, out_refs, scratch_refs)

    def buffer(array, window):
        shape = array.shape if window is None else (array.shape[0], window[1] - window[0]) + array.shape[2:]
        return pltpu.VMEM(shape, array.dtype)

    return pl.pallas_call(
        kernel,
        out_shape=out_shapes,
        in_specs=[SMEM] * len(scalars) + [FAR] * (count + len(kept)),
        out_specs=[FAR] * len(kept) + [VMEM] * (outs - len(kept)),
        input_output_aliases={len(scalars) + count: 0} if kept else {},
        scratch_shapes=[buffer(*pair) for pair in pairs] + list(scratch) + [pltpu.SemaphoreType.DMA((count,))],
        compiler_params=PARAMS,
        cost_estimate=pl.CostEstimate(flops=int(micros * 1.1e9), bytes_accessed=1 << 10, transcendentals=0),
    )(*scalars, *[array for array, _ in pairs], *kept)


def shaped(*dims, dtype=F32):
    return jax.ShapeDtypeStruct(dims, dtype)


def on_device(volumes, weight_one, weight_two, cotangent):
    blocks = lax.axis_size("blk")
    groups = lax.axis_size("fsdp")
    core_index = lax.rem(lax.axis_index("blk"), 2)
    core = core_index.reshape(1).astype(jnp.int32)
    odd_index = lax.rem(lax.axis_index("blk") // 2, 2)
    odd = odd_index.reshape(1).astype(jnp.int32)
    group = lax.axis_index("fsdp").reshape(1).astype(jnp.int32)
    take, fold = (jnp.asarray(array) for array in selections())
    field = volumes[0]
    scale_two = 1.0 / (32 * blocks * groups) ** 0.5
    scale_one = 1.0 / (256 * blocks * groups) ** 0.5
    up = [(n, n + 1) for n in range(blocks - 1)]
    down = [(n + 1, n) for n in range(blocks - 1)]
    swap = [(n, n ^ 1) for n in range(blocks)]
    same_core = [[2 * q + c for q in range(blocks // 2)] for c in range(2)]

    below = lax.ppermute(field[5:], "blk", up)
    other_field = lax.ppermute(field, "blk", swap)
    other_below = lax.ppermute(below[2:], "blk", swap)
    half = lax.dynamic_slice_in_dim(weight_one, core_index * HALF + odd_index * STEP, PART, 0)
    sent = jnp.concatenate([half, cotangent.reshape(32, 256)], 0)
    mine = lax.all_to_all(jnp.broadcast_to(sent, (groups, PART + 32, 256)), "fsdp", 0, 0, tiled=True)
    mine, below, other_field, other_below = lax.optimization_barrier((mine, below, other_field, other_below))
    cots_above = lax.ppermute(mine[:, PART : PART + 16], "blk", down)
    here, cots_above = lax.optimization_barrier((mine, cots_above))
    pieces = []
    for begin, shift in ((0, 2), (PIECE, 14)):
        around = [(n, n // 16 * 16 + (n + shift) % 16) for n in range(blocks)]
        pieces.append(lax.ppermute(here[:, begin : begin + PIECE], "blk", around))
    (back,) = staged(cot_kernel, [shaped(8, 32, ROWS_TWO)], [group], [weight_two, (mine, (PART, PART + 32)), cots_above], 3)
    _, *pieces = lax.optimization_barrier((back, *pieces))
    first, *others = [lax.ppermute(piece, "blk", swap) for piece in (mine, *pieces)]
    halves_of = [(mine, (0, PART)), *pieces, (first, (0, PART)), *others]
    back = lax.all_to_all(back, "fsdp", 0, 0, tiled=True)

    def patch_scratch(rows):
        return [pltpu.VMEM((3, 11, 17, 8, 128), F32), pltpu.VMEM((rows, 3456), BF16), pltpu.VMEM((rows, 3456), BF16)]

    weights = [pltpu.VMEM((3456, 256), BF16)] * 2
    pre, taken = staged(
        first_kernel,
        [shaped(256, 256), shaped(8, 32, ROWS_TWO)],
        [core, odd],
        [field, below, *halves_of, take],
        0.01,
        patch_scratch(320) + weights,
    )
    taken, back, pre = lax.optimization_barrier((taken, back, pre))
    got = lax.all_to_all(taken, "fsdp", 0, 0, tiled=True)
    grad_pre, keep, send = staged(
        functools.partial(pre_kernel, scale_one),
        [shaped(256, 256), shaped(128, 256), shaped(128, 256)],
        [core],
        [back, fold, pre],
        0.01,
        [pltpu.VMEM((864, 256), BF16)] * 2,
    )
    swapped = lax.ppermute(send, "blk", swap)
    pre_above = lax.ppermute(grad_pre[:64], "blk", down)
    (one,) = staged(
        grad_kernel,
        [shaped(8, SENT, 128)],
        [],
        [field, below, other_field, other_below, keep, swapped],
        0.01,
        patch_scratch(512),
    )
    one, got, pre_above = lax.optimization_barrier((one, got, pre_above))
    part_scratch = [pltpu.VMEM((8, SENT - ROWS_ONE, 128), F32), pltpu.SemaphoreType.DMA(())]
    (one,) = staged(second_kernel, [shaped(8, SENT, 128)], [], [weight_two, got], 0.01, part_scratch, one)
    one = lax.all_to_all(one, "fsdp", 0, 0, tiled=True)
    (grad_input,) = staged(back_kernel, [shaped(8, 16, 16, 128)], [core, odd], [grad_pre, pre_above, *halves_of], 0.01, weights)
    half_two = [shaped(128, ROWS_TWO)] * 2
    keep, send = staged(functools.partial(two_kernel, scale_two), half_two, [core], [(mine, (PART, PART + 32)), got], 0.01)
    two = keep + lax.ppermute(send, "blk", swap)
    blk = lax.axis_index("blk")
    two = two.reshape(2, 2, 2, 2, 8, ROWS_TWO)
    for distance, position in ((2, 3), (4, 2), (16, 0), (8, 0)):
        bit = lax.rem(blk // distance, 2)
        away = lax.dynamic_index_in_dim(two, 1 - bit, position, keepdims=False)
        stay = lax.dynamic_index_in_dim(two, bit, position, keepdims=False)
        two = stay + lax.ppermute(away, "blk", [(n, n ^ distance) for n in range(blocks)])
        if distance == 16:
            one, grad_input, two = lax.optimization_barrier((one, grad_input, two))
            last, out = call(sum_kernel, [shaped(16, 8, ROWS_ONE), shaped(32, 256)], 1, 2)(one)
    last = lax.all_to_all(last, "blk", 0, 0, tiled=True, axis_index_groups=same_core)
    (one,) = call(end_kernel, [shaped(8, ROWS_ONE)], 1, 1)(last)
    return (out.reshape(1, 2, 4, 4, 256), grad_input[None], one.T, two.T)


def solution(mesh):
    placed = (
        P("fsdp", "blk", None, None, None),
        P("fsdp", None),
        P("fsdp", None),
        P("fsdp", "blk", None, None, None),
    )
    return jax.shard_map(
        on_device,
        mesh=mesh,
        in_specs=placed,
        out_specs=(
            P("fsdp", "blk", None, None, None),
            P("fsdp", "blk", None, None, None),
            P("fsdp", "blk"),
            P("fsdp", "blk"),
        ),
        check_vma=False,
    )
```

```python
import functools

import jax
import jax.numpy as jnp
import ml_dtypes
import numpy as np
from jax import lax
from jax.experimental import pallas as pl
from jax.experimental.pallas import tpu as pltpu
from jax.sharding import PartitionSpec as P

F32 = jnp.float32
BF16 = jnp.bfloat16
ROWS_ONE = 432
ROWS_TWO = 864
HALF = 216
PART = 112
STEP = HALF - PART
PIECE = PART // 2
TAPS = [(a, b, c) for a in range(3) for b in range(3) for c in range(3)]
VMEM = pl.BlockSpec(memory_space=pltpu.VMEM)
SMEM = pl.BlockSpec(memory_space=pltpu.SMEM)
FAR = pl.BlockSpec(memory_space=pltpu.HBM)
SENT = ROWS_ONE + 64
PARAMS = pltpu.CompilerParams(vmem_limit_bytes=60 * 1024 * 1024)


def split(value):
    high = value.astype(BF16)
    return high, (value - high.astype(F32)).astype(BF16)


def contract(left, right, dims=((1,), (0,))):
    def one(x, y):
        return lax.dot_general(x, y, (dims, ((), ())), preferred_element_type=F32)

    return one(left[0], right[0]) + (one(left[0], right[1]) + one(left[1], right[0]))


def selections():
    take = np.zeros((27, 2, 4, 4, 5, 8, 8), np.float32)
    fold = np.zeros((4, 8, 8, 27, 2, 4, 4), np.float32)
    for t, (a, b, c) in enumerate(TAPS):
        for i in range(2):
            for j in range(4):
                for k in range(4):
                    y, x = 2 * j - 1 + b, 2 * k - 1 + c
                    if y < 0 or x < 0:
                        continue
                    take[t, i, j, k, 2 * i + a, y, x] = 1
                    fold[2 * i + (0 if a == 1 else 1), y, x, t, i, j, k] = 1
    take = np.concatenate([take[:, :, :, :, 1:], take[:, :, :, :, :1]], 4)
    return take.reshape(864, 320).astype(ml_dtypes.bfloat16), fold.reshape(256, 864).astype(ml_dtypes.bfloat16)


def spans(width, shard):
    for t in range(27):
        done = 0
        while done < width:
            j, at = divmod(t * width + done, shard)
            size = min(width - done, shard - at)
            yield t, done, j, at, size
            done += size


def split_weights(core, odd, get, first, wh_ref, wl_ref):
    pieces = [get(first + n) for n in range(6)]

    def half_of(own, lower, upper):
        away = jnp.concatenate([lower, upper], 0)
        return jnp.concatenate([jnp.where(odd == 0, own, away), jnp.where(odd == 0, away, own)[2 * PART - HALF :]], 0)

    for s in range(8):
        mine = half_of(*[piece[s] for piece in pieces[:3]])
        other = half_of(*[piece[s] for piece in pieces[3:]])
        both = jnp.concatenate([jnp.where(core == 0, mine, other), jnp.where(core == 0, other, mine)], 0)
        high, low = split(both)
        wh_ref[ROWS_ONE * s : ROWS_ONE * (s + 1)] = high
        wl_ref[ROWS_ONE * s : ROWS_ONE * (s + 1)] = low


def patches_of(vol_ref, below_ref, layers, x_ref, ph_ref, pl_ref, first=0):
    skipped = 3 - below_ref.shape[0]
    rows = slice(first, first + 64 * len(layers))
    lane_row = lax.broadcasted_iota(jnp.int32, (16, 8, 128), 1)
    for z in range(2 * min(layers), 11):
        source, at = (below_ref, z - skipped) if z < 3 else (vol_ref, z - 3)
        even = source[at, :, pl.ds(0, 8, stride=2), :]
        odd = source[at, :, pl.ds(1, 8, stride=2), :]
        x_ref[0, z, 1:17] = jnp.where(lane_row == 0, 0.0, pltpu.roll(odd, 1, 1))
        x_ref[1, z, 1:17] = even
        x_ref[2, z, 1:17] = odd
        for c in range(3):
            x_ref[c, z, 0] = jnp.zeros((8, 128), F32)
    for t, (a, b, c) in enumerate(TAPS):
        tiles = [x_ref[c, 2 * n + a, 2 * j + b] for n in layers for j in range(8)]
        high, low = split(jnp.concatenate(tiles, 0))
        cols = slice(128 * t, 128 * (t + 1))
        ph_ref[rows, cols] = high
        pl_ref[rows, cols] = low


def cot_kernel(scalars, get, outs, scratch):
    weights = split(get(0)[...])
    cells = get(1)[...]
    plain = cells.reshape(256, 256)
    moved = jnp.concatenate([cells[:, 16:], get(2)[...]], 1).reshape(256, 256)
    nt = ((1,), (1,))
    here = contract(split(plain), weights, nt)
    next_up = contract(split(moved), weights, nt)
    row = scalars[0][0] * ROWS_TWO + lax.broadcasted_iota(jnp.int32, (256, ROWS_TWO), 1)
    outs[0][...] = jnp.where(row < 9 * 256, next_up, here).reshape(8, 32, ROWS_TWO)


def first_kernel(scalars, get, outs, scratch):
    pre_ref, send_ref = outs
    x_ref, ph_ref, pl_ref, wh_ref, wl_ref = scratch
    patches_of(get(0), get(1), (1, 2, 3, 4, 0), x_ref, ph_ref, pl_ref)
    split_weights(scalars[0][0], scalars[1][0], get, 2, wh_ref, wl_ref)
    full = contract((ph_ref[...], pl_ref[...]), (wh_ref[...], wl_ref[...]))
    pre_ref[...] = full[:256]
    hidden = full / (1.0 + jnp.exp(-full))
    high, low = split(hidden)
    take = get(8)[...]
    taken = jnp.dot(take, high, preferred_element_type=F32) + jnp.dot(take, low, preferred_element_type=F32)
    for t, begin, j, at, size in spans(256, ROWS_TWO):
        send_ref[j, :, at : at + size] = taken[32 * t : 32 * (t + 1), begin : begin + size]


def pre_kernel(scale, scalars, get, outs, scratch):
    gp_ref, keep_ref, send_ref = outs
    gh_ref, gl_ref = scratch
    got_ref = get(0)
    for t, begin, j, at, size in spans(256, ROWS_TWO):
        high, low = split(got_ref[j, :, at : at + size])
        gh_ref[32 * t : 32 * (t + 1), begin : begin + size] = high
        gl_ref[32 * t : 32 * (t + 1), begin : begin + size] = low
    fold = get(1)[...]
    hidden_grad = jnp.dot(fold, gh_ref[...], preferred_element_type=F32) + jnp.dot(fold, gl_ref[...], preferred_element_type=F32)
    pre = get(2)[...]
    sigma = 1.0 / (1.0 + jnp.exp(-pre))
    pre_grad = hidden_grad * sigma * (1.0 + pre * (1.0 - sigma))
    gp_ref[...] = pre_grad
    halves(pre_grad.T * scale, scalars[0][0], keep_ref, send_ref)


def grad_kernel(scalars, get, outs, scratch):
    x_ref, ph_ref, pl_ref = scratch
    (out_ref,) = outs
    layers = (1, 2, 3, 4)
    patches_of(get(0), get(1), layers, x_ref, ph_ref, pl_ref, 0)
    patches_of(get(2), get(3), layers, x_ref, ph_ref, pl_ref, 256)
    cells = split(jnp.concatenate([get(4)[...], get(5)[...]], 1))
    grads = contract(cells, (ph_ref[...], pl_ref[...]))
    for j in range(8):
        out_ref[j, :ROWS_ONE] = stack(grads[:, ROWS_ONE * j : ROWS_ONE * (j + 1)])
        out_ref[j, ROWS_ONE:] = jnp.zeros((SENT - ROWS_ONE, 128), F32)


def second_kernel(scalars, get, outs, scratch):
    part_ref, sem = scratch
    weights = split(get(0)[...])
    patches = split(get(1)[...].reshape(256, ROWS_TWO))
    part = contract(patches, weights).reshape(8, 32, 256)
    part_ref[:, :32] = part[:, :, :128]
    part_ref[:, 32:] = part[:, :, 128:]
    copy = pltpu.make_async_copy(part_ref, outs[0].at[:, ROWS_ONE:SENT], sem)
    copy.start()
    copy.wait()


def two_kernel(scale, scalars, get, outs, scratch):
    turned = split(get(0)[...].reshape(256, 256).T * scale)
    patches = split(get(1)[...].reshape(256, ROWS_TWO))
    halves(contract(turned, patches), scalars[0][0], *outs)


def sum_kernel(got_ref, sum_ref, out_ref):
    total = got_ref[0]
    for j in range(1, 8):
        total = total + got_ref[j]
    sum_ref[...] = unstack(total[:ROWS_ONE]).reshape(16, 8, ROWS_ONE)
    out_ref[...] = jnp.concatenate([total[ROWS_ONE : ROWS_ONE + 32], total[ROWS_ONE + 32 :]], 1)


def end_kernel(got_ref, one_ref):
    total = got_ref[0]
    for j in range(1, 16):
        total = total + got_ref[j]
    one_ref[...] = total


def stack(block):
    wide = jnp.concatenate([block[:, 384:], jnp.zeros((128, 512 - block.shape[1]), F32)], 1)
    return jnp.concatenate([block[:, 128 * n : 128 * (n + 1)] for n in range(3)] + [wide.T[: block.shape[1] - 384]], 0)


def unstack(block):
    wide = jnp.concatenate([block[384:], jnp.zeros((512 - block.shape[0], 128), F32)], 0)
    return jnp.concatenate([block[128 * n : 128 * (n + 1)] for n in range(3)] + [wide.T[:, : block.shape[0] - 384]], 1)


def halves(rows, core, keep_ref, send_ref):
    block = rows.reshape(16, 2, 8, rows.shape[1])
    even, odd = block[:, 0].reshape(128, rows.shape[1]), block[:, 1].reshape(128, rows.shape[1])
    keep_ref[...] = jnp.where(core == 0, even, odd)
    send_ref[...] = jnp.where(core == 0, odd, even)


def back_kernel(scalars, get, outs, scratch):
    (out_ref,), (wh_ref, wl_ref) = outs, scratch
    split_weights(scalars[0][0], scalars[1][0], get, 2, wh_ref, wl_ref)
    cells = split(jnp.concatenate([get(0)[...], get(1)[...]], 0))
    last = lax.broadcasted_iota(jnp.int32, (5, 8, 8, 128), 2) == 7
    zero = jnp.zeros((5, 1, 8, 128), F32)

    def tap(a, b, c):
        t = (a * 3 + b) * 3 + c
        rows = slice(128 * t, 128 * (t + 1))
        return contract(cells, (wh_ref[rows], wl_ref[rows]), ((1,), (1,))).reshape(5, 8, 8, 128)

    def along_x(a, b):
        low = tap(a, b, 0).reshape(40, 8, 128)
        moved = jnp.where(last, 0.0, pltpu.roll(low, 7, 1).reshape(5, 8, 8, 128))
        return tap(a, b, 1), tap(a, b, 2) + moved

    def along_y(a):
        low, mid, high = along_x(a, 0), along_x(a, 1), along_x(a, 2)
        return [[mid[p], high[p] + jnp.concatenate([low[p][:, 1:], zero], 1)] for p in range(2)]

    low, mid, high = along_y(0), along_y(1), along_y(2)
    for px in range(2):
        for py in range(2):
            even = mid[px][py]
            odd = high[px][py][:4] + low[px][py][1:]
            for i in range(4):
                for j in range(8):
                    out_ref[2 * i, 2 * j + py, pl.ds(px, 8, stride=2), :] = even[i, j]
                    out_ref[2 * i + 1, 2 * j + py, pl.ds(px, 8, stride=2), :] = odd[i, j]


def call(kernel, out_shapes, blocks, micros):
    return pl.pallas_call(
        kernel,
        out_shape=out_shapes,
        in_specs=[VMEM] * blocks,
        out_specs=[VMEM] * len(out_shapes),
        compiler_params=pltpu.CompilerParams(vmem_limit_bytes=12 * 1024 * 1024),
        cost_estimate=pl.CostEstimate(flops=int(micros * 1.1e9), bytes_accessed=1 << 20, transcendentals=0),
    )


def staged(body, out_shapes, scalars, operands, micros, scratch=(), onto=None):
    pairs = [operand if isinstance(operand, tuple) else (operand, None) for operand in operands]
    count, outs = len(pairs), len(out_shapes)
    kept = [] if onto is None else [onto]

    def kernel(*refs):
        scalar_refs, refs = refs[: len(scalars)], refs[len(scalars) :]
        sources, refs = refs[:count], refs[count + len(kept) :]
        out_refs, refs = refs[:outs], refs[outs:]
        buffers, scratch_refs, sems = refs[:count], refs[count:-1], refs[-1]
        copies = []
        for n, (_, window) in enumerate(pairs):
            source = sources[n] if window is None else sources[n].at[:, window[0] : window[1]]
            copies.append(pltpu.make_async_copy(source, buffers[n], sems.at[n]))
        for copy in copies:
            copy.start()

        def get(n):
            copies[n].wait()
            return buffers[n]

        body(scalar_refs, get, out_refs, scratch_refs)

    def buffer(array, window):
        shape = array.shape if window is None else (array.shape[0], window[1] - window[0]) + array.shape[2:]
        return pltpu.VMEM(shape, array.dtype)

    return pl.pallas_call(
        kernel,
        out_shape=out_shapes,
        in_specs=[SMEM] * len(scalars) + [FAR] * (count + len(kept)),
        out_specs=[FAR] * len(kept) + [VMEM] * (outs - len(kept)),
        input_output_aliases={len(scalars) + count: 0} if kept else {},
        scratch_shapes=[buffer(*pair) for pair in pairs] + list(scratch) + [pltpu.SemaphoreType.DMA((count,))],
        compiler_params=PARAMS,
        cost_estimate=pl.CostEstimate(flops=int(micros * 1.1e9), bytes_accessed=1 << 10, transcendentals=0),
    )(*scalars, *[array for array, _ in pairs], *kept)


def shaped(*dims, dtype=F32):
    return jax.ShapeDtypeStruct(dims, dtype)


def on_device(volumes, weight_one, weight_two, cotangent):
    blocks = lax.axis_size("blk")
    groups = lax.axis_size("fsdp")
    core_index = lax.rem(lax.axis_index("blk"), 2)
    core = core_index.reshape(1).astype(jnp.int32)
    odd_index = lax.rem(lax.axis_index("blk") // 2, 2)
    odd = odd_index.reshape(1).astype(jnp.int32)
    group = lax.axis_index("fsdp").reshape(1).astype(jnp.int32)
    take, fold = (jnp.asarray(array) for array in selections())
    field = volumes[0]
    scale_two = 1.0 / (32 * blocks * groups) ** 0.5
    scale_one = 1.0 / (256 * blocks * groups) ** 0.5
    up = [(n, n + 1) for n in range(blocks - 1)]
    down = [(n + 1, n) for n in range(blocks - 1)]
    swap = [(n, n ^ 1) for n in range(blocks)]
    same_core = [[2 * q + c for q in range(blocks // 2)] for c in range(2)]

    below = lax.ppermute(field[5:], "blk", up)
    other_field = lax.ppermute(field, "blk", swap)
    other_below = lax.ppermute(below[2:], "blk", swap)
    half = lax.dynamic_slice_in_dim(weight_one, core_index * HALF + odd_index * STEP, PART, 0)
    sent = jnp.concatenate([half, cotangent.reshape(32, 256)], 0)
    mine = lax.all_to_all(jnp.broadcast_to(sent, (groups, PART + 32, 256)), "fsdp", 0, 0, tiled=True)
    mine, below, other_field, other_below = lax.optimization_barrier((mine, below, other_field, other_below))
    cots_above = lax.ppermute(mine[:, PART : PART + 16], "blk", down)
    pieces = []
    for begin, shift in ((0, 2), (PIECE, 14)):
        around = [(n, n // 16 * 16 + (n + shift) % 16) for n in range(blocks)]
        pieces.append(lax.ppermute(mine[:, begin : begin + PIECE], "blk", around))
    (back,) = staged(cot_kernel, [shaped(8, 32, ROWS_TWO)], [group], [weight_two, (mine, (PART, PART + 32)), cots_above], 3)
    _, *pieces = lax.optimization_barrier((back, *pieces))
    first, *others = [lax.ppermute(piece, "blk", swap) for piece in (mine, *pieces)]
    halves_of = [(mine, (0, PART)), *pieces, (first, (0, PART)), *others]
    back = lax.all_to_all(back, "fsdp", 0, 0, tiled=True)

    def patch_scratch(rows):
        return [pltpu.VMEM((3, 11, 17, 8, 128), F32), pltpu.VMEM((rows, 3456), BF16), pltpu.VMEM((rows, 3456), BF16)]

    weights = [pltpu.VMEM((3456, 256), BF16)] * 2
    pre, taken = staged(
        first_kernel,
        [shaped(256, 256), shaped(8, 32, ROWS_TWO)],
        [core, odd],
        [field, below, *halves_of, take],
        0.01,
        patch_scratch(320) + weights,
    )
    taken, back, pre = lax.optimization_barrier((taken, back, pre))
    got = lax.all_to_all(taken, "fsdp", 0, 0, tiled=True)
    grad_pre, keep, send = staged(
        functools.partial(pre_kernel, scale_one),
        [shaped(256, 256), shaped(128, 256), shaped(128, 256)],
        [core],
        [back, fold, pre],
        0.01,
        [pltpu.VMEM((864, 256), BF16)] * 2,
    )
    swapped = lax.ppermute(send, "blk", swap)
    pre_above = lax.ppermute(grad_pre[:64], "blk", down)
    (one,) = staged(
        grad_kernel,
        [shaped(8, SENT, 128)],
        [],
        [field, below, other_field, other_below, keep, swapped],
        0.01,
        patch_scratch(512),
    )
    one, got, pre_above = lax.optimization_barrier((one, got, pre_above))
    part_scratch = [pltpu.VMEM((8, SENT - ROWS_ONE, 128), F32), pltpu.SemaphoreType.DMA(())]
    (one,) = staged(second_kernel, [shaped(8, SENT, 128)], [], [weight_two, got], 0.01, part_scratch, one)
    one = lax.all_to_all(one, "fsdp", 0, 0, tiled=True)
    (grad_input,) = staged(back_kernel, [shaped(8, 16, 16, 128)], [core, odd], [grad_pre, pre_above, *halves_of], 0.01, weights)
    half_two = [shaped(128, ROWS_TWO)] * 2
    keep, send = staged(functools.partial(two_kernel, scale_two), half_two, [core], [(mine, (PART, PART + 32)), got], 0.01)
    two = keep + lax.ppermute(send, "blk", swap)
    blk = lax.axis_index("blk")
    two = two.reshape(4, 4, 8, ROWS_TWO)
    for position, lowest in ((1, 2), (0, 8)):
        place = lax.rem(blk // lowest, 4)
        total = lax.dynamic_index_in_dim(two, place, position, keepdims=False)
        for other in range(1, 4):
            away = lax.dynamic_index_in_dim(two, place ^ other, position, keepdims=False)
            total = total + lax.ppermute(away, "blk", [(n, n ^ (other * lowest)) for n in range(blocks)])
        two = total
    one, grad_input, two = lax.optimization_barrier((one, grad_input, two))
    last, out = call(sum_kernel, [shaped(16, 8, ROWS_ONE), shaped(32, 256)], 1, 2)(one)
    last = lax.all_to_all(last, "blk", 0, 0, tiled=True, axis_index_groups=same_core)
    (one,) = call(end_kernel, [shaped(8, ROWS_ONE)], 1, 1)(last)
    return (out.reshape(1, 2, 4, 4, 256), grad_input[None], one.T, two.T)


def solution(mesh):
    placed = (
        P("fsdp", "blk", None, None, None),
        P("fsdp", None),
        P("fsdp", None),
        P("fsdp", "blk", None, None, None),
    )
    return jax.shard_map(
        on_device,
        mesh=mesh,
        in_specs=placed,
        out_specs=(
            P("fsdp", "blk", None, None, None),
            P("fsdp", "blk", None, None, None),
            P("fsdp", "blk"),
            P("fsdp", "blk"),
        ),
        check_vma=False,
    )
```

```python
import functools

import jax
import jax.numpy as jnp
import ml_dtypes
import numpy as np
from jax import lax
from jax.experimental import pallas as pl
from jax.experimental.pallas import tpu as pltpu
from jax.sharding import PartitionSpec as P

F32 = jnp.float32
BF16 = jnp.bfloat16
ROWS_ONE = 432
ROWS_TWO = 864
HALF = 216
PART = 112
STEP = HALF - PART
PIECE = PART // 2
TAPS = [(a, b, c) for a in range(3) for b in range(3) for c in range(3)]
VMEM = pl.BlockSpec(memory_space=pltpu.VMEM)
SMEM = pl.BlockSpec(memory_space=pltpu.SMEM)
FAR = pl.BlockSpec(memory_space=pltpu.HBM)
SENT = ROWS_ONE + 64
PARAMS = pltpu.CompilerParams(vmem_limit_bytes=60 * 1024 * 1024)


def split(value):
    high = value.astype(BF16)
    return high, (value - high.astype(F32)).astype(BF16)


def contract(left, right, dims=((1,), (0,))):
    def one(x, y):
        return lax.dot_general(x, y, (dims, ((), ())), preferred_element_type=F32)

    return one(left[0], right[0]) + (one(left[0], right[1]) + one(left[1], right[0]))


def selections():
    take = np.zeros((27, 2, 4, 4, 5, 8, 8), np.float32)
    fold = np.zeros((4, 8, 8, 27, 2, 4, 4), np.float32)
    for t, (a, b, c) in enumerate(TAPS):
        for i in range(2):
            for j in range(4):
                for k in range(4):
                    y, x = 2 * j - 1 + b, 2 * k - 1 + c
                    if y < 0 or x < 0:
                        continue
                    take[t, i, j, k, 2 * i + a, y, x] = 1
                    fold[2 * i + (0 if a == 1 else 1), y, x, t, i, j, k] = 1
    take = np.concatenate([take[:, :, :, :, 1:], take[:, :, :, :, :1]], 4)
    return take.reshape(864, 320).astype(ml_dtypes.bfloat16), fold.reshape(256, 864).astype(ml_dtypes.bfloat16)


def spans(width, shard):
    for t in range(27):
        done = 0
        while done < width:
            j, at = divmod(t * width + done, shard)
            size = min(width - done, shard - at)
            yield t, done, j, at, size
            done += size


def split_weights(core, odd, get, first, wh_ref, wl_ref):
    pieces = [get(first + n) for n in range(6)]

    def half_of(own, lower, upper):
        away = jnp.concatenate([lower, upper], 0)
        return jnp.concatenate([jnp.where(odd == 0, own, away), jnp.where(odd == 0, away, own)[2 * PART - HALF :]], 0)

    for s in range(8):
        mine = half_of(*[piece[s] for piece in pieces[:3]])
        other = half_of(*[piece[s] for piece in pieces[3:]])
        both = jnp.concatenate([jnp.where(core == 0, mine, other), jnp.where(core == 0, other, mine)], 0)
        high, low = split(both)
        wh_ref[ROWS_ONE * s : ROWS_ONE * (s + 1)] = high
        wl_ref[ROWS_ONE * s : ROWS_ONE * (s + 1)] = low


def patches_of(vol_ref, below_ref, layers, x_ref, ph_ref, pl_ref, first=0):
    skipped = 3 - below_ref.shape[0]
    rows = slice(first, first + 64 * len(layers))
    lane_row = lax.broadcasted_iota(jnp.int32, (16, 8, 128), 1)
    for z in range(2 * min(layers), 11):
        source, at = (below_ref, z - skipped) if z < 3 else (vol_ref, z - 3)
        even = source[at, :, pl.ds(0, 8, stride=2), :]
        odd = source[at, :, pl.ds(1, 8, stride=2), :]
        x_ref[0, z, 1:17] = jnp.where(lane_row == 0, 0.0, pltpu.roll(odd, 1, 1))
        x_ref[1, z, 1:17] = even
        x_ref[2, z, 1:17] = odd
        for c in range(3):
            x_ref[c, z, 0] = jnp.zeros((8, 128), F32)
    for t, (a, b, c) in enumerate(TAPS):
        tiles = [x_ref[c, 2 * n + a, 2 * j + b] for n in layers for j in range(8)]
        high, low = split(jnp.concatenate(tiles, 0))
        cols = slice(128 * t, 128 * (t + 1))
        ph_ref[rows, cols] = high
        pl_ref[rows, cols] = low


def cot_kernel(scalars, get, outs, scratch):
    weights = split(get(0)[...])
    cells = get(1)[...]
    plain = cells.reshape(256, 256)
    moved = jnp.concatenate([cells[:, 16:], get(2)[...]], 1).reshape(256, 256)
    nt = ((1,), (1,))
    here = contract(split(plain), weights, nt)
    next_up = contract(split(moved), weights, nt)
    row = scalars[0][0] * ROWS_TWO + lax.broadcasted_iota(jnp.int32, (256, ROWS_TWO), 1)
    outs[0][...] = jnp.where(row < 9 * 256, next_up, here).reshape(8, 32, ROWS_TWO)


def first_kernel(scalars, get, outs, scratch):
    pre_ref, send_ref = outs
    x_ref, ph_ref, pl_ref, wh_ref, wl_ref = scratch
    patches_of(get(0), get(1), (1, 2, 3, 4, 0), x_ref, ph_ref, pl_ref)
    split_weights(scalars[0][0], scalars[1][0], get, 2, wh_ref, wl_ref)
    full = contract((ph_ref[...], pl_ref[...]), (wh_ref[...], wl_ref[...]))
    pre_ref[...] = full[:256]
    hidden = full / (1.0 + jnp.exp(-full))
    high, low = split(hidden)
    take = get(8)[...]
    taken = jnp.dot(take, high, preferred_element_type=F32) + jnp.dot(take, low, preferred_element_type=F32)
    for t, begin, j, at, size in spans(256, ROWS_TWO):
        send_ref[j, :, at : at + size] = taken[32 * t : 32 * (t + 1), begin : begin + size]


def pre_kernel(scale, scalars, get, outs, scratch):
    gp_ref, keep_ref, send_ref = outs
    gh_ref, gl_ref = scratch
    got_ref = get(0)
    for t, begin, j, at, size in spans(256, ROWS_TWO):
        high, low = split(got_ref[j, :, at : at + size])
        gh_ref[32 * t : 32 * (t + 1), begin : begin + size] = high
        gl_ref[32 * t : 32 * (t + 1), begin : begin + size] = low
    fold = get(1)[...]
    hidden_grad = jnp.dot(fold, gh_ref[...], preferred_element_type=F32) + jnp.dot(fold, gl_ref[...], preferred_element_type=F32)
    pre = get(2)[...]
    sigma = 1.0 / (1.0 + jnp.exp(-pre))
    pre_grad = hidden_grad * sigma * (1.0 + pre * (1.0 - sigma))
    gp_ref[...] = pre_grad
    halves(pre_grad.T * scale, scalars[0][0], keep_ref, send_ref)


def grad_kernel(scalars, get, outs, scratch):
    x_ref, ph_ref, pl_ref = scratch
    (out_ref,) = outs
    layers = (1, 2, 3, 4)
    patches_of(get(0), get(1), layers, x_ref, ph_ref, pl_ref, 0)
    patches_of(get(2), get(3), layers, x_ref, ph_ref, pl_ref, 256)
    cells = split(jnp.concatenate([get(4)[...], get(5)[...]], 1))
    grads = contract(cells, (ph_ref[...], pl_ref[...]))
    for j in range(8):
        out_ref[j, :ROWS_ONE] = stack(grads[:, ROWS_ONE * j : ROWS_ONE * (j + 1)])
        out_ref[j, ROWS_ONE:] = jnp.zeros((SENT - ROWS_ONE, 128), F32)


def second_kernel(scalars, get, outs, scratch):
    part_ref, sem = scratch
    weights = split(get(0)[...])
    patches = split(get(1)[...].reshape(256, ROWS_TWO))
    part = contract(patches, weights).reshape(8, 32, 256)
    part_ref[:, :32] = part[:, :, :128]
    part_ref[:, 32:] = part[:, :, 128:]
    copy = pltpu.make_async_copy(part_ref, outs[0].at[:, ROWS_ONE:SENT], sem)
    copy.start()
    copy.wait()


def two_kernel(scale, scalars, get, outs, scratch):
    turned = split(get(0)[...].reshape(256, 256).T * scale)
    patches = split(get(1)[...].reshape(256, ROWS_TWO))
    halves(contract(turned, patches), scalars[0][0], *outs)


def sum_kernel(got_ref, sum_ref, out_ref):
    total = got_ref[0]
    for j in range(1, 8):
        total = total + got_ref[j]
    sum_ref[...] = unstack(total[:ROWS_ONE]).reshape(16, 8, ROWS_ONE)
    out_ref[...] = jnp.concatenate([total[ROWS_ONE : ROWS_ONE + 32], total[ROWS_ONE + 32 :]], 1)


def end_kernel(got_ref, one_ref):
    total = got_ref[0]
    for j in range(1, 16):
        total = total + got_ref[j]
    one_ref[...] = total


def stack(block):
    wide = jnp.concatenate([block[:, 384:], jnp.zeros((128, 512 - block.shape[1]), F32)], 1)
    return jnp.concatenate([block[:, 128 * n : 128 * (n + 1)] for n in range(3)] + [wide.T[: block.shape[1] - 384]], 0)


def unstack(block):
    wide = jnp.concatenate([block[384:], jnp.zeros((512 - block.shape[0], 128), F32)], 0)
    return jnp.concatenate([block[128 * n : 128 * (n + 1)] for n in range(3)] + [wide.T[:, : block.shape[0] - 384]], 1)


def halves(rows, core, keep_ref, send_ref):
    block = rows.reshape(16, 2, 8, rows.shape[1])
    even, odd = block[:, 0].reshape(128, rows.shape[1]), block[:, 1].reshape(128, rows.shape[1])
    keep_ref[...] = jnp.where(core == 0, even, odd)
    send_ref[...] = jnp.where(core == 0, odd, even)


def back_kernel(scalars, get, outs, scratch):
    (out_ref,), (wh_ref, wl_ref) = outs, scratch
    split_weights(scalars[0][0], scalars[1][0], get, 2, wh_ref, wl_ref)
    cells = split(jnp.concatenate([get(0)[...], get(1)[...]], 0))
    last = lax.broadcasted_iota(jnp.int32, (5, 8, 8, 128), 2) == 7
    zero = jnp.zeros((5, 1, 8, 128), F32)

    def tap(a, b, c):
        t = (a * 3 + b) * 3 + c
        rows = slice(128 * t, 128 * (t + 1))
        return contract(cells, (wh_ref[rows], wl_ref[rows]), ((1,), (1,))).reshape(5, 8, 8, 128)

    def along_x(a, b):
        low = tap(a, b, 0).reshape(40, 8, 128)
        moved = jnp.where(last, 0.0, pltpu.roll(low, 7, 1).reshape(5, 8, 8, 128))
        return tap(a, b, 1), tap(a, b, 2) + moved

    def along_y(a):
        low, mid, high = along_x(a, 0), along_x(a, 1), along_x(a, 2)
        return [[mid[p], high[p] + jnp.concatenate([low[p][:, 1:], zero], 1)] for p in range(2)]

    low, mid, high = along_y(0), along_y(1), along_y(2)
    for px in range(2):
        for py in range(2):
            even = mid[px][py]
            odd = high[px][py][:4] + low[px][py][1:]
            for i in range(4):
                for j in range(8):
                    out_ref[2 * i, 2 * j + py, pl.ds(px, 8, stride=2), :] = even[i, j]
                    out_ref[2 * i + 1, 2 * j + py, pl.ds(px, 8, stride=2), :] = odd[i, j]


def call(kernel, out_shapes, blocks, micros):
    return pl.pallas_call(
        kernel,
        out_shape=out_shapes,
        in_specs=[VMEM] * blocks,
        out_specs=[VMEM] * len(out_shapes),
        compiler_params=pltpu.CompilerParams(vmem_limit_bytes=12 * 1024 * 1024),
        cost_estimate=pl.CostEstimate(flops=int(micros * 1.1e9), bytes_accessed=1 << 20, transcendentals=0),
    )


def staged(body, out_shapes, scalars, operands, micros, scratch=(), onto=None):
    pairs = [operand if isinstance(operand, tuple) else (operand, None) for operand in operands]
    count, outs = len(pairs), len(out_shapes)
    kept = [] if onto is None else [onto]

    def kernel(*refs):
        scalar_refs, refs = refs[: len(scalars)], refs[len(scalars) :]
        sources, refs = refs[:count], refs[count + len(kept) :]
        out_refs, refs = refs[:outs], refs[outs:]
        buffers, scratch_refs, sems = refs[:count], refs[count:-1], refs[-1]
        copies = []
        for n, (_, window) in enumerate(pairs):
            source = sources[n] if window is None else sources[n].at[:, window[0] : window[1]]
            copies.append(pltpu.make_async_copy(source, buffers[n], sems.at[n]))
        for copy in copies:
            copy.start()

        def get(n):
            copies[n].wait()
            return buffers[n]

        body(scalar_refs, get, out_refs, scratch_refs)

    def buffer(array, window):
        shape = array.shape if window is None else (array.shape[0], window[1] - window[0]) + array.shape[2:]
        return pltpu.VMEM(shape, array.dtype)

    return pl.pallas_call(
        kernel,
        out_shape=out_shapes,
        in_specs=[SMEM] * len(scalars) + [FAR] * (count + len(kept)),
        out_specs=[FAR] * len(kept) + [VMEM] * (outs - len(kept)),
        input_output_aliases={len(scalars) + count: 0} if kept else {},
        scratch_shapes=[buffer(*pair) for pair in pairs] + list(scratch) + [pltpu.SemaphoreType.DMA((count,))],
        compiler_params=PARAMS,
        cost_estimate=pl.CostEstimate(flops=int(micros * 1.1e9), bytes_accessed=1 << 10, transcendentals=0),
    )(*scalars, *[array for array, _ in pairs], *kept)


def shaped(*dims, dtype=F32):
    return jax.ShapeDtypeStruct(dims, dtype)


def on_device(volumes, weight_one, weight_two, cotangent):
    blocks = lax.axis_size("blk")
    groups = lax.axis_size("fsdp")
    core_index = lax.rem(lax.axis_index("blk"), 2)
    core = core_index.reshape(1).astype(jnp.int32)
    odd_index = lax.rem(lax.axis_index("blk") // 2, 2)
    odd = odd_index.reshape(1).astype(jnp.int32)
    group = lax.axis_index("fsdp").reshape(1).astype(jnp.int32)
    take, fold = (jnp.asarray(array) for array in selections())
    field = volumes[0]
    scale_two = 1.0 / (32 * blocks * groups) ** 0.5
    scale_one = 1.0 / (256 * blocks * groups) ** 0.5
    up = [(n, n + 1) for n in range(blocks - 1)]
    down = [(n + 1, n) for n in range(blocks - 1)]
    swap = [(n, n ^ 1) for n in range(blocks)]
    same_core = [[2 * q + c for q in range(blocks // 2)] for c in range(2)]

    below = lax.ppermute(field[5:], "blk", up)
    other_field = lax.ppermute(field, "blk", swap)
    other_below = lax.ppermute(below[2:], "blk", swap)
    half = lax.dynamic_slice_in_dim(weight_one, core_index * HALF + odd_index * STEP, PART, 0)
    sent = jnp.concatenate([half, cotangent.reshape(32, 256)], 0)
    mine = lax.all_to_all(jnp.broadcast_to(sent, (groups, PART + 32, 256)), "fsdp", 0, 0, tiled=True)
    mine, below, other_field, other_below = lax.optimization_barrier((mine, below, other_field, other_below))
    cots_above = lax.ppermute(mine[:, PART : PART + 16], "blk", down)
    pieces = []
    for begin, shift in ((0, 2), (PIECE, 14)):
        around = [(n, n // 16 * 16 + (n + shift) % 16) for n in range(blocks)]
        pieces.append(lax.ppermute(mine[:, begin : begin + PIECE], "blk", around))
    (back,) = staged(cot_kernel, [shaped(8, 32, ROWS_TWO)], [group], [weight_two, (mine, (PART, PART + 32)), cots_above], 3)
    _, *pieces = lax.optimization_barrier((back, *pieces))
    first, *others = [lax.ppermute(piece, "blk", swap) for piece in (mine, *pieces)]
    halves_of = [(mine, (0, PART)), *pieces, (first, (0, PART)), *others]
    back = lax.all_to_all(back, "fsdp", 0, 0, tiled=True)

    def patch_scratch(rows):
        return [pltpu.VMEM((3, 11, 17, 8, 128), F32), pltpu.VMEM((rows, 3456), BF16), pltpu.VMEM((rows, 3456), BF16)]

    weights = [pltpu.VMEM((3456, 256), BF16)] * 2
    pre, taken = staged(
        first_kernel,
        [shaped(256, 256), shaped(8, 32, ROWS_TWO)],
        [core, odd],
        [field, below, *halves_of, take],
        0.01,
        patch_scratch(320) + weights,
    )
    taken, back, pre = lax.optimization_barrier((taken, back, pre))
    got = lax.all_to_all(taken, "fsdp", 0, 0, tiled=True)
    grad_pre, keep, send = staged(
        functools.partial(pre_kernel, scale_one),
        [shaped(256, 256), shaped(128, 256), shaped(128, 256)],
        [core],
        [back, fold, pre],
        0.01,
        [pltpu.VMEM((864, 256), BF16)] * 2,
    )
    swapped = lax.ppermute(send, "blk", swap)
    (one,) = staged(
        grad_kernel,
        [shaped(8, SENT, 128)],
        [],
        [field, below, other_field, other_below, keep, swapped],
        0.01,
        patch_scratch(512),
    )
    one, got, edge = lax.optimization_barrier((one, got, grad_pre[:64]))
    pre_above = lax.ppermute(edge, "blk", down)
    part_scratch = [pltpu.VMEM((8, SENT - ROWS_ONE, 128), F32), pltpu.SemaphoreType.DMA(())]
    (one,) = staged(second_kernel, [shaped(8, SENT, 128)], [], [weight_two, got], 0.01, part_scratch, one)
    one = lax.all_to_all(one, "fsdp", 0, 0, tiled=True)
    (grad_input,) = staged(back_kernel, [shaped(8, 16, 16, 128)], [core, odd], [grad_pre, pre_above, *halves_of], 0.01, weights)
    half_two = [shaped(128, ROWS_TWO)] * 2
    keep, send = staged(functools.partial(two_kernel, scale_two), half_two, [core], [(mine, (PART, PART + 32)), got], 0.01)
    two = keep + lax.ppermute(send, "blk", swap)
    blk = lax.axis_index("blk")
    two = two.reshape(4, 4, 8, ROWS_TWO)
    for position, lowest in ((1, 2), (0, 8)):
        place = lax.rem(blk // lowest, 4)
        total = lax.dynamic_index_in_dim(two, place, position, keepdims=False)
        for other in range(1, 4):
            away = lax.dynamic_index_in_dim(two, place ^ other, position, keepdims=False)
            total = total + lax.ppermute(away, "blk", [(n, n ^ (other * lowest)) for n in range(blocks)])
        two, grad_input = lax.optimization_barrier((total, grad_input))
    one, grad_input, two = lax.optimization_barrier((one, grad_input, two))
    last, out = call(sum_kernel, [shaped(16, 8, ROWS_ONE), shaped(32, 256)], 1, 2)(one)
    last = lax.all_to_all(last, "blk", 0, 0, tiled=True, axis_index_groups=same_core)
    (one,) = call(end_kernel, [shaped(8, ROWS_ONE)], 1, 1)(last)
    return (out.reshape(1, 2, 4, 4, 256), grad_input[None], one.T, two.T)


def solution(mesh):
    placed = (
        P("fsdp", "blk", None, None, None),
        P("fsdp", None),
        P("fsdp", None),
        P("fsdp", "blk", None, None, None),
    )
    return jax.shard_map(
        on_device,
        mesh=mesh,
        in_specs=placed,
        out_specs=(
            P("fsdp", "blk", None, None, None),
            P("fsdp", "blk", None, None, None),
            P("fsdp", "blk"),
            P("fsdp", "blk"),
        ),
        check_vma=False,
    )
```

```python
import functools

import jax
import jax.numpy as jnp
import ml_dtypes
import numpy as np
from jax import lax
from jax.experimental import pallas as pl
from jax.experimental.pallas import tpu as pltpu
from jax.sharding import PartitionSpec as P

F32 = jnp.float32
BF16 = jnp.bfloat16
ROWS_ONE = 432
ROWS_TWO = 864
HALF = 216
PART = 112
STEP = HALF - PART
PIECE = PART // 2
TAPS = [(a, b, c) for a in range(3) for b in range(3) for c in range(3)]
VMEM = pl.BlockSpec(memory_space=pltpu.VMEM)
SMEM = pl.BlockSpec(memory_space=pltpu.SMEM)
FAR = pl.BlockSpec(memory_space=pltpu.HBM)
SENT = ROWS_ONE + 64
PARAMS = pltpu.CompilerParams(vmem_limit_bytes=60 * 1024 * 1024)


def split(value):
    high = value.astype(BF16)
    return high, (value - high.astype(F32)).astype(BF16)


def contract(left, right, dims=((1,), (0,))):
    def one(x, y):
        return lax.dot_general(x, y, (dims, ((), ())), preferred_element_type=F32)

    return one(left[0], right[0]) + (one(left[0], right[1]) + one(left[1], right[0]))


def selections():
    take = np.zeros((27, 2, 4, 4, 5, 8, 8), np.float32)
    fold = np.zeros((4, 8, 8, 27, 2, 4, 4), np.float32)
    for t, (a, b, c) in enumerate(TAPS):
        for i in range(2):
            for j in range(4):
                for k in range(4):
                    y, x = 2 * j - 1 + b, 2 * k - 1 + c
                    if y < 0 or x < 0:
                        continue
                    take[t, i, j, k, 2 * i + a, y, x] = 1
                    fold[2 * i + (0 if a == 1 else 1), y, x, t, i, j, k] = 1
    take = np.concatenate([take[:, :, :, :, 1:], take[:, :, :, :, :1]], 4)
    return take.reshape(864, 320).astype(ml_dtypes.bfloat16), fold.reshape(256, 864).astype(ml_dtypes.bfloat16)


def spans(width, shard):
    for t in range(27):
        done = 0
        while done < width:
            j, at = divmod(t * width + done, shard)
            size = min(width - done, shard - at)
            yield t, done, j, at, size
            done += size


def split_weights(core, odd, get, first, wh_ref, wl_ref):
    pieces = [get(first + n) for n in range(6)]

    def half_of(own, lower, upper):
        away = jnp.concatenate([lower, upper], 0)
        return jnp.concatenate([jnp.where(odd == 0, own, away), jnp.where(odd == 0, away, own)[2 * PART - HALF :]], 0)

    for s in range(8):
        mine = half_of(*[piece[s] for piece in pieces[:3]])
        other = half_of(*[piece[s] for piece in pieces[3:]])
        both = jnp.concatenate([jnp.where(core == 0, mine, other), jnp.where(core == 0, other, mine)], 0)
        high, low = split(both)
        wh_ref[ROWS_ONE * s : ROWS_ONE * (s + 1)] = high
        wl_ref[ROWS_ONE * s : ROWS_ONE * (s + 1)] = low


def patches_of(vol_ref, below_ref, layers, x_ref, ph_ref, pl_ref, first=0):
    skipped = 3 - below_ref.shape[0]
    rows = slice(first, first + 64 * len(layers))
    lane_row = lax.broadcasted_iota(jnp.int32, (16, 8, 128), 1)
    for z in range(2 * min(layers), 11):
        source, at = (below_ref, z - skipped) if z < 3 else (vol_ref, z - 3)
        even = source[at, :, pl.ds(0, 8, stride=2), :]
        odd = source[at, :, pl.ds(1, 8, stride=2), :]
        x_ref[0, z, 1:17] = jnp.where(lane_row == 0, 0.0, pltpu.roll(odd, 1, 1))
        x_ref[1, z, 1:17] = even
        x_ref[2, z, 1:17] = odd
        for c in range(3):
            x_ref[c, z, 0] = jnp.zeros((8, 128), F32)
    for t, (a, b, c) in enumerate(TAPS):
        tiles = [x_ref[c, 2 * n + a, 2 * j + b] for n in layers for j in range(8)]
        high, low = split(jnp.concatenate(tiles, 0))
        cols = slice(128 * t, 128 * (t + 1))
        ph_ref[rows, cols] = high
        pl_ref[rows, cols] = low


def cot_kernel(scalars, get, outs, scratch):
    weights = split(get(0)[...])
    cells = get(1)[...]
    plain = cells.reshape(256, 256)
    moved = jnp.concatenate([cells[:, 16:], get(2)[...]], 1).reshape(256, 256)
    nt = ((1,), (1,))
    here = contract(split(plain), weights, nt)
    next_up = contract(split(moved), weights, nt)
    row = scalars[0][0] * ROWS_TWO + lax.broadcasted_iota(jnp.int32, (256, ROWS_TWO), 1)
    outs[0][...] = jnp.where(row < 9 * 256, next_up, here).reshape(8, 32, ROWS_TWO)


def first_kernel(scalars, get, outs, scratch):
    pre_ref, send_ref = outs
    x_ref, ph_ref, pl_ref, wh_ref, wl_ref = scratch
    patches_of(get(0), get(1), (1, 2, 3, 4, 0), x_ref, ph_ref, pl_ref)
    split_weights(scalars[0][0], scalars[1][0], get, 2, wh_ref, wl_ref)
    full = contract((ph_ref[...], pl_ref[...]), (wh_ref[...], wl_ref[...]))
    pre_ref[...] = full[:256]
    hidden = full / (1.0 + jnp.exp(-full))
    high, low = split(hidden)
    take = get(8)[...]
    taken = jnp.dot(take, high, preferred_element_type=F32) + jnp.dot(take, low, preferred_element_type=F32)
    for t, begin, j, at, size in spans(256, ROWS_TWO):
        send_ref[j, :, at : at + size] = taken[32 * t : 32 * (t + 1), begin : begin + size]


def pre_kernel(scale, scalars, get, outs, scratch):
    gp_ref, keep_ref, send_ref = outs
    gh_ref, gl_ref = scratch
    got_ref = get(0)
    for t, begin, j, at, size in spans(256, ROWS_TWO):
        high, low = split(got_ref[j, :, at : at + size])
        gh_ref[32 * t : 32 * (t + 1), begin : begin + size] = high
        gl_ref[32 * t : 32 * (t + 1), begin : begin + size] = low
    fold = get(1)[...]
    hidden_grad = jnp.dot(fold, gh_ref[...], preferred_element_type=F32) + jnp.dot(fold, gl_ref[...], preferred_element_type=F32)
    pre = get(2)[...]
    sigma = 1.0 / (1.0 + jnp.exp(-pre))
    pre_grad = hidden_grad * sigma * (1.0 + pre * (1.0 - sigma))
    gp_ref[...] = pre_grad
    halves(pre_grad.T * scale, scalars[0][0], keep_ref, send_ref)


def grad_kernel(scalars, get, outs, scratch):
    x_ref, ph_ref, pl_ref = scratch
    (out_ref,) = outs
    layers = (1, 2, 3, 4)
    patches_of(get(0), get(1), layers, x_ref, ph_ref, pl_ref, 0)
    patches_of(get(2), get(3), layers, x_ref, ph_ref, pl_ref, 256)
    cells = split(jnp.concatenate([get(4)[...], get(5)[...]], 1))
    grads = contract(cells, (ph_ref[...], pl_ref[...]))
    for j in range(8):
        out_ref[j, :ROWS_ONE] = stack(grads[:, ROWS_ONE * j : ROWS_ONE * (j + 1)])
        out_ref[j, ROWS_ONE:] = jnp.zeros((SENT - ROWS_ONE, 128), F32)


def second_kernel(scalars, get, outs, scratch):
    part_ref, sem = scratch
    weights = split(get(0)[...])
    patches = split(get(1)[...].reshape(256, ROWS_TWO))
    part = contract(patches, weights).reshape(8, 32, 256)
    part_ref[:, :32] = part[:, :, :128]
    part_ref[:, 32:] = part[:, :, 128:]
    copy = pltpu.make_async_copy(part_ref, outs[0].at[:, ROWS_ONE:SENT], sem)
    copy.start()
    copy.wait()


def two_kernel(scale, scalars, get, outs, scratch):
    turned = split(get(0)[...].reshape(256, 256).T * scale)
    patches = split(get(1)[...].reshape(256, ROWS_TWO))
    halves(contract(turned, patches), scalars[0][0], *outs)


def sum_kernel(got_ref, sum_ref, out_ref):
    total = got_ref[0]
    for j in range(1, 8):
        total = total + got_ref[j]
    sum_ref[...] = unstack(total[:ROWS_ONE]).reshape(16, 8, ROWS_ONE)
    out_ref[...] = jnp.concatenate([total[ROWS_ONE : ROWS_ONE + 32], total[ROWS_ONE + 32 :]], 1)


def end_kernel(got_ref, one_ref):
    total = got_ref[0]
    for j in range(1, 16):
        total = total + got_ref[j]
    one_ref[...] = total


def stack(block):
    wide = jnp.concatenate([block[:, 384:], jnp.zeros((128, 512 - block.shape[1]), F32)], 1)
    return jnp.concatenate([block[:, 128 * n : 128 * (n + 1)] for n in range(3)] + [wide.T[: block.shape[1] - 384]], 0)


def unstack(block):
    wide = jnp.concatenate([block[384:], jnp.zeros((512 - block.shape[0], 128), F32)], 0)
    return jnp.concatenate([block[128 * n : 128 * (n + 1)] for n in range(3)] + [wide.T[:, : block.shape[0] - 384]], 1)


def halves(rows, core, keep_ref, send_ref):
    block = rows.reshape(16, 2, 8, rows.shape[1])
    even, odd = block[:, 0].reshape(128, rows.shape[1]), block[:, 1].reshape(128, rows.shape[1])
    keep_ref[...] = jnp.where(core == 0, even, odd)
    send_ref[...] = jnp.where(core == 0, odd, even)


def back_kernel(scalars, get, outs, scratch):
    (out_ref,), (wh_ref, wl_ref) = outs, scratch
    split_weights(scalars[0][0], scalars[1][0], get, 2, wh_ref, wl_ref)
    cells = split(jnp.concatenate([get(0)[...], get(1)[...]], 0))
    last = lax.broadcasted_iota(jnp.int32, (5, 8, 8, 128), 2) == 7
    zero = jnp.zeros((5, 1, 8, 128), F32)

    def tap(a, b, c):
        t = (a * 3 + b) * 3 + c
        rows = slice(128 * t, 128 * (t + 1))
        return contract(cells, (wh_ref[rows], wl_ref[rows]), ((1,), (1,))).reshape(5, 8, 8, 128)

    def along_x(a, b):
        low = tap(a, b, 0).reshape(40, 8, 128)
        moved = jnp.where(last, 0.0, pltpu.roll(low, 7, 1).reshape(5, 8, 8, 128))
        return tap(a, b, 1), tap(a, b, 2) + moved

    def along_y(a):
        low, mid, high = along_x(a, 0), along_x(a, 1), along_x(a, 2)
        return [[mid[p], high[p] + jnp.concatenate([low[p][:, 1:], zero], 1)] for p in range(2)]

    low, mid, high = along_y(0), along_y(1), along_y(2)
    for px in range(2):
        for py in range(2):
            even = mid[px][py]
            odd = high[px][py][:4] + low[px][py][1:]
            for i in range(4):
                for j in range(8):
                    out_ref[2 * i, 2 * j + py, pl.ds(px, 8, stride=2), :] = even[i, j]
                    out_ref[2 * i + 1, 2 * j + py, pl.ds(px, 8, stride=2), :] = odd[i, j]


def call(kernel, out_shapes, blocks, micros):
    return pl.pallas_call(
        kernel,
        out_shape=out_shapes,
        in_specs=[VMEM] * blocks,
        out_specs=[VMEM] * len(out_shapes),
        compiler_params=pltpu.CompilerParams(vmem_limit_bytes=12 * 1024 * 1024),
        cost_estimate=pl.CostEstimate(flops=int(micros * 1.1e9), bytes_accessed=1 << 20, transcendentals=0),
    )


def staged(body, out_shapes, scalars, operands, micros, scratch=(), onto=None):
    pairs = [operand if isinstance(operand, tuple) else (operand, None) for operand in operands]
    count, outs = len(pairs), len(out_shapes)
    kept = [] if onto is None else [onto]

    def kernel(*refs):
        scalar_refs, refs = refs[: len(scalars)], refs[len(scalars) :]
        sources, refs = refs[:count], refs[count + len(kept) :]
        out_refs, refs = refs[:outs], refs[outs:]
        buffers, scratch_refs, sems = refs[:count], refs[count:-1], refs[-1]
        copies = []
        for n, (_, window) in enumerate(pairs):
            source = sources[n] if window is None else sources[n].at[:, window[0] : window[1]]
            copies.append(pltpu.make_async_copy(source, buffers[n], sems.at[n]))
        for copy in copies:
            copy.start()

        def get(n):
            copies[n].wait()
            return buffers[n]

        body(scalar_refs, get, out_refs, scratch_refs)

    def buffer(array, window):
        shape = array.shape if window is None else (array.shape[0], window[1] - window[0]) + array.shape[2:]
        return pltpu.VMEM(shape, array.dtype)

    return pl.pallas_call(
        kernel,
        out_shape=out_shapes,
        in_specs=[SMEM] * len(scalars) + [FAR] * (count + len(kept)),
        out_specs=[FAR] * len(kept) + [VMEM] * (outs - len(kept)),
        input_output_aliases={len(scalars) + count: 0} if kept else {},
        scratch_shapes=[buffer(*pair) for pair in pairs] + list(scratch) + [pltpu.SemaphoreType.DMA((count,))],
        compiler_params=PARAMS,
        cost_estimate=pl.CostEstimate(flops=int(micros * 1.1e9), bytes_accessed=1 << 10, transcendentals=0),
    )(*scalars, *[array for array, _ in pairs], *kept)


def shaped(*dims, dtype=F32):
    return jax.ShapeDtypeStruct(dims, dtype)


def on_device(volumes, weight_one, weight_two, cotangent):
    blocks = lax.axis_size("blk")
    groups = lax.axis_size("fsdp")
    core_index = lax.rem(lax.axis_index("blk"), 2)
    core = core_index.reshape(1).astype(jnp.int32)
    odd_index = lax.rem(lax.axis_index("blk") // 2, 2)
    odd = odd_index.reshape(1).astype(jnp.int32)
    group = lax.axis_index("fsdp").reshape(1).astype(jnp.int32)
    take, fold = (jnp.asarray(array) for array in selections())
    field = volumes[0]
    scale_two = 1.0 / (32 * blocks * groups) ** 0.5
    scale_one = 1.0 / (256 * blocks * groups) ** 0.5
    up = [(n, n + 1) for n in range(blocks - 1)]
    down = [(n + 1, n) for n in range(blocks - 1)]
    swap = [(n, n ^ 1) for n in range(blocks)]
    same_core = [[2 * q + c for q in range(blocks // 2)] for c in range(2)]

    below = lax.ppermute(field[5:], "blk", up)
    other_field = lax.ppermute(field, "blk", swap)
    other_below = lax.ppermute(below[2:], "blk", swap)
    half = lax.dynamic_slice_in_dim(weight_one, core_index * HALF + odd_index * STEP, PART, 0)
    sent = jnp.concatenate([half, cotangent.reshape(32, 256)], 0)
    mine = lax.all_to_all(jnp.broadcast_to(sent, (groups, PART + 32, 256)), "fsdp", 0, 0, tiled=True)
    mine, below, other_field, other_below = lax.optimization_barrier((mine, below, other_field, other_below))
    cots_above = lax.ppermute(mine[:, PART : PART + 16], "blk", down)
    pieces = []
    for begin, shift in ((0, 2), (PIECE, 14)):
        around = [(n, n // 16 * 16 + (n + shift) % 16) for n in range(blocks)]
        pieces.append(lax.ppermute(mine[:, begin : begin + PIECE], "blk", around))
    (back,) = staged(cot_kernel, [shaped(8, 32, ROWS_TWO)], [group], [weight_two, (mine, (PART, PART + 32)), cots_above], 3)
    _, *pieces = lax.optimization_barrier((back, *pieces))
    first, *others = [lax.ppermute(piece, "blk", swap) for piece in (mine, *pieces)]
    halves_of = [(mine, (0, PART)), *pieces, (first, (0, PART)), *others]
    back = lax.all_to_all(back, "fsdp", 0, 0, tiled=True)

    def patch_scratch(rows):
        return [pltpu.VMEM((3, 11, 17, 8, 128), F32), pltpu.VMEM((rows, 3456), BF16), pltpu.VMEM((rows, 3456), BF16)]

    weights = [pltpu.VMEM((3456, 256), BF16)] * 2
    pre, taken = staged(
        first_kernel,
        [shaped(256, 256), shaped(8, 32, ROWS_TWO)],
        [core, odd],
        [field, below, *halves_of, take],
        0.01,
        patch_scratch(320) + weights,
    )
    taken, back, pre = lax.optimization_barrier((taken, back, pre))
    got = lax.all_to_all(taken, "fsdp", 0, 0, tiled=True)
    grad_pre, keep, send = staged(
        functools.partial(pre_kernel, scale_one),
        [shaped(256, 256), shaped(128, 256), shaped(128, 256)],
        [core],
        [back, fold, pre],
        0.01,
        [pltpu.VMEM((864, 256), BF16)] * 2,
    )
    swapped = lax.ppermute(send, "blk", swap)
    (one,) = staged(
        grad_kernel,
        [shaped(8, SENT, 128)],
        [],
        [field, below, other_field, other_below, keep, swapped],
        0.01,
        patch_scratch(512),
    )
    one, got, edge = lax.optimization_barrier((one, got, grad_pre[:64]))
    pre_above = lax.ppermute(edge, "blk", down)
    part_scratch = [pltpu.VMEM((8, SENT - ROWS_ONE, 128), F32), pltpu.SemaphoreType.DMA(())]
    (one,) = staged(second_kernel, [shaped(8, SENT, 128)], [], [weight_two, got], 0.01, part_scratch, one)
    one = lax.all_to_all(one, "fsdp", 0, 0, tiled=True)
    half_two = [shaped(128, ROWS_TWO)] * 2
    keep, send = staged(functools.partial(two_kernel, scale_two), half_two, [core], [(mine, (PART, PART + 32)), got], 0.01)
    two = keep + lax.ppermute(send, "blk", swap)
    blk = lax.axis_index("blk")
    two = two.reshape(2, 2, 2, 2, 8, ROWS_TWO)
    for distance, position in ((2, 3), (4, 2), (16, 0), (8, 0)):
        bit = lax.rem(blk // distance, 2)
        away = lax.dynamic_index_in_dim(two, 1 - bit, position, keepdims=False)
        stay = lax.dynamic_index_in_dim(two, bit, position, keepdims=False)
        two = stay + lax.ppermute(away, "blk", [(n, n ^ distance) for n in range(blocks)])
        if distance == 2:
            two, pre_above = lax.optimization_barrier((two, pre_above))
    one, two = lax.optimization_barrier((one, two))
    last, out = call(sum_kernel, [shaped(16, 8, ROWS_ONE), shaped(32, 256)], 1, 2)(one)
    last, grad_pre = lax.optimization_barrier((last, grad_pre))
    (grad_input,) = staged(back_kernel, [shaped(8, 16, 16, 128)], [core, odd], [grad_pre, pre_above, *halves_of], 0.01, weights)
    last = lax.all_to_all(last, "blk", 0, 0, tiled=True, axis_index_groups=same_core)
    (one,) = call(end_kernel, [shaped(8, ROWS_ONE)], 1, 1)(last)
    return (out.reshape(1, 2, 4, 4, 256), grad_input[None], one.T, two.T)


def solution(mesh):
    placed = (
        P("fsdp", "blk", None, None, None),
        P("fsdp", None),
        P("fsdp", None),
        P("fsdp", "blk", None, None, None),
    )
    return jax.shard_map(
        on_device,
        mesh=mesh,
        in_specs=placed,
        out_specs=(
            P("fsdp", "blk", None, None, None),
            P("fsdp", "blk", None, None, None),
            P("fsdp", "blk"),
            P("fsdp", "blk"),
        ),
        check_vma=False,
    )
```

```python
import functools

import jax
import jax.numpy as jnp
import ml_dtypes
import numpy as np
from jax import lax
from jax.experimental import pallas as pl
from jax.experimental.pallas import tpu as pltpu
from jax.sharding import PartitionSpec as P

F32 = jnp.float32
BF16 = jnp.bfloat16
ROWS_ONE = 432
ROWS_TWO = 864
HALF = 216
PART = 112
STEP = HALF - PART
PIECE = PART // 2
TAPS = [(a, b, c) for a in range(3) for b in range(3) for c in range(3)]
VMEM = pl.BlockSpec(memory_space=pltpu.VMEM)
SMEM = pl.BlockSpec(memory_space=pltpu.SMEM)
FAR = pl.BlockSpec(memory_space=pltpu.HBM)
SENT = ROWS_ONE + 64


def split(value):
    high = value.astype(BF16)
    return high, (value - high.astype(F32)).astype(BF16)


def contract(left, right, dims=((1,), (0,))):
    def one(x, y):
        return lax.dot_general(x, y, (dims, ((), ())), preferred_element_type=F32)

    return one(left[0], right[0]) + (one(left[0], right[1]) + one(left[1], right[0]))


def selections():
    take = np.zeros((27, 2, 4, 4, 5, 8, 8), np.float32)
    fold = np.zeros((4, 8, 8, 27, 2, 4, 4), np.float32)
    for t, (a, b, c) in enumerate(TAPS):
        for i in range(2):
            for j in range(4):
                for k in range(4):
                    y, x = 2 * j - 1 + b, 2 * k - 1 + c
                    if y < 0 or x < 0:
                        continue
                    take[t, i, j, k, 2 * i + a, y, x] = 1
                    fold[2 * i + (0 if a == 1 else 1), y, x, t, i, j, k] = 1
    take = np.concatenate([take[:, :, :, :, 1:], take[:, :, :, :, :1]], 4)
    return take.reshape(864, 320).astype(ml_dtypes.bfloat16), fold.reshape(256, 864).astype(ml_dtypes.bfloat16)


def spans(width, shard):
    for t in range(27):
        done = 0
        while done < width:
            j, at = divmod(t * width + done, shard)
            size = min(width - done, shard - at)
            yield t, done, j, at, size
            done += size


def split_weights(core, odd, get, first, wh_ref, wl_ref):
    pieces = [get(first + n) for n in range(6)]

    def half_of(own, lower, upper):
        away = jnp.concatenate([lower, upper], 0)
        return jnp.concatenate([jnp.where(odd == 0, own, away), jnp.where(odd == 0, away, own)[2 * PART - HALF :]], 0)

    for s in range(8):
        mine = half_of(*[piece[s] for piece in pieces[:3]])
        other = half_of(*[piece[s] for piece in pieces[3:]])
        both = jnp.concatenate([jnp.where(core == 0, mine, other), jnp.where(core == 0, other, mine)], 0)
        high, low = split(both)
        wh_ref[ROWS_ONE * s : ROWS_ONE * (s + 1)] = high
        wl_ref[ROWS_ONE * s : ROWS_ONE * (s + 1)] = low


def patches_of(vol_ref, below_ref, layers, x_ref, ph_ref, pl_ref, first=0):
    skipped = 3 - below_ref.shape[0]
    rows = slice(first, first + 64 * len(layers))
    lane_row = lax.broadcasted_iota(jnp.int32, (16, 8, 128), 1)
    for z in range(2 * min(layers), 11):
        source, at = (below_ref, z - skipped) if z < 3 else (vol_ref, z - 3)
        even = source[at, :, pl.ds(0, 8, stride=2), :]
        odd = source[at, :, pl.ds(1, 8, stride=2), :]
        x_ref[0, z, 1:17] = jnp.where(lane_row == 0, 0.0, pltpu.roll(odd, 1, 1))
        x_ref[1, z, 1:17] = even
        x_ref[2, z, 1:17] = odd
        for c in range(3):
            x_ref[c, z, 0] = jnp.zeros((8, 128), F32)
    for t, (a, b, c) in enumerate(TAPS):
        tiles = [x_ref[c, 2 * n + a, 2 * j + b] for n in layers for j in range(8)]
        high, low = split(jnp.concatenate(tiles, 0))
        cols = slice(128 * t, 128 * (t + 1))
        ph_ref[rows, cols] = high
        pl_ref[rows, cols] = low


def cot_kernel(scalars, get, outs, scratch):
    weights = split(get(0)[...])
    cells = get(1)[...]
    plain = cells.reshape(256, 256)
    moved = jnp.concatenate([cells[:, 16:], get(2)[...]], 1).reshape(256, 256)
    nt = ((1,), (1,))
    here = contract(split(plain), weights, nt)
    next_up = contract(split(moved), weights, nt)
    row = scalars[0][0] * ROWS_TWO + lax.broadcasted_iota(jnp.int32, (256, ROWS_TWO), 1)
    outs[0][...] = jnp.where(row < 9 * 256, next_up, here).reshape(8, 32, ROWS_TWO)


def first_kernel(scalars, get, outs, scratch):
    pre_ref, send_ref = outs
    x_ref, ph_ref, pl_ref, wh_ref, wl_ref = scratch
    patches_of(get(0), get(1), (1, 2, 3, 4, 0), x_ref, ph_ref, pl_ref)
    split_weights(scalars[0][0], scalars[1][0], get, 2, wh_ref, wl_ref)
    full = contract((ph_ref[...], pl_ref[...]), (wh_ref[...], wl_ref[...]))
    pre_ref[...] = full[:256]
    hidden = full / (1.0 + jnp.exp(-full))
    high, low = split(hidden)
    take = get(8)[...]
    taken = jnp.dot(take, high, preferred_element_type=F32) + jnp.dot(take, low, preferred_element_type=F32)
    for t, begin, j, at, size in spans(256, ROWS_TWO):
        send_ref[j, :, at : at + size] = taken[32 * t : 32 * (t + 1), begin : begin + size]


def pre_kernel(scale, scalars, get, outs, scratch):
    gp_ref, keep_ref, send_ref = outs
    gh_ref, gl_ref = scratch
    got_ref = get(0)
    for t, begin, j, at, size in spans(256, ROWS_TWO):
        high, low = split(got_ref[j, :, at : at + size])
        gh_ref[32 * t : 32 * (t + 1), begin : begin + size] = high
        gl_ref[32 * t : 32 * (t + 1), begin : begin + size] = low
    fold = get(1)[...]
    hidden_grad = jnp.dot(fold, gh_ref[...], preferred_element_type=F32) + jnp.dot(fold, gl_ref[...], preferred_element_type=F32)
    pre = get(2)[...]
    sigma = 1.0 / (1.0 + jnp.exp(-pre))
    pre_grad = hidden_grad * sigma * (1.0 + pre * (1.0 - sigma))
    gp_ref[...] = pre_grad
    halves(pre_grad.T * scale, scalars[0][0], keep_ref, send_ref)


def grad_kernel(scalars, get, outs, scratch):
    x_ref, ph_ref, pl_ref = scratch
    (out_ref,) = outs
    layers = (1, 2, 3, 4)
    patches_of(get(0), get(1), layers, x_ref, ph_ref, pl_ref, 0)
    patches_of(get(2), get(3), layers, x_ref, ph_ref, pl_ref, 256)
    cells = split(jnp.concatenate([get(4)[...], get(5)[...]], 1))
    grads = contract(cells, (ph_ref[...], pl_ref[...]))
    for j in range(8):
        out_ref[j, :ROWS_ONE] = stack(grads[:, ROWS_ONE * j : ROWS_ONE * (j + 1)])
        out_ref[j, ROWS_ONE:] = jnp.zeros((SENT - ROWS_ONE, 128), F32)


def second_kernel(scalars, get, outs, scratch):
    part_ref, sem = scratch
    weights = split(get(0)[...])
    patches = split(get(1)[...].reshape(256, ROWS_TWO))
    part = contract(patches, weights).reshape(8, 32, 256)
    part_ref[:, :32] = part[:, :, :128]
    part_ref[:, 32:] = part[:, :, 128:]
    copy = pltpu.make_async_copy(part_ref, outs[0].at[:, ROWS_ONE:SENT], sem)
    copy.start()
    copy.wait()


def two_kernel(scale, scalars, get, outs, scratch):
    turned = split(get(0)[...].reshape(256, 256).T * scale)
    patches = split(get(1)[...].reshape(256, ROWS_TWO))
    halves(contract(turned, patches), scalars[0][0], *outs)


def sum_kernel(got_ref, sum_ref, out_ref):
    total = got_ref[0]
    for j in range(1, 8):
        total = total + got_ref[j]
    sum_ref[...] = unstack(total[:ROWS_ONE]).reshape(16, 8, ROWS_ONE)
    out_ref[...] = jnp.concatenate([total[ROWS_ONE : ROWS_ONE + 32], total[ROWS_ONE + 32 :]], 1)


def end_kernel(got_ref, one_ref):
    total = got_ref[0]
    for j in range(1, 16):
        total = total + got_ref[j]
    one_ref[...] = total


def stack(block):
    wide = jnp.concatenate([block[:, 384:], jnp.zeros((128, 512 - block.shape[1]), F32)], 1)
    return jnp.concatenate([block[:, 128 * n : 128 * (n + 1)] for n in range(3)] + [wide.T[: block.shape[1] - 384]], 0)


def unstack(block):
    wide = jnp.concatenate([block[384:], jnp.zeros((512 - block.shape[0], 128), F32)], 0)
    return jnp.concatenate([block[128 * n : 128 * (n + 1)] for n in range(3)] + [wide.T[:, : block.shape[0] - 384]], 1)


def halves(rows, core, keep_ref, send_ref):
    block = rows.reshape(16, 2, 8, rows.shape[1])
    even, odd = block[:, 0].reshape(128, rows.shape[1]), block[:, 1].reshape(128, rows.shape[1])
    keep_ref[...] = jnp.where(core == 0, even, odd)
    send_ref[...] = jnp.where(core == 0, odd, even)


def back_kernel(scalars, get, outs, scratch):
    (out_ref,), (wh_ref, wl_ref) = outs, scratch
    split_weights(scalars[0][0], scalars[1][0], get, 2, wh_ref, wl_ref)
    cells = split(jnp.concatenate([get(0)[...], get(1)[...]], 0))
    last = lax.broadcasted_iota(jnp.int32, (5, 8, 8, 128), 2) == 7
    zero = jnp.zeros((5, 1, 8, 128), F32)

    def tap(a, b, c):
        t = (a * 3 + b) * 3 + c
        rows = slice(128 * t, 128 * (t + 1))
        return contract(cells, (wh_ref[rows], wl_ref[rows]), ((1,), (1,))).reshape(5, 8, 8, 128)

    def along_x(a, b):
        low = tap(a, b, 0).reshape(40, 8, 128)
        moved = jnp.where(last, 0.0, pltpu.roll(low, 7, 1).reshape(5, 8, 8, 128))
        return tap(a, b, 1), tap(a, b, 2) + moved

    def along_y(a):
        low, mid, high = along_x(a, 0), along_x(a, 1), along_x(a, 2)
        return [[mid[p], high[p] + jnp.concatenate([low[p][:, 1:], zero], 1)] for p in range(2)]

    low, mid, high = along_y(0), along_y(1), along_y(2)
    for px in range(2):
        for py in range(2):
            even = mid[px][py]
            odd = high[px][py][:4] + low[px][py][1:]
            for i in range(4):
                for j in range(8):
                    out_ref[2 * i, 2 * j + py, pl.ds(px, 8, stride=2), :] = even[i, j]
                    out_ref[2 * i + 1, 2 * j + py, pl.ds(px, 8, stride=2), :] = odd[i, j]


def call(kernel, out_shapes, blocks, micros):
    return pl.pallas_call(
        kernel,
        out_shape=out_shapes,
        in_specs=[VMEM] * blocks,
        out_specs=[VMEM] * len(out_shapes),
        compiler_params=pltpu.CompilerParams(vmem_limit_bytes=12 * 1024 * 1024),
        cost_estimate=pl.CostEstimate(flops=int(micros * 1.1e9), bytes_accessed=1 << 20, transcendentals=0),
    )


def staged(body, out_shapes, scalars, operands, micros, scratch=(), onto=None, grant=60):
    pairs = [operand if isinstance(operand, tuple) else (operand, None) for operand in operands]
    count, outs = len(pairs), len(out_shapes)
    kept = [] if onto is None else [onto]

    def kernel(*refs):
        scalar_refs, refs = refs[: len(scalars)], refs[len(scalars) :]
        sources, refs = refs[:count], refs[count + len(kept) :]
        out_refs, refs = refs[:outs], refs[outs:]
        buffers, scratch_refs, sems = refs[:count], refs[count:-1], refs[-1]
        copies = []
        for n, (_, window) in enumerate(pairs):
            source = sources[n] if window is None else sources[n].at[:, window[0] : window[1]]
            copies.append(pltpu.make_async_copy(source, buffers[n], sems.at[n]))
        for copy in copies:
            copy.start()

        def get(n):
            copies[n].wait()
            return buffers[n]

        body(scalar_refs, get, out_refs, scratch_refs)

    def buffer(array, window):
        shape = array.shape if window is None else (array.shape[0], window[1] - window[0]) + array.shape[2:]
        return pltpu.VMEM(shape, array.dtype)

    return pl.pallas_call(
        kernel,
        out_shape=out_shapes,
        in_specs=[SMEM] * len(scalars) + [FAR] * (count + len(kept)),
        out_specs=[FAR] * len(kept) + [VMEM] * (outs - len(kept)),
        input_output_aliases={len(scalars) + count: 0} if kept else {},
        scratch_shapes=[buffer(*pair) for pair in pairs] + list(scratch) + [pltpu.SemaphoreType.DMA((count,))],
        compiler_params=pltpu.CompilerParams(vmem_limit_bytes=grant * 1024 * 1024),
        cost_estimate=pl.CostEstimate(flops=int(micros * 1.1e9), bytes_accessed=1 << 10, transcendentals=0),
    )(*scalars, *[array for array, _ in pairs], *kept)


def shaped(*dims, dtype=F32):
    return jax.ShapeDtypeStruct(dims, dtype)


def on_device(volumes, weight_one, weight_two, cotangent):
    blocks = lax.axis_size("blk")
    groups = lax.axis_size("fsdp")
    core_index = lax.rem(lax.axis_index("blk"), 2)
    core = core_index.reshape(1).astype(jnp.int32)
    odd_index = lax.rem(lax.axis_index("blk") // 2, 2)
    odd = odd_index.reshape(1).astype(jnp.int32)
    group = lax.axis_index("fsdp").reshape(1).astype(jnp.int32)
    take, fold = (jnp.asarray(array) for array in selections())
    field = volumes[0]
    scale_two = 1.0 / (32 * blocks * groups) ** 0.5
    scale_one = 1.0 / (256 * blocks * groups) ** 0.5
    up = [(n, n + 1) for n in range(blocks - 1)]
    down = [(n + 1, n) for n in range(blocks - 1)]
    swap = [(n, n ^ 1) for n in range(blocks)]
    same_core = [[2 * q + c for q in range(blocks // 2)] for c in range(2)]

    below = lax.ppermute(field[5:], "blk", up)
    other_field = lax.ppermute(field, "blk", swap)
    other_below = lax.ppermute(below[2:], "blk", swap)
    half = lax.dynamic_slice_in_dim(weight_one, core_index * HALF + odd_index * STEP, PART, 0)
    sent = jnp.concatenate([half, cotangent.reshape(32, 256)], 0)
    mine = lax.all_to_all(jnp.broadcast_to(sent, (groups, PART + 32, 256)), "fsdp", 0, 0, tiled=True)
    mine, below, other_below = lax.optimization_barrier((mine, below, other_below))
    cots_above = lax.ppermute(mine[:, PART : PART + 16], "blk", down)
    pieces = []
    for begin, shift in ((0, 2), (PIECE, 14)):
        around = [(n, n // 16 * 16 + (n + shift) % 16) for n in range(blocks)]
        pieces.append(lax.ppermute(mine[:, begin : begin + PIECE], "blk", around))
    (back,) = staged(cot_kernel, [shaped(8, 32, ROWS_TWO)], [group], [weight_two, (mine, (PART, PART + 32)), cots_above], 3)
    _, *pieces = lax.optimization_barrier((back, *pieces))
    first, *others = [lax.ppermute(piece, "blk", swap) for piece in (mine, *pieces)]
    halves_of = [(mine, (0, PART)), *pieces, (first, (0, PART)), *others]
    back = lax.all_to_all(back, "fsdp", 0, 0, tiled=True)

    def patch_scratch(rows):
        return [pltpu.VMEM((3, 11, 17, 8, 128), F32), pltpu.VMEM((rows, 3456), BF16), pltpu.VMEM((rows, 3456), BF16)]

    weights = [pltpu.VMEM((3456, 256), BF16)] * 2
    pre, taken = staged(
        first_kernel,
        [shaped(256, 256), shaped(8, 32, ROWS_TWO)],
        [core, odd],
        [field, below, *halves_of, take],
        0.01,
        patch_scratch(320) + weights,
        grant=60,
    )
    taken, back, pre = lax.optimization_barrier((taken, back, pre))
    got = lax.all_to_all(taken, "fsdp", 0, 0, tiled=True)
    grad_pre, keep, send = staged(
        functools.partial(pre_kernel, scale_one),
        [shaped(256, 256), shaped(128, 256), shaped(128, 256)],
        [core],
        [back, fold, pre],
        0.01,
        [pltpu.VMEM((864, 256), BF16)] * 2,
    )
    swapped = lax.ppermute(send, "blk", swap)
    (one,) = staged(
        grad_kernel,
        [shaped(8, SENT, 128)],
        [],
        [field, below, other_field, other_below, keep, swapped],
        0.01,
        patch_scratch(512),
    )
    one, got, edge = lax.optimization_barrier((one, got, grad_pre[:64]))
    pre_above = lax.ppermute(edge, "blk", down)
    part_scratch = [pltpu.VMEM((8, SENT - ROWS_ONE, 128), F32), pltpu.SemaphoreType.DMA(())]
    (one,) = staged(second_kernel, [shaped(8, SENT, 128)], [], [weight_two, got], 0.01, part_scratch, one)
    one = lax.all_to_all(one, "fsdp", 0, 0, tiled=True)
    half_two = [shaped(128, ROWS_TWO)] * 2
    keep, send = staged(functools.partial(two_kernel, scale_two), half_two, [core], [(mine, (PART, PART + 32)), got], 0.01)
    two = keep + lax.ppermute(send, "blk", swap)
    blk = lax.axis_index("blk")
    two = two.reshape(2, 2, 2, 2, 8, ROWS_TWO)
    for distance, position in ((2, 3), (4, 2), (16, 0), (8, 0)):
        bit = lax.rem(blk // distance, 2)
        away = lax.dynamic_index_in_dim(two, 1 - bit, position, keepdims=False)
        stay = lax.dynamic_index_in_dim(two, bit, position, keepdims=False)
        two = stay + lax.ppermute(away, "blk", [(n, n ^ distance) for n in range(blocks)])
        if distance == 2:
            two, pre_above = lax.optimization_barrier((two, pre_above))
        if distance == 4:
            two, pre_above = lax.optimization_barrier((two, pre_above))
            (grad_input,) = staged(back_kernel, [shaped(8, 16, 16, 128)], [core, odd], [grad_pre, pre_above, *halves_of], 0.01, weights)
        if distance == 16:
            one, two, grad_input = lax.optimization_barrier((one, two, grad_input))
            last, out = call(sum_kernel, [shaped(16, 8, ROWS_ONE), shaped(32, 256)], 1, 2)(one)
    last = lax.all_to_all(last, "blk", 0, 0, tiled=True, axis_index_groups=same_core)
    (one,) = call(end_kernel, [shaped(8, ROWS_ONE)], 1, 1)(last)
    return (out.reshape(1, 2, 4, 4, 256), grad_input[None], one.T, two.T)


def solution(mesh):
    placed = (
        P("fsdp", "blk", None, None, None),
        P("fsdp", None),
        P("fsdp", None),
        P("fsdp", "blk", None, None, None),
    )
    return jax.shard_map(
        on_device,
        mesh=mesh,
        in_specs=placed,
        out_specs=(
            P("fsdp", "blk", None, None, None),
            P("fsdp", "blk", None, None, None),
            P("fsdp", "blk"),
            P("fsdp", "blk"),
        ),
        check_vma=False,
    )
```

```python
import functools

import jax
import jax.numpy as jnp
import ml_dtypes
import numpy as np
from jax import lax
from jax.experimental import pallas as pl
from jax.experimental.pallas import tpu as pltpu
from jax.sharding import PartitionSpec as P

F32 = jnp.float32
BF16 = jnp.bfloat16
ROWS_ONE = 432
ROWS_TWO = 864
HALF = 216
PART = 112
STEP = HALF - PART
PIECE = PART // 2
TAPS = [(a, b, c) for a in range(3) for b in range(3) for c in range(3)]
VMEM = pl.BlockSpec(memory_space=pltpu.VMEM)
SMEM = pl.BlockSpec(memory_space=pltpu.SMEM)
FAR = pl.BlockSpec(memory_space=pltpu.HBM)
SENT = ROWS_ONE + 64


def split(value):
    high = value.astype(BF16)
    return high, (value - high.astype(F32)).astype(BF16)


def contract(left, right, dims=((1,), (0,))):
    def one(x, y):
        return lax.dot_general(x, y, (dims, ((), ())), preferred_element_type=F32)

    return one(left[0], right[0]) + (one(left[0], right[1]) + one(left[1], right[0]))


def selections():
    take = np.zeros((27, 2, 4, 4, 5, 8, 8), np.float32)
    fold = np.zeros((4, 8, 8, 27, 2, 4, 4), np.float32)
    for t, (a, b, c) in enumerate(TAPS):
        for i in range(2):
            for j in range(4):
                for k in range(4):
                    y, x = 2 * j - 1 + b, 2 * k - 1 + c
                    if y < 0 or x < 0:
                        continue
                    take[t, i, j, k, 2 * i + a, y, x] = 1
                    fold[2 * i + (0 if a == 1 else 1), y, x, t, i, j, k] = 1
    take = np.concatenate([take[:, :, :, :, 1:], take[:, :, :, :, :1]], 4)
    return take.reshape(864, 320).astype(ml_dtypes.bfloat16), fold.reshape(256, 864).astype(ml_dtypes.bfloat16)


def spans(width, shard):
    for t in range(27):
        done = 0
        while done < width:
            j, at = divmod(t * width + done, shard)
            size = min(width - done, shard - at)
            yield t, done, j, at, size
            done += size


def split_weights(core, odd, get, first, wh_ref, wl_ref):
    pieces = [get(first + n) for n in range(6)]

    def half_of(own, lower, upper):
        away = jnp.concatenate([lower, upper], 0)
        return jnp.concatenate([jnp.where(odd == 0, own, away), jnp.where(odd == 0, away, own)[2 * PART - HALF :]], 0)

    for s in range(8):
        mine = half_of(*[piece[s] for piece in pieces[:3]])
        other = half_of(*[piece[s] for piece in pieces[3:]])
        both = jnp.concatenate([jnp.where(core == 0, mine, other), jnp.where(core == 0, other, mine)], 0)
        high, low = split(both)
        wh_ref[ROWS_ONE * s : ROWS_ONE * (s + 1)] = high
        wl_ref[ROWS_ONE * s : ROWS_ONE * (s + 1)] = low


def patches_of(vol_ref, below_ref, layers, x_ref, ph_ref, pl_ref, first=0):
    skipped = 3 - below_ref.shape[0]
    rows = slice(first, first + 64 * len(layers))
    lane_row = lax.broadcasted_iota(jnp.int32, (16, 8, 128), 1)
    for z in range(2 * min(layers), 11):
        source, at = (below_ref, z - skipped) if z < 3 else (vol_ref, z - 3)
        even = source[at, :, pl.ds(0, 8, stride=2), :]
        odd = source[at, :, pl.ds(1, 8, stride=2), :]
        x_ref[0, z, 1:17] = jnp.where(lane_row == 0, 0.0, pltpu.roll(odd, 1, 1))
        x_ref[1, z, 1:17] = even
        x_ref[2, z, 1:17] = odd
        for c in range(3):
            x_ref[c, z, 0] = jnp.zeros((8, 128), F32)
    for t, (a, b, c) in enumerate(TAPS):
        tiles = [x_ref[c, 2 * n + a, 2 * j + b] for n in layers for j in range(8)]
        high, low = split(jnp.concatenate(tiles, 0))
        cols = slice(128 * t, 128 * (t + 1))
        ph_ref[rows, cols] = high
        pl_ref[rows, cols] = low


def cot_kernel(scalars, get, outs, scratch):
    weights = split(get(0)[...])
    cells = get(1)[...]
    plain = cells.reshape(256, 256)
    moved = jnp.concatenate([cells[:, 16:], get(2)[...]], 1).reshape(256, 256)
    nt = ((1,), (1,))
    here = contract(split(plain), weights, nt)
    next_up = contract(split(moved), weights, nt)
    row = scalars[0][0] * ROWS_TWO + lax.broadcasted_iota(jnp.int32, (256, ROWS_TWO), 1)
    outs[0][...] = jnp.where(row < 9 * 256, next_up, here).reshape(8, 32, ROWS_TWO)


def first_kernel(scalars, get, outs, scratch):
    pre_ref, send_ref = outs
    x_ref, ph_ref, pl_ref, wh_ref, wl_ref = scratch
    patches_of(get(0), get(1), (1, 2, 3, 4, 0), x_ref, ph_ref, pl_ref)
    split_weights(scalars[0][0], scalars[1][0], get, 2, wh_ref, wl_ref)
    full = contract((ph_ref[...], pl_ref[...]), (wh_ref[...], wl_ref[...]))
    pre_ref[...] = full[:256]
    hidden = full / (1.0 + jnp.exp(-full))
    high, low = split(hidden)
    take = get(8)[...]
    taken = jnp.dot(take, high, preferred_element_type=F32) + jnp.dot(take, low, preferred_element_type=F32)
    for t, begin, j, at, size in spans(256, ROWS_TWO):
        send_ref[j, :, at : at + size] = taken[32 * t : 32 * (t + 1), begin : begin + size]


def pre_kernel(scale, scalars, get, outs, scratch):
    gp_ref, edge_ref, keep_ref, send_ref = outs
    gh_ref, gl_ref = scratch
    got_ref = get(0)
    for t, begin, j, at, size in spans(256, ROWS_TWO):
        high, low = split(got_ref[j, :, at : at + size])
        gh_ref[32 * t : 32 * (t + 1), begin : begin + size] = high
        gl_ref[32 * t : 32 * (t + 1), begin : begin + size] = low
    fold = get(1)[...]
    hidden_grad = jnp.dot(fold, gh_ref[...], preferred_element_type=F32) + jnp.dot(fold, gl_ref[...], preferred_element_type=F32)
    pre = get(2)[...]
    sigma = 1.0 / (1.0 + jnp.exp(-pre))
    pre_grad = hidden_grad * sigma * (1.0 + pre * (1.0 - sigma))
    gp_ref[...] = pre_grad
    edge_ref[...] = pre_grad[:64]
    halves(pre_grad.T * scale, scalars[0][0], keep_ref, send_ref)


def grad_kernel(scalars, get, outs, scratch):
    x_ref, ph_ref, pl_ref = scratch
    (out_ref,) = outs
    layers = (1, 2, 3, 4)
    patches_of(get(0), get(1), layers, x_ref, ph_ref, pl_ref, 0)
    patches_of(get(2), get(3), layers, x_ref, ph_ref, pl_ref, 256)
    cells = split(jnp.concatenate([get(4)[...], get(5)[...]], 1))
    grads = contract(cells, (ph_ref[...], pl_ref[...]))
    for j in range(8):
        out_ref[j, :ROWS_ONE] = stack(grads[:, ROWS_ONE * j : ROWS_ONE * (j + 1)])
        out_ref[j, ROWS_ONE:] = jnp.zeros((SENT - ROWS_ONE, 128), F32)


def second_kernel(scalars, get, outs, scratch):
    part_ref, sem = scratch
    weights = split(get(0)[...])
    patches = split(get(1)[...].reshape(256, ROWS_TWO))
    part = contract(patches, weights).reshape(8, 32, 256)
    part_ref[:, :32] = part[:, :, :128]
    part_ref[:, 32:] = part[:, :, 128:]
    copy = pltpu.make_async_copy(part_ref, outs[0].at[:, ROWS_ONE:SENT], sem)
    copy.start()
    copy.wait()


def two_kernel(scale, scalars, get, outs, scratch):
    turned = split(get(0)[...].reshape(256, 256).T * scale)
    patches = split(get(1)[...].reshape(256, ROWS_TWO))
    halves(contract(turned, patches), scalars[0][0], *outs)


def sum_kernel(got_ref, sum_ref, out_ref):
    total = got_ref[0]
    for j in range(1, 8):
        total = total + got_ref[j]
    sum_ref[...] = unstack(total[:ROWS_ONE]).reshape(16, 8, ROWS_ONE)
    out_ref[...] = jnp.concatenate([total[ROWS_ONE : ROWS_ONE + 32], total[ROWS_ONE + 32 :]], 1)


def end_kernel(got_ref, one_ref):
    total = got_ref[0]
    for j in range(1, 16):
        total = total + got_ref[j]
    one_ref[...] = total


def stack(block):
    wide = jnp.concatenate([block[:, 384:], jnp.zeros((128, 512 - block.shape[1]), F32)], 1)
    return jnp.concatenate([block[:, 128 * n : 128 * (n + 1)] for n in range(3)] + [wide.T[: block.shape[1] - 384]], 0)


def unstack(block):
    wide = jnp.concatenate([block[384:], jnp.zeros((512 - block.shape[0], 128), F32)], 0)
    return jnp.concatenate([block[128 * n : 128 * (n + 1)] for n in range(3)] + [wide.T[:, : block.shape[0] - 384]], 1)


def halves(rows, core, keep_ref, send_ref):
    block = rows.reshape(16, 2, 8, rows.shape[1])
    even, odd = block[:, 0].reshape(128, rows.shape[1]), block[:, 1].reshape(128, rows.shape[1])
    keep_ref[...] = jnp.where(core == 0, even, odd)
    send_ref[...] = jnp.where(core == 0, odd, even)


def back_kernel(scalars, get, outs, scratch):
    (out_ref,), (wh_ref, wl_ref) = outs, scratch
    split_weights(scalars[0][0], scalars[1][0], get, 2, wh_ref, wl_ref)
    cells = split(jnp.concatenate([get(0)[...], get(1)[...]], 0))
    last = lax.broadcasted_iota(jnp.int32, (5, 8, 8, 128), 2) == 7
    zero = jnp.zeros((5, 1, 8, 128), F32)

    def tap(a, b, c):
        t = (a * 3 + b) * 3 + c
        rows = slice(128 * t, 128 * (t + 1))
        return contract(cells, (wh_ref[rows], wl_ref[rows]), ((1,), (1,))).reshape(5, 8, 8, 128)

    def along_x(a, b):
        low = tap(a, b, 0).reshape(40, 8, 128)
        moved = jnp.where(last, 0.0, pltpu.roll(low, 7, 1).reshape(5, 8, 8, 128))
        return tap(a, b, 1), tap(a, b, 2) + moved

    def along_y(a):
        low, mid, high = along_x(a, 0), along_x(a, 1), along_x(a, 2)
        return [[mid[p], high[p] + jnp.concatenate([low[p][:, 1:], zero], 1)] for p in range(2)]

    low, mid, high = along_y(0), along_y(1), along_y(2)
    for px in range(2):
        for py in range(2):
            even = mid[px][py]
            odd = high[px][py][:4] + low[px][py][1:]
            for i in range(4):
                for j in range(8):
                    out_ref[2 * i, 2 * j + py, pl.ds(px, 8, stride=2), :] = even[i, j]
                    out_ref[2 * i + 1, 2 * j + py, pl.ds(px, 8, stride=2), :] = odd[i, j]


def call(kernel, out_shapes, blocks, micros):
    return pl.pallas_call(
        kernel,
        out_shape=out_shapes,
        in_specs=[VMEM] * blocks,
        out_specs=[VMEM] * len(out_shapes),
        compiler_params=pltpu.CompilerParams(vmem_limit_bytes=12 * 1024 * 1024),
        cost_estimate=pl.CostEstimate(flops=int(micros * 1.1e9), bytes_accessed=1 << 20, transcendentals=0),
    )


def staged(body, out_shapes, scalars, operands, micros, scratch=(), onto=None, grant=60):
    pairs = [operand if isinstance(operand, tuple) else (operand, None) for operand in operands]
    count, outs = len(pairs), len(out_shapes)
    kept = [] if onto is None else [onto]

    def kernel(*refs):
        scalar_refs, refs = refs[: len(scalars)], refs[len(scalars) :]
        sources, refs = refs[:count], refs[count + len(kept) :]
        out_refs, refs = refs[:outs], refs[outs:]
        buffers, scratch_refs, sems = refs[:count], refs[count:-1], refs[-1]
        copies = []
        for n, (_, window) in enumerate(pairs):
            source = sources[n] if window is None else sources[n].at[:, window[0] : window[1]]
            copies.append(pltpu.make_async_copy(source, buffers[n], sems.at[n]))
        for copy in copies:
            copy.start()

        def get(n):
            copies[n].wait()
            return buffers[n]

        body(scalar_refs, get, out_refs, scratch_refs)

    def buffer(array, window):
        shape = array.shape if window is None else (array.shape[0], window[1] - window[0]) + array.shape[2:]
        return pltpu.VMEM(shape, array.dtype)

    return pl.pallas_call(
        kernel,
        out_shape=out_shapes,
        in_specs=[SMEM] * len(scalars) + [FAR] * (count + len(kept)),
        out_specs=[FAR] * len(kept) + [VMEM] * (outs - len(kept)),
        input_output_aliases={len(scalars) + count: 0} if kept else {},
        scratch_shapes=[buffer(*pair) for pair in pairs] + list(scratch) + [pltpu.SemaphoreType.DMA((count,))],
        compiler_params=pltpu.CompilerParams(vmem_limit_bytes=grant * 1024 * 1024),
        cost_estimate=pl.CostEstimate(flops=int(micros * 1.1e9), bytes_accessed=1 << 10, transcendentals=0),
    )(*scalars, *[array for array, _ in pairs], *kept)


def shaped(*dims, dtype=F32):
    return jax.ShapeDtypeStruct(dims, dtype)


def on_device(volumes, weight_one, weight_two, cotangent):
    blocks = lax.axis_size("blk")
    groups = lax.axis_size("fsdp")
    core_index = lax.rem(lax.axis_index("blk"), 2)
    core = core_index.reshape(1).astype(jnp.int32)
    odd_index = lax.rem(lax.axis_index("blk") // 2, 2)
    odd = odd_index.reshape(1).astype(jnp.int32)
    group = lax.axis_index("fsdp").reshape(1).astype(jnp.int32)
    take, fold = (jnp.asarray(array) for array in selections())
    field = volumes[0]
    scale_two = 1.0 / (32 * blocks * groups) ** 0.5
    scale_one = 1.0 / (256 * blocks * groups) ** 0.5
    up = [(n, n + 1) for n in range(blocks - 1)]
    down = [(n + 1, n) for n in range(blocks - 1)]
    swap = [(n, n ^ 1) for n in range(blocks)]
    same_core = [[2 * q + c for q in range(blocks // 2)] for c in range(2)]

    below = lax.ppermute(field[5:], "blk", up)
    other_field = lax.ppermute(field, "blk", swap)
    other_below = lax.ppermute(below[2:], "blk", swap)
    half = lax.dynamic_slice_in_dim(weight_one, core_index * HALF + odd_index * STEP, PART, 0)
    sent = jnp.concatenate([half, cotangent.reshape(32, 256)], 0)
    mine = lax.all_to_all(jnp.broadcast_to(sent, (groups, PART + 32, 256)), "fsdp", 0, 0, tiled=True)
    mine, below, other_below = lax.optimization_barrier((mine, below, other_below))
    cots_above = lax.ppermute(mine[:, PART : PART + 16], "blk", down)
    pieces = []
    for begin, shift in ((0, 2), (PIECE, 14)):
        around = [(n, n // 16 * 16 + (n + shift) % 16) for n in range(blocks)]
        pieces.append(lax.ppermute(mine[:, begin : begin + PIECE], "blk", around))
    (back,) = staged(cot_kernel, [shaped(8, 32, ROWS_TWO)], [group], [weight_two, (mine, (PART, PART + 32)), cots_above], 3)
    _, *pieces = lax.optimization_barrier((back, *pieces))
    first, *others = [lax.ppermute(piece, "blk", swap) for piece in (mine, *pieces)]
    halves_of = [(mine, (0, PART)), *pieces, (first, (0, PART)), *others]
    back = lax.all_to_all(back, "fsdp", 0, 0, tiled=True)

    def patch_scratch(rows):
        return [pltpu.VMEM((3, 11, 17, 8, 128), F32), pltpu.VMEM((rows, 3456), BF16), pltpu.VMEM((rows, 3456), BF16)]

    weights = [pltpu.VMEM((3456, 256), BF16)] * 2
    pre, taken = staged(
        first_kernel,
        [shaped(256, 256), shaped(8, 32, ROWS_TWO)],
        [core, odd],
        [field, below, *halves_of, take],
        0.01,
        patch_scratch(320) + weights,
        grant=60,
    )
    taken, back, pre = lax.optimization_barrier((taken, back, pre))
    got = lax.all_to_all(taken, "fsdp", 0, 0, tiled=True)
    grad_pre, edge, keep, send = staged(
        functools.partial(pre_kernel, scale_one),
        [shaped(256, 256), shaped(64, 256), shaped(128, 256), shaped(128, 256)],
        [core],
        [back, fold, pre],
        0.01,
        [pltpu.VMEM((864, 256), BF16)] * 2,
        grant=63,
    )
    swapped = lax.ppermute(send, "blk", swap)
    (one,) = staged(
        grad_kernel,
        [shaped(8, SENT, 128)],
        [],
        [field, below, other_field, other_below, keep, swapped],
        0.01,
        patch_scratch(512),
        grant=63,
    )
    one, got, edge = lax.optimization_barrier((one, got, edge))
    pre_above = lax.ppermute(edge, "blk", down)
    part_scratch = [pltpu.VMEM((8, SENT - ROWS_ONE, 128), F32), pltpu.SemaphoreType.DMA(())]
    (one,) = staged(second_kernel, [shaped(8, SENT, 128)], [], [weight_two, got], 0.01, part_scratch, one)
    _, got = lax.optimization_barrier((one, got))
    one = lax.all_to_all(one, "fsdp", 0, 0, tiled=True)
    half_two = [shaped(128, ROWS_TWO)] * 2
    keep, send = staged(functools.partial(two_kernel, scale_two), half_two, [core], [(mine, (PART, PART + 32)), got], 0.01)
    terms = [keep, lax.ppermute(send, "blk", swap)]
    blk = lax.axis_index("blk")
    terms = [term.reshape(2, 2, 2, 2, 8, ROWS_TWO) for term in terms]
    for distance, position in ((2, 3), (4, 2), (16, 0), (8, 0)):
        bit = lax.rem(blk // distance, 2)
        away = sum(lax.dynamic_index_in_dim(term, 1 - bit, position, keepdims=False) for term in terms)
        terms = [lax.dynamic_index_in_dim(term, bit, position, keepdims=False) for term in terms]
        if distance == 4:
            away, pre_above = lax.optimization_barrier((away, pre_above))
        if distance == 16:
            away, pre_above = lax.optimization_barrier((away, pre_above))
            (grad_input,) = staged(back_kernel, [shaped(8, 16, 16, 128)], [core, odd], [grad_pre, pre_above, *halves_of], 0.01, weights)
        terms.append(lax.ppermute(away, "blk", [(n, n ^ distance) for n in range(blocks)]))
        if distance == 16:
            one, terms[-1], grad_input = lax.optimization_barrier((one, terms[-1], grad_input))
            last, out = call(sum_kernel, [shaped(16, 8, ROWS_ONE), shaped(32, 256)], 1, 2)(one)
    two = sum(terms)
    last = lax.all_to_all(last, "blk", 0, 0, tiled=True, axis_index_groups=same_core)
    (one,) = call(end_kernel, [shaped(8, ROWS_ONE)], 1, 1)(last)
    return (out.reshape(1, 2, 4, 4, 256), grad_input[None], one.T, two.T)


def solution(mesh):
    placed = (
        P("fsdp", "blk", None, None, None),
        P("fsdp", None),
        P("fsdp", None),
        P("fsdp", "blk", None, None, None),
    )
    return jax.shard_map(
        on_device,
        mesh=mesh,
        in_specs=placed,
        out_specs=(
            P("fsdp", "blk", None, None, None),
            P("fsdp", "blk", None, None, None),
            P("fsdp", "blk"),
            P("fsdp", "blk"),
        ),
        check_vma=False,
    )
```

```python
import functools

import jax
import jax.numpy as jnp
import ml_dtypes
import numpy as np
from jax import lax
from jax.experimental import pallas as pl
from jax.experimental.pallas import tpu as pltpu
from jax.sharding import PartitionSpec as P

F32 = jnp.float32
BF16 = jnp.bfloat16
ROWS_ONE = 432
ROWS_TWO = 864
HALF = 216
PART = 112
STEP = HALF - PART
PIECE = PART // 2
TAPS = [(a, b, c) for a in range(3) for b in range(3) for c in range(3)]
VMEM = pl.BlockSpec(memory_space=pltpu.VMEM)
SMEM = pl.BlockSpec(memory_space=pltpu.SMEM)
FAR = pl.BlockSpec(memory_space=pltpu.HBM)
SENT = ROWS_ONE + 64


def split(value):
    high = value.astype(BF16)
    return high, (value - high.astype(F32)).astype(BF16)


def contract(left, right, dims=((1,), (0,))):
    def one(x, y):
        return lax.dot_general(x, y, (dims, ((), ())), preferred_element_type=F32)

    return one(left[0], right[0]) + (one(left[0], right[1]) + one(left[1], right[0]))


def selections():
    take = np.zeros((27, 2, 4, 4, 5, 8, 8), np.float32)
    fold = np.zeros((4, 8, 8, 27, 2, 4, 4), np.float32)
    for t, (a, b, c) in enumerate(TAPS):
        for i in range(2):
            for j in range(4):
                for k in range(4):
                    y, x = 2 * j - 1 + b, 2 * k - 1 + c
                    if y < 0 or x < 0:
                        continue
                    take[t, i, j, k, 2 * i + a, y, x] = 1
                    fold[2 * i + (0 if a == 1 else 1), y, x, t, i, j, k] = 1
    take = np.concatenate([take[:, :, :, :, 1:], take[:, :, :, :, :1]], 4)
    return take.reshape(864, 320).astype(ml_dtypes.bfloat16), fold.reshape(256, 864).astype(ml_dtypes.bfloat16)


def spans(width, shard):
    for t in range(27):
        done = 0
        while done < width:
            j, at = divmod(t * width + done, shard)
            size = min(width - done, shard - at)
            yield t, done, j, at, size
            done += size


def split_weights(core, odd, get, first, wh_ref, wl_ref):
    pieces = [get(first + n) for n in range(6)]

    def half_of(own, lower, upper):
        away = jnp.concatenate([lower, upper], 0)
        return jnp.concatenate([jnp.where(odd == 0, own, away), jnp.where(odd == 0, away, own)[2 * PART - HALF :]], 0)

    for s in range(8):
        mine = half_of(*[piece[s] for piece in pieces[:3]])
        other = half_of(*[piece[s] for piece in pieces[3:]])
        both = jnp.concatenate([jnp.where(core == 0, mine, other), jnp.where(core == 0, other, mine)], 0)
        high, low = split(both)
        wh_ref[ROWS_ONE * s : ROWS_ONE * (s + 1)] = high
        wl_ref[ROWS_ONE * s : ROWS_ONE * (s + 1)] = low


def patches_of(vol_ref, below_ref, layers, x_ref, ph_ref, pl_ref, first=0):
    skipped = 3 - below_ref.shape[0]
    rows = slice(first, first + 64 * len(layers))
    lane_row = lax.broadcasted_iota(jnp.int32, (16, 8, 128), 1)
    for z in range(2 * min(layers), 11):
        source, at = (below_ref, z - skipped) if z < 3 else (vol_ref, z - 3)
        even = source[at, :, pl.ds(0, 8, stride=2), :]
        odd = source[at, :, pl.ds(1, 8, stride=2), :]
        x_ref[0, z, 1:17] = jnp.where(lane_row == 0, 0.0, pltpu.roll(odd, 1, 1))
        x_ref[1, z, 1:17] = even
        x_ref[2, z, 1:17] = odd
        for c in range(3):
            x_ref[c, z, 0] = jnp.zeros((8, 128), F32)
    for t, (a, b, c) in enumerate(TAPS):
        tiles = [x_ref[c, 2 * n + a, 2 * j + b] for n in layers for j in range(8)]
        high, low = split(jnp.concatenate(tiles, 0))
        cols = slice(128 * t, 128 * (t + 1))
        ph_ref[rows, cols] = high
        pl_ref[rows, cols] = low


def cot_kernel(scalars, get, outs, scratch):
    weights = split(get(0)[...])
    cells = get(1)[...]
    plain = cells.reshape(256, 256)
    moved = jnp.concatenate([cells[:, 16:], get(2)[...]], 1).reshape(256, 256)
    nt = ((1,), (1,))
    here = contract(split(plain), weights, nt)
    next_up = contract(split(moved), weights, nt)
    row = scalars[0][0] * ROWS_TWO + lax.broadcasted_iota(jnp.int32, (256, ROWS_TWO), 1)
    outs[0][...] = jnp.where(row < 9 * 256, next_up, here).reshape(8, 32, ROWS_TWO)


def first_kernel(scalars, get, outs, scratch):
    pre_ref, send_ref = outs
    x_ref, ph_ref, pl_ref, wh_ref, wl_ref = scratch
    patches_of(get(0), get(1), (1, 2, 3, 4, 0), x_ref, ph_ref, pl_ref)
    split_weights(scalars[0][0], scalars[1][0], get, 2, wh_ref, wl_ref)
    full = contract((ph_ref[...], pl_ref[...]), (wh_ref[...], wl_ref[...]))
    pre_ref[...] = full[:256]
    hidden = full / (1.0 + jnp.exp(-full))
    high, low = split(hidden)
    take = get(8)[...]
    taken = jnp.dot(take, high, preferred_element_type=F32) + jnp.dot(take, low, preferred_element_type=F32)
    for t, begin, j, at, size in spans(256, ROWS_TWO):
        send_ref[j, :, at : at + size] = taken[32 * t : 32 * (t + 1), begin : begin + size]


def pre_kernel(scale, scalars, get, outs, scratch):
    gp_ref, edge_ref, keep_ref, send_ref = outs
    gh_ref, gl_ref = scratch
    got_ref = get(0)
    for t, begin, j, at, size in spans(256, ROWS_TWO):
        high, low = split(got_ref[j, :, at : at + size])
        gh_ref[32 * t : 32 * (t + 1), begin : begin + size] = high
        gl_ref[32 * t : 32 * (t + 1), begin : begin + size] = low
    fold = get(1)[...]
    hidden_grad = jnp.dot(fold, gh_ref[...], preferred_element_type=F32) + jnp.dot(fold, gl_ref[...], preferred_element_type=F32)
    pre = get(2)[...]
    sigma = 1.0 / (1.0 + jnp.exp(-pre))
    pre_grad = hidden_grad * sigma * (1.0 + pre * (1.0 - sigma))
    gp_ref[...] = pre_grad
    edge_ref[...] = pre_grad[:64]
    halves(pre_grad.T * scale, scalars[0][0], keep_ref, send_ref)


def grad_kernel(scalars, get, outs, scratch):
    x_ref, ph_ref, pl_ref = scratch
    (out_ref,) = outs
    layers = (1, 2, 3, 4)
    patches_of(get(0), get(1), layers, x_ref, ph_ref, pl_ref, 0)
    patches_of(get(2), get(3), layers, x_ref, ph_ref, pl_ref, 256)
    cells = split(jnp.concatenate([get(4)[...], get(5)[...]], 1))
    grads = contract(cells, (ph_ref[...], pl_ref[...]))
    for j in range(8):
        out_ref[j, :ROWS_ONE] = stack(grads[:, ROWS_ONE * j : ROWS_ONE * (j + 1)])
        out_ref[j, ROWS_ONE:] = jnp.zeros((SENT - ROWS_ONE, 128), F32)


def second_kernel(scalars, get, outs, scratch):
    part_ref, sem = scratch
    weights = split(get(0)[...])
    patches = split(get(1)[...].reshape(256, ROWS_TWO))
    part = contract(patches, weights).reshape(8, 32, 256)
    part_ref[:, :32] = part[:, :, :128]
    part_ref[:, 32:] = part[:, :, 128:]
    copy = pltpu.make_async_copy(part_ref, outs[0].at[:, ROWS_ONE:SENT], sem)
    copy.start()
    copy.wait()


def two_kernel(scale, scalars, get, outs, scratch):
    turned = split(get(0)[...].reshape(256, 256).T * scale)
    patches = split(get(1)[...].reshape(256, ROWS_TWO))
    halves(contract(turned, patches), scalars[0][0], *outs)


def sum_kernel(got_ref, sum_ref, out_ref):
    total = got_ref[0]
    for j in range(1, 8):
        total = total + got_ref[j]
    sum_ref[...] = unstack(total[:ROWS_ONE]).reshape(16, 8, ROWS_ONE)
    out_ref[...] = jnp.concatenate([total[ROWS_ONE : ROWS_ONE + 32], total[ROWS_ONE + 32 :]], 1)


def end_kernel(got_ref, one_ref):
    total = got_ref[0]
    for j in range(1, 16):
        total = total + got_ref[j]
    one_ref[...] = total


def stack(block):
    wide = jnp.concatenate([block[:, 384:], jnp.zeros((128, 512 - block.shape[1]), F32)], 1)
    return jnp.concatenate([block[:, 128 * n : 128 * (n + 1)] for n in range(3)] + [wide.T[: block.shape[1] - 384]], 0)


def unstack(block):
    wide = jnp.concatenate([block[384:], jnp.zeros((512 - block.shape[0], 128), F32)], 0)
    return jnp.concatenate([block[128 * n : 128 * (n + 1)] for n in range(3)] + [wide.T[:, : block.shape[0] - 384]], 1)


def halves(rows, core, keep_ref, send_ref):
    block = rows.reshape(16, 2, 8, rows.shape[1])
    even, odd = block[:, 0].reshape(128, rows.shape[1]), block[:, 1].reshape(128, rows.shape[1])
    keep_ref[...] = jnp.where(core == 0, even, odd)
    send_ref[...] = jnp.where(core == 0, odd, even)


def back_kernel(scalars, get, outs, scratch):
    (out_ref,), (wh_ref, wl_ref) = outs, scratch
    split_weights(scalars[0][0], scalars[1][0], get, 2, wh_ref, wl_ref)
    cells = split(jnp.concatenate([get(0)[...], get(1)[...]], 0))
    last = lax.broadcasted_iota(jnp.int32, (5, 8, 8, 128), 2) == 7
    zero = jnp.zeros((5, 1, 8, 128), F32)

    def tap(a, b, c):
        t = (a * 3 + b) * 3 + c
        rows = slice(128 * t, 128 * (t + 1))
        return contract(cells, (wh_ref[rows], wl_ref[rows]), ((1,), (1,))).reshape(5, 8, 8, 128)

    def along_x(a, b):
        low = tap(a, b, 0).reshape(40, 8, 128)
        moved = jnp.where(last, 0.0, pltpu.roll(low, 7, 1).reshape(5, 8, 8, 128))
        return tap(a, b, 1), tap(a, b, 2) + moved

    def along_y(a):
        low, mid, high = along_x(a, 0), along_x(a, 1), along_x(a, 2)
        return [[mid[p], high[p] + jnp.concatenate([low[p][:, 1:], zero], 1)] for p in range(2)]

    low, mid, high = along_y(0), along_y(1), along_y(2)
    for px in range(2):
        for py in range(2):
            even = mid[px][py]
            odd = high[px][py][:4] + low[px][py][1:]
            for i in range(4):
                for j in range(8):
                    out_ref[2 * i, 2 * j + py, pl.ds(px, 8, stride=2), :] = even[i, j]
                    out_ref[2 * i + 1, 2 * j + py, pl.ds(px, 8, stride=2), :] = odd[i, j]


def call(kernel, out_shapes, blocks, micros):
    return pl.pallas_call(
        kernel,
        out_shape=out_shapes,
        in_specs=[VMEM] * blocks,
        out_specs=[VMEM] * len(out_shapes),
        compiler_params=pltpu.CompilerParams(vmem_limit_bytes=12 * 1024 * 1024),
        cost_estimate=pl.CostEstimate(flops=int(micros * 1.1e9), bytes_accessed=1 << 20, transcendentals=0),
    )


def staged(body, out_shapes, scalars, operands, micros, scratch=(), onto=None, grant=60):
    pairs = [operand if isinstance(operand, tuple) else (operand, None) for operand in operands]
    count, outs = len(pairs), len(out_shapes)
    kept = [] if onto is None else [onto]

    def kernel(*refs):
        scalar_refs, refs = refs[: len(scalars)], refs[len(scalars) :]
        sources, refs = refs[:count], refs[count + len(kept) :]
        out_refs, refs = refs[:outs], refs[outs:]
        buffers, scratch_refs, sems = refs[:count], refs[count:-1], refs[-1]
        copies = []
        for n, (_, window) in enumerate(pairs):
            source = sources[n] if window is None else sources[n].at[:, window[0] : window[1]]
            copies.append(pltpu.make_async_copy(source, buffers[n], sems.at[n]))
        for copy in copies:
            copy.start()

        def get(n):
            copies[n].wait()
            return buffers[n]

        body(scalar_refs, get, out_refs, scratch_refs)

    def buffer(array, window):
        shape = array.shape if window is None else (array.shape[0], window[1] - window[0]) + array.shape[2:]
        return pltpu.VMEM(shape, array.dtype)

    return pl.pallas_call(
        kernel,
        out_shape=out_shapes,
        in_specs=[SMEM] * len(scalars) + [FAR] * (count + len(kept)),
        out_specs=[FAR] * len(kept) + [VMEM] * (outs - len(kept)),
        input_output_aliases={len(scalars) + count: 0} if kept else {},
        scratch_shapes=[buffer(*pair) for pair in pairs] + list(scratch) + [pltpu.SemaphoreType.DMA((count,))],
        compiler_params=pltpu.CompilerParams(vmem_limit_bytes=grant * 1024 * 1024),
        cost_estimate=pl.CostEstimate(flops=int(micros * 1.1e9), bytes_accessed=1 << 10, transcendentals=0),
    )(*scalars, *[array for array, _ in pairs], *kept)


def shaped(*dims, dtype=F32):
    return jax.ShapeDtypeStruct(dims, dtype)


def on_device(volumes, weight_one, weight_two, cotangent):
    blocks = lax.axis_size("blk")
    groups = lax.axis_size("fsdp")
    core_index = lax.rem(lax.axis_index("blk"), 2)
    core = core_index.reshape(1).astype(jnp.int32)
    odd_index = lax.rem(lax.axis_index("blk") // 2, 2)
    odd = odd_index.reshape(1).astype(jnp.int32)
    group = lax.axis_index("fsdp").reshape(1).astype(jnp.int32)
    take, fold = (jnp.asarray(array) for array in selections())
    field = volumes[0]
    scale_two = 1.0 / (32 * blocks * groups) ** 0.5
    scale_one = 1.0 / (256 * blocks * groups) ** 0.5
    up = [(n, n + 1) for n in range(blocks - 1)]
    down = [(n + 1, n) for n in range(blocks - 1)]
    swap = [(n, n ^ 1) for n in range(blocks)]
    same_core = [[2 * q + c for q in range(blocks // 2)] for c in range(2)]

    below = lax.ppermute(field[5:], "blk", up)
    other_field = lax.ppermute(field, "blk", swap)
    other_below = lax.ppermute(below[2:], "blk", swap)
    half = lax.dynamic_slice_in_dim(weight_one, core_index * HALF + odd_index * STEP, PART, 0)
    sent = jnp.concatenate([half, cotangent.reshape(32, 256)], 0)
    mine = lax.all_to_all(jnp.broadcast_to(sent, (groups, PART + 32, 256)), "fsdp", 0, 0, tiled=True)
    mine, below, other_below = lax.optimization_barrier((mine, below, other_below))
    cots_above = lax.ppermute(mine[:, PART : PART + 16], "blk", down)
    pieces = []
    for begin, shift in ((0, 2), (PIECE, 14)):
        around = [(n, n // 16 * 16 + (n + shift) % 16) for n in range(blocks)]
        pieces.append(lax.ppermute(mine[:, begin : begin + PIECE], "blk", around))
    (back,) = staged(cot_kernel, [shaped(8, 32, ROWS_TWO)], [group], [weight_two, (mine, (PART, PART + 32)), cots_above], 3)
    _, *pieces = lax.optimization_barrier((back, *pieces))
    first, *others = [lax.ppermute(piece, "blk", swap) for piece in (mine, *pieces)]
    halves_of = [(mine, (0, PART)), *pieces, (first, (0, PART)), *others]
    back = lax.all_to_all(back, "fsdp", 0, 0, tiled=True)

    def patch_scratch(rows):
        return [pltpu.VMEM((3, 11, 17, 8, 128), F32), pltpu.VMEM((rows, 3456), BF16), pltpu.VMEM((rows, 3456), BF16)]

    weights = [pltpu.VMEM((3456, 256), BF16)] * 2
    pre, taken = staged(
        first_kernel,
        [shaped(256, 256), shaped(8, 32, ROWS_TWO)],
        [core, odd],
        [field, below, *halves_of, take],
        0.01,
        patch_scratch(320) + weights,
        grant=60,
    )
    taken, back, pre = lax.optimization_barrier((taken, back, pre))
    got = lax.all_to_all(taken, "fsdp", 0, 0, tiled=True)
    grad_pre, edge, keep, send = staged(
        functools.partial(pre_kernel, scale_one),
        [shaped(256, 256), shaped(64, 256), shaped(128, 256), shaped(128, 256)],
        [core],
        [back, fold, pre],
        0.01,
        [pltpu.VMEM((864, 256), BF16)] * 2,
        grant=63,
    )
    swapped = lax.ppermute(send, "blk", swap)
    (one,) = staged(
        grad_kernel,
        [shaped(8, SENT, 128)],
        [],
        [field, below, other_field, other_below, keep, swapped],
        0.01,
        patch_scratch(512),
        grant=63,
    )
    one, got, edge = lax.optimization_barrier((one, got, edge))
    pre_above = lax.ppermute(edge, "blk", down)
    part_scratch = [pltpu.VMEM((8, SENT - ROWS_ONE, 128), F32), pltpu.SemaphoreType.DMA(())]
    (one,) = staged(second_kernel, [shaped(8, SENT, 128)], [], [weight_two, got], 0.01, part_scratch, one)
    one = lax.all_to_all(one, "fsdp", 0, 0, tiled=True)
    half_two = [shaped(128, ROWS_TWO)] * 2
    keep, send = staged(functools.partial(two_kernel, scale_two), half_two, [core], [(mine, (PART, PART + 32)), got], 0.01)
    two = keep + lax.ppermute(send, "blk", swap)
    blk = lax.axis_index("blk")
    two = two.reshape(2, 2, 2, 2, 8, ROWS_TWO)
    for distance, position in ((2, 3), (4, 2), (16, 0), (8, 0)):
        bit = lax.rem(blk // distance, 2)
        away = lax.dynamic_index_in_dim(two, 1 - bit, position, keepdims=False)
        stay = lax.dynamic_index_in_dim(two, bit, position, keepdims=False)
        two = stay + lax.ppermute(away, "blk", [(n, n ^ distance) for n in range(blocks)])
        if distance == 2:
            two, pre_above = lax.optimization_barrier((two, pre_above))
        if distance == 4:
            two, pre_above = lax.optimization_barrier((two, pre_above))
            (grad_input,) = staged(back_kernel, [shaped(8, 16, 16, 128)], [core, odd], [grad_pre, pre_above, *halves_of], 0.01, weights)
        if distance == 16:
            one, two, grad_input = lax.optimization_barrier((one, two, grad_input))
            last, out = call(sum_kernel, [shaped(16, 8, ROWS_ONE), shaped(32, 256)], 1, 2)(one)
    last = lax.all_to_all(last, "blk", 0, 0, tiled=True, axis_index_groups=same_core)
    (one,) = call(end_kernel, [shaped(8, ROWS_ONE)], 1, 1)(last)
    return (out.reshape(1, 2, 4, 4, 256), grad_input[None], one.T, two.T)


def solution(mesh):
    placed = (
        P("fsdp", "blk", None, None, None),
        P("fsdp", None),
        P("fsdp", None),
        P("fsdp", "blk", None, None, None),
    )
    return jax.shard_map(
        on_device,
        mesh=mesh,
        in_specs=placed,
        out_specs=(
            P("fsdp", "blk", None, None, None),
            P("fsdp", "blk", None, None, None),
            P("fsdp", "blk"),
            P("fsdp", "blk"),
        ),
        check_vma=False,
    )
```

```python
import functools

import jax
import jax.numpy as jnp
import ml_dtypes
import numpy as np
from jax import lax
from jax.experimental import pallas as pl
from jax.experimental.pallas import tpu as pltpu
from jax.sharding import PartitionSpec as P

F32 = jnp.float32
BF16 = jnp.bfloat16
ROWS_ONE = 432
ROWS_TWO = 864
HALF = 216
PART = 112
STEP = HALF - PART
PIECE = PART // 2
TAPS = [(a, b, c) for a in range(3) for b in range(3) for c in range(3)]
VMEM = pl.BlockSpec(memory_space=pltpu.VMEM)
SMEM = pl.BlockSpec(memory_space=pltpu.SMEM)
FAR = pl.BlockSpec(memory_space=pltpu.HBM)
SENT = ROWS_ONE + 64


def split(value):
    high = value.astype(BF16)
    return high, (value - high.astype(F32)).astype(BF16)


def contract(left, right, dims=((1,), (0,))):
    def one(x, y):
        return lax.dot_general(x, y, (dims, ((), ())), preferred_element_type=F32)

    return one(left[0], right[0]) + (one(left[0], right[1]) + one(left[1], right[0]))


def selections():
    take = np.zeros((27, 2, 4, 4, 5, 8, 8), np.float32)
    fold = np.zeros((4, 8, 8, 27, 2, 4, 4), np.float32)
    for t, (a, b, c) in enumerate(TAPS):
        for i in range(2):
            for j in range(4):
                for k in range(4):
                    y, x = 2 * j - 1 + b, 2 * k - 1 + c
                    if y < 0 or x < 0:
                        continue
                    take[t, i, j, k, 2 * i + a, y, x] = 1
                    fold[2 * i + (0 if a == 1 else 1), y, x, t, i, j, k] = 1
    take = np.concatenate([take[:, :, :, :, 1:], take[:, :, :, :, :1]], 4)
    return take.reshape(864, 320).astype(ml_dtypes.bfloat16), fold.reshape(256, 864).astype(ml_dtypes.bfloat16)


def spans(width, shard):
    for t in range(27):
        done = 0
        while done < width:
            j, at = divmod(t * width + done, shard)
            size = min(width - done, shard - at)
            yield t, done, j, at, size
            done += size


def split_weights(core, odd, get, first, wh_ref, wl_ref):
    pieces = [get(first + n) for n in range(6)]

    def half_of(own, lower, upper):
        away = jnp.concatenate([lower, upper], 0)
        return jnp.concatenate([jnp.where(odd == 0, own, away), jnp.where(odd == 0, away, own)[2 * PART - HALF :]], 0)

    for s in range(8):
        mine = half_of(*[piece[s] for piece in pieces[:3]])
        other = half_of(*[piece[s] for piece in pieces[3:]])
        both = jnp.concatenate([jnp.where(core == 0, mine, other), jnp.where(core == 0, other, mine)], 0)
        high, low = split(both)
        wh_ref[ROWS_ONE * s : ROWS_ONE * (s + 1)] = high
        wl_ref[ROWS_ONE * s : ROWS_ONE * (s + 1)] = low


def patches_of(vol_ref, below_ref, layers, x_ref, ph_ref, pl_ref, first=0):
    skipped = 3 - below_ref.shape[0]
    rows = slice(first, first + 64 * len(layers))
    lane_row = lax.broadcasted_iota(jnp.int32, (16, 8, 128), 1)
    for z in range(2 * min(layers), 11):
        source, at = (below_ref, z - skipped) if z < 3 else (vol_ref, z - 3)
        even = source[at, :, pl.ds(0, 8, stride=2), :]
        odd = source[at, :, pl.ds(1, 8, stride=2), :]
        x_ref[0, z, 1:17] = jnp.where(lane_row == 0, 0.0, pltpu.roll(odd, 1, 1))
        x_ref[1, z, 1:17] = even
        x_ref[2, z, 1:17] = odd
        for c in range(3):
            x_ref[c, z, 0] = jnp.zeros((8, 128), F32)
    for t, (a, b, c) in enumerate(TAPS):
        tiles = [x_ref[c, 2 * n + a, 2 * j + b] for n in layers for j in range(8)]
        high, low = split(jnp.concatenate(tiles, 0))
        cols = slice(128 * t, 128 * (t + 1))
        ph_ref[rows, cols] = high
        pl_ref[rows, cols] = low


def cot_kernel(scalars, get, outs, scratch):
    weights = split(get(0)[...])
    cells = get(1)[...]
    plain = cells.reshape(256, 256)
    moved = jnp.concatenate([cells[:, 16:], get(2)[...]], 1).reshape(256, 256)
    nt = ((1,), (1,))
    here = contract(split(plain), weights, nt)
    next_up = contract(split(moved), weights, nt)
    row = scalars[0][0] * ROWS_TWO + lax.broadcasted_iota(jnp.int32, (256, ROWS_TWO), 1)
    outs[0][...] = jnp.where(row < 9 * 256, next_up, here).reshape(8, 32, ROWS_TWO)


def first_kernel(scalars, get, outs, scratch):
    pre_ref, send_ref = outs
    x_ref, ph_ref, pl_ref, wh_ref, wl_ref = scratch
    patches_of(get(0), get(1), (1, 2, 3, 4, 0), x_ref, ph_ref, pl_ref)
    split_weights(scalars[0][0], scalars[1][0], get, 2, wh_ref, wl_ref)
    full = contract((ph_ref[...], pl_ref[...]), (wh_ref[...], wl_ref[...]))
    pre_ref[...] = full[:256]
    hidden = full / (1.0 + jnp.exp(-full))
    high, low = split(hidden)
    take = get(8)[...]
    taken = jnp.dot(take, high, preferred_element_type=F32) + jnp.dot(take, low, preferred_element_type=F32)
    for t, begin, j, at, size in spans(256, ROWS_TWO):
        send_ref[j, :, at : at + size] = taken[32 * t : 32 * (t + 1), begin : begin + size]


def pre_kernel(scale, scalars, get, outs, scratch):
    gp_ref, keep_ref, send_ref = outs
    gh_ref, gl_ref = scratch
    got_ref = get(0)
    for t, begin, j, at, size in spans(256, ROWS_TWO):
        high, low = split(got_ref[j, :, at : at + size])
        gh_ref[32 * t : 32 * (t + 1), begin : begin + size] = high
        gl_ref[32 * t : 32 * (t + 1), begin : begin + size] = low
    fold = get(1)[...]
    hidden_grad = jnp.dot(fold, gh_ref[...], preferred_element_type=F32) + jnp.dot(fold, gl_ref[...], preferred_element_type=F32)
    pre = get(2)[...]
    sigma = 1.0 / (1.0 + jnp.exp(-pre))
    pre_grad = hidden_grad * sigma * (1.0 + pre * (1.0 - sigma))
    gp_ref[...] = pre_grad
    halves(pre_grad.T * scale, scalars[0][0], keep_ref, send_ref)


def grad_kernel(scalars, get, outs, scratch):
    x_ref, ph_ref, pl_ref = scratch
    (out_ref,) = outs
    layers = (1, 2, 3, 4)
    patches_of(get(0), get(1), layers, x_ref, ph_ref, pl_ref, 0)
    patches_of(get(2), get(3), layers, x_ref, ph_ref, pl_ref, 256)
    cells = split(jnp.concatenate([get(4)[...], get(5)[...]], 1))
    grads = contract(cells, (ph_ref[...], pl_ref[...]))
    for j in range(8):
        out_ref[j, :ROWS_ONE] = stack(grads[:, ROWS_ONE * j : ROWS_ONE * (j + 1)])
        out_ref[j, ROWS_ONE:] = jnp.zeros((SENT - ROWS_ONE, 128), F32)


def second_kernel(scalars, get, outs, scratch):
    part_ref, sem = scratch
    weights = split(get(0)[...])
    patches = split(get(1)[...].reshape(256, ROWS_TWO))
    part = contract(patches, weights).reshape(8, 32, 256)
    part_ref[:, :32] = part[:, :, :128]
    part_ref[:, 32:] = part[:, :, 128:]
    copy = pltpu.make_async_copy(part_ref, outs[0].at[:, ROWS_ONE:SENT], sem)
    copy.start()
    copy.wait()


def two_kernel(scale, scalars, get, outs, scratch):
    turned = split(get(0)[...].reshape(256, 256).T * scale)
    patches = split(get(1)[...].reshape(256, ROWS_TWO))
    halves(contract(turned, patches), scalars[0][0], *outs)


def sum_kernel(got_ref, sum_ref, out_ref):
    total = got_ref[0]
    for j in range(1, 8):
        total = total + got_ref[j]
    sum_ref[...] = unstack(total[:ROWS_ONE]).reshape(16, 8, ROWS_ONE)
    out_ref[...] = jnp.concatenate([total[ROWS_ONE : ROWS_ONE + 32], total[ROWS_ONE + 32 :]], 1)


def end_kernel(got_ref, one_ref):
    total = got_ref[0]
    for j in range(1, 16):
        total = total + got_ref[j]
    one_ref[...] = total


def stack(block):
    wide = jnp.concatenate([block[:, 384:], jnp.zeros((128, 512 - block.shape[1]), F32)], 1)
    return jnp.concatenate([block[:, 128 * n : 128 * (n + 1)] for n in range(3)] + [wide.T[: block.shape[1] - 384]], 0)


def unstack(block):
    wide = jnp.concatenate([block[384:], jnp.zeros((512 - block.shape[0], 128), F32)], 0)
    return jnp.concatenate([block[128 * n : 128 * (n + 1)] for n in range(3)] + [wide.T[:, : block.shape[0] - 384]], 1)


def halves(rows, core, keep_ref, send_ref):
    block = rows.reshape(16, 2, 8, rows.shape[1])
    even, odd = block[:, 0].reshape(128, rows.shape[1]), block[:, 1].reshape(128, rows.shape[1])
    keep_ref[...] = jnp.where(core == 0, even, odd)
    send_ref[...] = jnp.where(core == 0, odd, even)


def back_kernel(scalars, get, outs, scratch):
    (out_ref,), (wh_ref, wl_ref) = outs, scratch
    split_weights(scalars[0][0], scalars[1][0], get, 2, wh_ref, wl_ref)
    cells = split(jnp.concatenate([get(0)[...], get(1)[...]], 0))
    last = lax.broadcasted_iota(jnp.int32, (5, 8, 8, 128), 2) == 7
    zero = jnp.zeros((5, 1, 8, 128), F32)

    def tap(a, b, c):
        t = (a * 3 + b) * 3 + c
        rows = slice(128 * t, 128 * (t + 1))
        return contract(cells, (wh_ref[rows], wl_ref[rows]), ((1,), (1,))).reshape(5, 8, 8, 128)

    def along_x(a, b):
        low = tap(a, b, 0).reshape(40, 8, 128)
        moved = jnp.where(last, 0.0, pltpu.roll(low, 7, 1).reshape(5, 8, 8, 128))
        return tap(a, b, 1), tap(a, b, 2) + moved

    def along_y(a):
        low, mid, high = along_x(a, 0), along_x(a, 1), along_x(a, 2)
        return [[mid[p], high[p] + jnp.concatenate([low[p][:, 1:], zero], 1)] for p in range(2)]

    low, mid, high = along_y(0), along_y(1), along_y(2)
    for px in range(2):
        for py in range(2):
            even = mid[px][py]
            odd = high[px][py][:4] + low[px][py][1:]
            for i in range(4):
                for j in range(8):
                    out_ref[2 * i, 2 * j + py, pl.ds(px, 8, stride=2), :] = even[i, j]
                    out_ref[2 * i + 1, 2 * j + py, pl.ds(px, 8, stride=2), :] = odd[i, j]


def call(kernel, out_shapes, blocks, micros):
    return pl.pallas_call(
        kernel,
        out_shape=out_shapes,
        in_specs=[VMEM] * blocks,
        out_specs=[VMEM] * len(out_shapes),
        compiler_params=pltpu.CompilerParams(vmem_limit_bytes=12 * 1024 * 1024),
        cost_estimate=pl.CostEstimate(flops=int(micros * 1.1e9), bytes_accessed=1 << 20, transcendentals=0),
    )


def staged(body, out_shapes, scalars, operands, micros, scratch=(), onto=None, grant=60):
    pairs = [operand if isinstance(operand, tuple) else (operand, None) for operand in operands]
    count, outs = len(pairs), len(out_shapes)
    kept = [] if onto is None else [onto]

    def kernel(*refs):
        scalar_refs, refs = refs[: len(scalars)], refs[len(scalars) :]
        sources, refs = refs[:count], refs[count + len(kept) :]
        out_refs, refs = refs[:outs], refs[outs:]
        buffers, scratch_refs, sems = refs[:count], refs[count:-1], refs[-1]
        copies = []
        for n, (_, window) in enumerate(pairs):
            source = sources[n] if window is None else sources[n].at[:, window[0] : window[1]]
            copies.append(pltpu.make_async_copy(source, buffers[n], sems.at[n]))
        for copy in copies:
            copy.start()

        def get(n):
            copies[n].wait()
            return buffers[n]

        body(scalar_refs, get, out_refs, scratch_refs)

    def buffer(array, window):
        shape = array.shape if window is None else (array.shape[0], window[1] - window[0]) + array.shape[2:]
        return pltpu.VMEM(shape, array.dtype)

    return pl.pallas_call(
        kernel,
        out_shape=out_shapes,
        in_specs=[SMEM] * len(scalars) + [FAR] * (count + len(kept)),
        out_specs=[FAR] * len(kept) + [VMEM] * (outs - len(kept)),
        input_output_aliases={len(scalars) + count: 0} if kept else {},
        scratch_shapes=[buffer(*pair) for pair in pairs] + list(scratch) + [pltpu.SemaphoreType.DMA((count,))],
        compiler_params=pltpu.CompilerParams(vmem_limit_bytes=grant * 1024 * 1024),
        cost_estimate=pl.CostEstimate(flops=int(micros * 1.1e9), bytes_accessed=1 << 10, transcendentals=0),
    )(*scalars, *[array for array, _ in pairs], *kept)


def shaped(*dims, dtype=F32):
    return jax.ShapeDtypeStruct(dims, dtype)


def on_device(volumes, weight_one, weight_two, cotangent):
    blocks = lax.axis_size("blk")
    groups = lax.axis_size("fsdp")
    core_index = lax.rem(lax.axis_index("blk"), 2)
    core = core_index.reshape(1).astype(jnp.int32)
    odd_index = lax.rem(lax.axis_index("blk") // 2, 2)
    odd = odd_index.reshape(1).astype(jnp.int32)
    group = lax.axis_index("fsdp").reshape(1).astype(jnp.int32)
    take, fold = (jnp.asarray(array) for array in selections())
    field = volumes[0]
    scale_two = 1.0 / (32 * blocks * groups) ** 0.5
    scale_one = 1.0 / (256 * blocks * groups) ** 0.5
    up = [(n, n + 1) for n in range(blocks - 1)]
    down = [(n + 1, n) for n in range(blocks - 1)]
    swap = [(n, n ^ 1) for n in range(blocks)]
    same_core = [[2 * q + c for q in range(blocks // 2)] for c in range(2)]

    below = lax.ppermute(field[5:], "blk", up)
    other_field = lax.ppermute(field, "blk", swap)
    other_below = lax.ppermute(below[2:], "blk", swap)
    half = lax.dynamic_slice_in_dim(weight_one, core_index * HALF + odd_index * STEP, PART, 0)
    sent = jnp.concatenate([half, cotangent.reshape(32, 256)], 0)
    mine = lax.all_to_all(jnp.broadcast_to(sent, (groups, PART + 32, 256)), "fsdp", 0, 0, tiled=True)
    mine, below, other_below = lax.optimization_barrier((mine, below, other_below))
    cots_above = lax.ppermute(mine[:, PART : PART + 16], "blk", down)
    pieces = []
    for begin, shift in ((0, 2), (PIECE, 14)):
        around = [(n, n // 16 * 16 + (n + shift) % 16) for n in range(blocks)]
        pieces.append(lax.ppermute(mine[:, begin : begin + PIECE], "blk", around))
    (back,) = staged(cot_kernel, [shaped(8, 32, ROWS_TWO)], [group], [weight_two, (mine, (PART, PART + 32)), cots_above], 3)
    _, *pieces = lax.optimization_barrier((back, *pieces))
    first, *others = [lax.ppermute(piece, "blk", swap) for piece in (mine, *pieces)]
    halves_of = [(mine, (0, PART)), *pieces, (first, (0, PART)), *others]
    back = lax.all_to_all(back, "fsdp", 0, 0, tiled=True)

    def patch_scratch(rows):
        return [pltpu.VMEM((3, 11, 17, 8, 128), F32), pltpu.VMEM((rows, 3456), BF16), pltpu.VMEM((rows, 3456), BF16)]

    weights = [pltpu.VMEM((3456, 256), BF16)] * 2
    pre, taken = staged(
        first_kernel,
        [shaped(256, 256), shaped(8, 32, ROWS_TWO)],
        [core, odd],
        [field, below, *halves_of, take],
        0.01,
        patch_scratch(320) + weights,
        grant=60,
    )
    taken, back, pre = lax.optimization_barrier((taken, back, pre))
    got = lax.all_to_all(taken, "fsdp", 0, 0, tiled=True)
    grad_pre, keep, send = staged(
        functools.partial(pre_kernel, scale_one),
        [shaped(256, 256), shaped(128, 256), shaped(128, 256)],
        [core],
        [back, fold, pre],
        0.01,
        [pltpu.VMEM((864, 256), BF16)] * 2,
    )
    swapped = lax.ppermute(send, "blk", swap)
    (one,) = staged(
        grad_kernel,
        [shaped(8, SENT, 128)],
        [],
        [field, below, other_field, other_below, keep, swapped],
        0.01,
        patch_scratch(512),
    )
    one, got, edge = lax.optimization_barrier((one, got, grad_pre[:64]))
    pre_above = lax.ppermute(edge, "blk", down)
    part_scratch = [pltpu.VMEM((8, SENT - ROWS_ONE, 128), F32), pltpu.SemaphoreType.DMA(())]
    (one,) = staged(second_kernel, [shaped(8, SENT, 128)], [], [weight_two, got], 0.01, part_scratch, one)
    one = lax.all_to_all(one, "fsdp", 0, 0, tiled=True)
    half_two = [shaped(128, ROWS_TWO)] * 2
    keep, send = staged(functools.partial(two_kernel, scale_two), half_two, [core], [(mine, (PART, PART + 32)), got], 0.01)
    two = keep + lax.ppermute(send, "blk", swap)
    blk = lax.axis_index("blk")
    two = two.reshape(2, 2, 2, 2, 8, ROWS_TWO)
    for distance, position in ((2, 3), (4, 2), (8, 1), (16, 0)):
        bit = lax.rem(blk // distance, 2)
        away = lax.dynamic_index_in_dim(two, 1 - bit, position, keepdims=False)
        stay = lax.dynamic_index_in_dim(two, bit, position, keepdims=False)
        two = stay + lax.ppermute(away, "blk", [(n, n ^ distance) for n in range(blocks)])
        if distance == 2:
            two, pre_above = lax.optimization_barrier((two, pre_above))
        if distance == 4:
            two, pre_above = lax.optimization_barrier((two, pre_above))
            (grad_input,) = staged(back_kernel, [shaped(8, 16, 16, 128)], [core, odd], [grad_pre, pre_above, *halves_of], 0.01, weights)
        if distance == 8:
            one, two, grad_input = lax.optimization_barrier((one, two, grad_input))
            last, out = call(sum_kernel, [shaped(16, 8, ROWS_ONE), shaped(32, 256)], 1, 2)(one)
    last = lax.all_to_all(last, "blk", 0, 0, tiled=True, axis_index_groups=same_core)
    (one,) = call(end_kernel, [shaped(8, ROWS_ONE)], 1, 1)(last)
    return (out.reshape(1, 2, 4, 4, 256), grad_input[None], one.T, two.T)


def solution(mesh):
    placed = (
        P("fsdp", "blk", None, None, None),
        P("fsdp", None),
        P("fsdp", None),
        P("fsdp", "blk", None, None, None),
    )
    return jax.shard_map(
        on_device,
        mesh=mesh,
        in_specs=placed,
        out_specs=(
            P("fsdp", "blk", None, None, None),
            P("fsdp", "blk", None, None, None),
            P("fsdp", "blk"),
            P("fsdp", "blk"),
        ),
        check_vma=False,
    )
```
